256 devices in a mesh: grp: 32 (over z, x), seq: 8 (over y, core).
Axes of the slice: x: 4, y: 4, z: 8, core: 2. Of those that a mesh axis runs over, the one named last changes fastest.
Arguments:
- tokens: bfloat16 [32, 8, 256, 1152], P('grp', 'seq'), may hold values from -6 to 6
- grad_out: bfloat16 [32, 8, 256, 1152], P('grp', 'seq'), may hold values from -6 to 6
- modulation: float32 [32, 3, 1152], P('grp'), may hold values from -4 to 4
- frame_counts: int32 [32], P('grp'), may hold values from 3 to 8, as said below
- w_qkv: bfloat16 [1152, 1728], P('grp'), may hold values from -0.1875 to 0.1875
- w_proj: bfloat16 [576, 1152], P('grp'), may hold values from -0.25 to 0.25
Outputs:
- grad_tokens: bfloat16 [32, 8, 256, 1152], P('grp', 'seq')
- grad_qkv: float32 [1152, 1728], P('grp')
- grad_proj: float32 [576, 1152], P('grp')
The draws below stay inside these ranges and needn't reach their ends.
Inputs may be any that keep to these rules, and one draw needn't show every extreme that they name: `frame_counts`: every sample has at least one quarter of 8 frames live; some sample has all 8.
All inputs are finite; a program needn't handle non-finite values.
Results may differ from the reference program's by a relative error of at most 0.029.
Values may be sent and summed in bfloat16 or wider, within the bound.
No kernel may reach another device: no remote copies, remote signals or barrier semaphores. Data moves between devices by JAX's collectives and lax.ppermute only.
A program may use at most 64 MiB of HBM per device.

```python
import jax
import jax.numpy as jnp
from jax import lax

D = 1152
HEADS = 8
POS = 256
INNER = 576
QKV = 1728
FRAMES = 8
SAMPLES = 32


def draw_frame_counts(key, part):
    key = jax.random.fold_in(key, 1)
    first, second = jax.random.split(key)
    counts = jax.random.randint(first, (SAMPLES,), FRAMES // 4 + 1, FRAMES + 1)
    chosen = jax.random.randint(second, (), 0, SAMPLES)
    return jnp.where(jnp.arange(SAMPLES) == chosen, FRAMES, counts).astype(jnp.int32)


def shard_levels(rng, extent, cuts, least, high):
    def one(position, parts):
        steps = jax.random.uniform(jax.random.fold_in(jax.random.fold_in(rng, 6), position), (parts,), jnp.float32, least / len(cuts), high / len(cuts))
        return jnp.repeat(jnp.exp(steps), extent[position] // parts).reshape((-1,) + (1,) * (len(extent) - position - 1))

    loudness = one(*cuts[0])
    for cut in cuts[1:]:
        loudness = loudness * one(*cut)
    return loudness


def bell_draw(stream_key, extent, scale, bound, cuts=(), kind=jnp.bfloat16):
    loudness = shard_levels(stream_key, extent, cuts, -0.22, 0.18) if cuts else 1.0
    values = jax.random.normal(stream_key, extent, jnp.float32) * scale * loudness
    return jnp.minimum(jnp.maximum(values, -bound), bound).astype(kind)


def setup_inputs(seed: int = 0) -> dict:
    key_of = jax.random.split(jax.random.key(seed), 7)
    return {
        "tokens": bell_draw(key_of[0], (SAMPLES, FRAMES, POS, D), 1.0, 6.0, ((0, 32), (1, 8))),
        "grad_out": bell_draw(key_of[1], (SAMPLES, FRAMES, POS, D), 1.0, 6.0, ((0, 32), (1, 8))),
        "modulation": bell_draw(key_of[2], (SAMPLES, 3, D), 1.0, 4.0, ((0, 32),), jnp.float32),
        "frame_counts": draw_frame_counts(jax.random.fold_in(key_of[6], 71), 0),
        "w_qkv": bell_draw(key_of[4], (D, QKV), D ** -0.5, 0.1875, ((0, 32),)),
        "w_proj": bell_draw(key_of[5], (INNER, D), INNER ** -0.5, 0.25, ((0, 32),)),
    }


def normalize(x):
    xf = x.astype(jnp.float32)
    mean = lax.optimization_barrier(jnp.mean(xf, axis=-1, keepdims=True))
    cent = xf - mean
    rstd = lax.rsqrt(lax.optimization_barrier(jnp.mean(cent * cent, axis=-1, keepdims=True)) + 1e-06)
    return (cent * rstd, rstd)

def attend(query, key_all, value, keep):
    factor = query.shape[-1] ** (-0.5)
    scores = jnp.einsum('fphd,gphd->phfg', query.astype(jnp.float32), key_all.astype(jnp.float32)) * factor
    scores = jnp.where(keep[None, None, None, :], scores, -1e+30)
    top = lax.optimization_barrier(jnp.max(scores, axis=-1, keepdims=True))
    expd = jnp.exp(scores - top)
    probs = expd / lax.optimization_barrier(jnp.sum(expd, axis=-1, keepdims=True))
    probs_b = probs.astype(jnp.bfloat16)
    heads_out = jnp.einsum('phfg,gphd->fphd', probs_b.astype(jnp.float32), value.astype(jnp.float32)).astype(jnp.bfloat16)
    return (heads_out, probs, probs_b)

def attend_back(query, key_all, value, probs, probs_b, grad_heads):
    factor = query.shape[-1] ** (-0.5)
    dgrad = grad_heads.astype(jnp.float32)
    dprobs = jnp.einsum('fphd,gphd->phfg', dgrad, value.astype(jnp.float32))
    dvalue = jnp.einsum('phfg,fphd->gphd', probs_b.astype(jnp.float32), dgrad)
    delta = lax.optimization_barrier(jnp.sum(probs * dprobs, axis=-1, keepdims=True))
    dscores = probs * (dprobs - delta) * factor
    dquery = jnp.einsum('phfg,gphd->fphd', dscores, key_all.astype(jnp.float32))
    dkey = jnp.einsum('phfg,fphd->gphd', dscores, query.astype(jnp.float32))
    return (dquery, dkey, dvalue)

def reference(tokens, grad_out, modulation, frame_counts, w_qkv, w_proj):
    inner = w_proj.shape[0]
    head_size = inner // HEADS

    def one_sample(carry, item):
        x, dy, mods, count = item
        frames, positions, width = x.shape
        normed, rstd = normalize(x)
        modded = (normed * (1.0 + mods[1]) + mods[0]).astype(jnp.bfloat16)
        qkv = jnp.dot(modded, w_qkv, preferred_element_type=jnp.float32).astype(jnp.bfloat16)
        qkv = qkv.reshape(frames, positions, 3, HEADS, head_size)
        query, key_all, value = (qkv[:, :, 0], qkv[:, :, 1], qkv[:, :, 2])
        keep = jnp.arange(frames) < count
        heads_out, probs, probs_b = attend(query, key_all, value, keep)
        heads_flat = heads_out.reshape(frames * positions, inner)
        live = keep.astype(jnp.float32)[:, None, None]
        gated = (mods[2] * live * dy.astype(jnp.float32)).astype(jnp.bfloat16).reshape(frames * positions, width)
        grad_heads = jnp.dot(gated, w_proj.T, preferred_element_type=jnp.float32).astype(jnp.bfloat16)
        grad_proj = jnp.dot(heads_flat.T, gated, preferred_element_type=jnp.float32)
        grad_heads = grad_heads.reshape(frames, positions, HEADS, head_size)
        dquery, dkey, dvalue = attend_back(query, key_all, value, probs, probs_b, grad_heads)
        grad_rows = jnp.stack([dquery, dkey, dvalue], axis=2).astype(jnp.bfloat16).reshape(frames * positions, 3 * inner)
        grad_modded = jnp.dot(grad_rows, w_qkv.T, preferred_element_type=jnp.float32).astype(jnp.bfloat16)
        grad_qkv = jnp.dot(modded.reshape(frames * positions, width).T, grad_rows, preferred_element_type=jnp.float32)
        dn = grad_modded.reshape(frames, positions, width).astype(jnp.float32) * (1.0 + mods[1])
        mean_dn = lax.optimization_barrier(jnp.mean(dn, axis=-1, keepdims=True))
        mean_dnn = lax.optimization_barrier(jnp.mean(dn * normed, axis=-1, keepdims=True))
        grad_x = dy.astype(jnp.float32) + rstd * (dn - mean_dn - normed * mean_dnn)
        return ((carry[0] + grad_qkv, carry[1] + grad_proj), grad_x.astype(jnp.bfloat16))
    init = (jnp.zeros(w_qkv.shape, jnp.float32), jnp.zeros(w_proj.shape, jnp.float32))
    sums, grad_tokens = lax.scan(one_sample, init, (tokens, grad_out, modulation, frame_counts))
    return (grad_tokens, sums[0], sums[1])
```

```python
import functools

import jax
import jax.numpy as jnp
import numpy as np
from jax import lax
from jax.experimental import pallas as pl
from jax.experimental.pallas import tpu as pltpu
from jax.sharding import PartitionSpec as P

BF = jnp.bfloat16
F32 = jnp.float32
HEADS = 8
HEAD = 72
D = 1152
INNER = 576
QKV = 1728
NX, NY, NZ = 4, 4, 8
HALF = 24
RING = 4 * HALF
KZ = ((0, 4, 1, 5), (7, 3, 2, 6))
ORDER = (1, 3, 2)
ROWS = 16 * RING
WIDE = 640
VMEM_LIMIT = 56 * 1024 * 1024


def gid(z, x):
    return (z % NZ) * NX + x % NX


def sid(y, c):
    return (y % NY) * 2 + c % 2


CORE_SWAP = [(s, s ^ 1) for s in range(8)]


def along_z(dz):
    return [(gid(z, x), gid(z + dz, x)) for z in range(NZ) for x in range(NX)]


def along_x(dx):
    return [(gid(z, x), gid(z, x + dx)) for z in range(NZ) for x in range(NX)]


def along_y(dy):
    return [(sid(y, c), sid(y + dy, c)) for y in range(NY) for c in range(2)]


def crossed(dz):
    return [
        (gid(z, x) * 8 + sid(y, c), gid(z + dz, y) * 8 + sid(x, c))
        for z in range(NZ)
        for x in range(NX)
        for y in range(NY)
        for c in range(2)
    ]


def row_table():
    n = np.arange(ROWS)
    half, n = n // (ROWS // 2), n % (ROWS // 2)
    ring, n = n // (4 * RING), n % (4 * RING)
    step, n = n // RING, n % RING
    kz = np.array(KZ)[ring, n // HALF]
    row = half * HALF + n % HALF
    zero = np.zeros_like(n)
    return np.stack([ring, step, kz, row, zero, zero, zero, zero]).astype(np.int32)


def position():
    g = lax.axis_index("grp")
    s = lax.axis_index("seq")
    return g & 3, s >> 1, g >> 2, s & 1


def pack_kernel(wq_ref, wp_ref, out_ref, buf):
    _, _, _, c = position()
    buf[0:36, :] = wq_ref[...].astype(F32)
    wp = wp_ref[...].astype(F32)
    buf[36:48, 0:D] = wp[0:12, :]
    tail = wp[12:18, :]
    buf[36:42, D:QKV] = tail[:, 0:INNER]
    buf[42:48, D:QKV] = pltpu.roll(tail[:, 512:D], 640 - 64, 1)[:, 0:INNER]
    out_ref[...] = buf[pl.ds(pl.multiple_of(c * HALF, 8), HALF), :].astype(BF)


def pack(w_qkv, w_proj):
    return pl.pallas_call(
        pack_kernel,
        out_shape=jax.ShapeDtypeStruct((HALF, QKV), BF),
        scratch_shapes=[pltpu.VMEM((48, QKV), F32)],
        name="pack_weights",
    )(w_qkv, w_proj)


def split_kernel(tok_ref, dy_ref, *outs):
    _, y, _, c = position()
    for k in range(4):
        base = ((y + k) & 3) * 64
        for part, core in ((0, c), (1, 1 - c)):
            off = pl.multiple_of(base + core * 32, 32)
            outs[k][part * 64 : part * 64 + 32, :] = tok_ref[pl.ds(off, 32), :]
            outs[k][part * 64 + 32 : part * 64 + 64, :] = dy_ref[pl.ds(off, 32), :]


def split_tokens(x, dy):
    return pl.pallas_call(
        split_kernel,
        out_shape=[jax.ShapeDtypeStruct((128, D), BF)] * 4,
        name="split_tokens",
    )(x, dy)


def join_kernel(g0, g1, g2, g3, swapped, out_ref):
    _, y, _, c = position()
    for k, g in enumerate((g0, g1, g2, g3)):
        base = ((y + k) & 3) * 64
        out_ref[pl.ds(pl.multiple_of(base + c * 32, 32), 32), :] = g[0:32, :]
        out_ref[pl.ds(pl.multiple_of(base + (1 - c) * 32, 32), 32), :] = swapped[
            k * 32 : k * 32 + 32, :
        ]


def join_tokens(parts, swapped):
    return pl.pallas_call(
        join_kernel,
        out_shape=jax.ShapeDtypeStruct((256, D), BF),
        name="join_tokens",
    )(*parts, swapped)


def dot(a, b, ca, cb):
    return lax.dot_general(a, b, (((ca,), (cb,)), ((), ())), preferred_element_type=F32)


def main_kernel(*refs):
    count_ref, tab_ref, mods_ref = refs[0:3]
    td = refs[3:7]
    tsw = refs[7]
    own_w = refs[8:16]
    other_w = refs[16:24]
    gt = refs[24:28]
    keep = refs[28:36]
    send = refs[36:44]
    wbuf, g, perm, nrm, modp, q_s, k_s, v_s, h_s, o_s, dq_s, dk_s, dv_s, rows_s, in_sem, out_sem = refs[44:]
    x, y, z, c = position()
    count = count_ref[0]
    half_rows = ROWS // 2

    loads = []
    for i in range(8):
        for side, src in ((c, own_w[i]), (1 - c, other_w[i])):
            off = pl.multiple_of(side * half_rows + i * RING, 32)
            copy = pltpu.make_async_copy(src, wbuf.at[pl.ds(off, RING), :], in_sem.at[len(loads)])
            copy.start()
            loads.append(copy)

    ring = tab_ref[0:1, :]
    step = tab_ref[1:2, :]
    kz = tab_ref[2:3, :]
    row = tab_ref[3:4, :]
    shard = ((z + kz) & 7) * 4 + ((jnp.where(ring == 0, x, y) + step) & 3)
    natural = jnp.where(row < 36, shard * 36 + row, -1)
    for i in range(0, D, 128):
        ids = lax.broadcasted_iota(jnp.int32, (128, ROWS), 0) + i
        perm[i : i + 128, :] = jnp.where(ids == natural, 1.0, 0.0).astype(BF)

    xf = jnp.concatenate(
        [t[0:32, :].astype(F32) for t in td]
        + [tsw[64 * k : 64 * k + 32, :].astype(F32) for k in range(4)],
        axis=0,
    )
    mean = jnp.mean(xf, axis=-1, keepdims=True)
    cent = xf - mean
    rstd = lax.rsqrt(jnp.mean(cent * cent, axis=-1, keepdims=True) + 1e-06)
    normed = cent * rstd
    nrm[...] = normed
    modded = (normed * (1.0 + mods_ref[1:2, :]) + mods_ref[0:1, :]).astype(BF)
    modp[...] = dot(modded, perm[...], 1, 0).astype(BF)

    for copy in loads:
        copy.wait()

    lane = lax.broadcasted_iota(jnp.int32, (1, WIDE), 1)
    inner_lane = lane < INNER
    mp = modp[...]
    front = dot(mp, wbuf[:, 0:D], 1, 0)
    q_s[...] = jnp.where(inner_lane, front[:, 0:WIDE], 0.0).astype(BF)
    k_s[...] = jnp.where(inner_lane, pltpu.roll(front[:, 512:D], WIDE - 64, 1), 0.0).astype(BF)
    v_s[:, 512:WIDE] = jnp.zeros((256, 128), BF)
    v_s[:, 0:INNER] = dot(mp, wbuf[:, D:QKV], 1, 0).astype(BF)

    r = lax.broadcasted_iota(jnp.int32, (256, 1), 0)
    rf = (((y - (r >> 5)) & 3) * 2) + (c ^ (r >> 7))
    col = lax.broadcasted_iota(jnp.int32, (1, 256), 1)
    cf = (((y - (col >> 5)) & 3) * 2) + (c ^ (col >> 7))
    live = jnp.where(rf < count, 1.0, 0.0)
    dyf = jnp.concatenate(
        [t[32:64, :].astype(F32) for t in td]
        + [tsw[64 * k + 32 : 64 * k + 64, :].astype(F32) for k in range(4)],
        axis=0,
    )
    gated_f = mods_ref[2:3, :] * live * dyf
    gated = gated_f.astype(BF)
    gated_lo = gated[:, 0:INNER]
    gated_hi = pltpu.roll(gated_f[:, 512:D], WIDE - 64, 1)[:, 0:INNER].astype(BF)

    row1 = row[:, half_rows:]
    shard1 = shard[:, half_rows:]
    ids = lax.broadcasted_iota(jnp.int32, (INNER, half_rows), 0)
    pick_main = jnp.where(ids == jnp.where(row1 >= 36, shard1 * 18 + row1 - 36, -1), 1.0, 0.0).astype(BF)
    pick_lo = jnp.where(
        ids == jnp.where((row1 >= 36) & (row1 < 42), shard1 * 18 + row1 - 24, -1), 1.0, 0.0
    ).astype(BF)
    pick_hi = jnp.where(ids == jnp.where(row1 >= 42, shard1 * 18 + row1 - 30, -1), 1.0, 0.0).astype(BF)
    w1 = wbuf[half_rows:, :]
    gh_main = dot(gated, w1[:, 0:D], 1, 1).astype(BF)
    gh_lo = dot(gated_lo, w1[:, D:QKV], 1, 1).astype(BF)
    gh_hi = dot(gated_hi, w1[:, D:QKV], 1, 1).astype(BF)
    gh = dot(gh_main, pick_main, 1, 1) + dot(gh_lo, pick_lo, 1, 1) + dot(gh_hi, pick_hi, 1, 1)
    h_s[:, 512:WIDE] = jnp.zeros((256, 128), BF)
    h_s[:, 0:INNER] = gh.astype(BF)

    same = ((r & 31) == (col & 31)) & (cf < count)
    factor = HEAD ** (-0.5)
    for ref in (o_s, dq_s, dk_s, dv_s):
        ref[...] = jnp.zeros_like(ref)
    for h in range(HEADS):
        lo = h * HEAD
        start = lo // 128 * 128
        stop = -(-(lo + HEAD) // 128) * 128
        win = slice(start, stop)
        lanes = lax.broadcasted_iota(jnp.int32, (1, stop - start), 1) + start
        inside = (lanes >= lo) & (lanes < lo + HEAD)
        zero = jnp.zeros((), BF)
        qm = jnp.where(inside, q_s[:, win], zero)
        km = jnp.where(inside, k_s[:, win], zero)
        vm = jnp.where(inside, v_s[:, win], zero)
        gm = jnp.where(inside, h_s[:, win], zero)
        scores = jnp.where(same, dot(qm, km, 1, 1) * factor, -1e30)
        top = jnp.max(scores, axis=-1, keepdims=True)
        expd = jnp.exp(scores - top)
        probs = expd / jnp.sum(expd, axis=-1, keepdims=True)
        probs_b = probs.astype(BF)
        o_s[:, win] += dot(probs_b, vm, 1, 0)
        dprobs = dot(gm, vm, 1, 1)
        dv_s[:, win] += dot(probs_b, gm, 0, 0)
        delta = jnp.sum(probs * dprobs, axis=-1, keepdims=True)
        ds = (probs * (dprobs - delta) * factor).astype(BF)
        dq_s[:, win] += dot(ds, km, 1, 0)
        dk_s[:, win] += dot(ds, qm, 0, 0)

    dkr = pltpu.roll(dk_s[...], 64, 1)
    rows_s[:, 0:512] = dq_s[:, 0:512].astype(BF)
    rows_s[:, 512:640] = (dq_s[:, 512:640] + dkr[:, 0:128]).astype(BF)
    rows_s[:, 640:D] = dkr[:, 128:640].astype(BF)
    rows_s[:, D:QKV] = dv_s[:, 0:INNER].astype(BF)

    heads_out = o_s[:, 0:INNER].astype(BF)
    h_main = dot(heads_out, pick_main, 1, 0).astype(BF)
    h_lo = dot(heads_out, pick_lo, 1, 0).astype(BF)
    h_hi = dot(heads_out, pick_hi, 1, 0).astype(BF)
    rows = rows_s[...]
    for i in range(0, half_rows, 256):
        g[i : i + 256, :] = dot(modp[:, i : i + 256], rows, 0, 0).astype(BF)
    for i in range(0, half_rows, 256):
        m = modp[:, half_rows + i : half_rows + i + 256]
        at = slice(half_rows + i, half_rows + i + 256)
        g[at, 0:D] = (dot(m, rows[:, 0:D], 0, 0) + dot(h_main[:, i : i + 256], gated, 0, 0)).astype(BF)
        g[at, D:QKV] = (
            dot(m, rows[:, D:QKV], 0, 0)
            + dot(h_lo[:, i : i + 256], gated_lo, 0, 0)
            + dot(h_hi[:, i : i + 256], gated_hi, 0, 0)
        ).astype(BF)
    stores = []
    for side, dst in ((1 - c, send), (c, keep)):
        for i in range(8):
            off = pl.multiple_of(side * half_rows + i * RING, 32)
            copy = pltpu.make_async_copy(g.at[pl.ds(off, RING), :], dst[i], out_sem.at[len(stores)])
            copy.start()
            stores.append(copy)

    gmp = dot(rows, wbuf[...], 1, 1).astype(BF)
    grad_modded = dot(gmp, perm[...], 1, 1)
    dn = grad_modded * (1.0 + mods_ref[1:2, :])
    normed = nrm[...]
    mean_dn = jnp.mean(dn, axis=-1, keepdims=True)
    mean_dnn = jnp.mean(dn * normed, axis=-1, keepdims=True)
    grad_x = (dyf + rstd * (dn - mean_dn - normed * mean_dnn)).astype(BF)
    for k in range(4):
        gt[k][0:32, :] = grad_x[32 * k : 32 * k + 32, :]
        gt[k][32:64, :] = grad_x[128 + 32 * k : 128 + 32 * k + 32, :]
    for copy in stores:
        copy.wait()


def compute(count, table, mods, td, tsw, own_w, other_w):
    vmem = pl.BlockSpec(memory_space=pltpu.VMEM)
    smem = pl.BlockSpec(memory_space=pltpu.SMEM)
    hbm = pl.BlockSpec(memory_space=pl.ANY)
    wide = pltpu.VMEM((256, WIDE), F32)
    wide_b = pltpu.VMEM((256, WIDE), BF)
    outs = pl.pallas_call(
        main_kernel,
        in_specs=[smem, vmem, vmem] + [vmem] * 5 + [hbm] * 16,
        out_specs=[vmem] * 4 + [hbm] * 16,
        out_shape=[jax.ShapeDtypeStruct((64, D), BF)] * 4
        + [jax.ShapeDtypeStruct((RING, QKV), BF)] * 16,
        scratch_shapes=[
            pltpu.VMEM((ROWS, QKV), BF),
            pltpu.VMEM((ROWS, QKV), BF),
            pltpu.VMEM((D, ROWS), BF),
            pltpu.VMEM((256, D), F32),
            pltpu.VMEM((256, ROWS), BF),
            wide_b,
            wide_b,
            wide_b,
            wide_b,
            wide,
            wide,
            wide,
            wide,
            pltpu.VMEM((256, QKV), BF),
            pltpu.SemaphoreType.DMA((16,)),
            pltpu.SemaphoreType.DMA((16,)),
        ],
        compiler_params=pltpu.CompilerParams(vmem_limit_bytes=VMEM_LIMIT),
        cost_estimate=pl.CostEstimate(
            flops=10_000_000_000, bytes_accessed=14_000_000, transcendentals=600_000
        ),
        name="block",
    )(count, table, mods, *td, tsw, *own_w, *other_w)
    return outs[0:4], outs[4:12], outs[12:20]


def add(*parts):
    total = parts[0].astype(F32)
    for part in parts[1:]:
        total = total + part.astype(F32)
    return total.astype(BF)


def local(tokens, grad_out, modulation, frame_counts, w_qkv, w_proj):
    both = ("grp", "seq")
    mine = pack(w_qkv, w_proj)
    far = lax.ppermute(mine, "grp", along_z(4))
    td = split_tokens(tokens[0, 0], grad_out[0, 0])
    tdr = {k: lax.ppermute(td[k], "seq", along_y(k)) for k in ORDER}
    tdr[0] = td[0]
    pair = jnp.concatenate([mine, far], axis=0)
    x_b = lax.ppermute(pair, "grp", along_z(-1))
    y_a = lax.ppermute(pair, both, crossed(1))
    y_b = lax.ppermute(pair, both, crossed(-2))
    xs = {0: jnp.concatenate([pair, x_b], axis=0)}
    ys = {0: jnp.concatenate([y_a, y_b], axis=0)}
    for k in ORDER:
        xs[k] = lax.ppermute(xs[0], "grp", along_x(-k))
        ys[k] = lax.ppermute(ys[0], "seq", along_y(-k))
    own = [xs[k] for k in range(4)] + [ys[k] for k in range(4)]
    other = [lax.ppermute(w, "seq", CORE_SWAP) for w in own]
    tsw = lax.ppermute(
        jnp.concatenate([tdr[k][64:128] for k in range(4)], axis=0), "seq", CORE_SWAP
    )

    gt, keep, send = compute(
        frame_counts, jnp.asarray(row_table()), modulation[0], [tdr[k] for k in range(4)], tsw, own, other
    )

    part = [None] * 8
    for i in (1, 5, 3, 7, 2, 6, 0, 4):
        part[i] = add(keep[i], lax.ppermute(send[i], "seq", CORE_SWAP))
    x_in = [lax.ppermute(part[k], "grp", along_x(k)) for k in ORDER]
    y_in = [lax.ppermute(part[4 + k], "seq", along_y(k)) for k in ORDER]
    sum_x = add(part[0], *x_in)
    sum_y = add(part[4], *y_in)
    z_in = [
        lax.ppermute(sum_x[48:96], "grp", along_z(1)),
        lax.ppermute(sum_y[0:48], both, crossed(-1)),
        lax.ppermute(sum_y[48:96], both, crossed(2)),
    ]
    near = add(sum_x[0:48], *z_in)
    block = add(near[0:HALF], lax.ppermute(near[HALF:], "grp", along_z(4)))
    r1, r3, r2 = [lax.ppermute(block, "seq", along_y(k)) for k in ORDER]
    total = (block.astype(F32) + r2.astype(F32)) + (r1.astype(F32) + r3.astype(F32))
    other_total = lax.ppermute(total, "seq", CORE_SWAP)
    first = (lax.axis_index("seq") & 1) == 0
    lower = jnp.where(first, total, other_total)
    upper = jnp.where(first, other_total, total)
    grad_qkv = jnp.concatenate([lower, upper[0:12]], axis=0)
    tail = jnp.concatenate([upper[12:18, D:QKV], upper[18:24, D:QKV]], axis=1)
    grad_proj = jnp.concatenate([upper[12:24, 0:D], tail], axis=0)

    gtr = [gt[0]] + [lax.ppermute(gt[k], "seq", along_y(-k)) for k in range(1, 4)]
    gsw = lax.ppermute(jnp.concatenate([t[32:64] for t in gtr], axis=0), "seq", CORE_SWAP)
    grad_x = join_tokens(gtr, gsw)
    return (grad_x[None, None], grad_qkv, grad_proj)


def solution(mesh):
    in_specs = (
        P("grp", "seq", None, None),
        P("grp", "seq", None, None),
        P("grp", None, None),
        P("grp"),
        P("grp", None),
        P("grp", None),
    )
    out_specs = (P("grp", "seq", None, None), P("grp", None), P("grp", None))
    return jax.shard_map(local, mesh=mesh, in_specs=in_specs, out_specs=out_specs, check_vma=False)
```

```python
import functools

import jax
import jax.numpy as jnp
import numpy as np
from jax import lax
from jax.experimental import pallas as pl
from jax.experimental.pallas import tpu as pltpu
from jax.sharding import PartitionSpec as P

BF = jnp.bfloat16
F32 = jnp.float32
HEADS = 8
HEAD = 72
D = 1152
INNER = 576
QKV = 1728
NX, NY, NZ = 4, 4, 8
HALF = 24
RING = 4 * HALF
KZ = (0, 1, 7, 2)
ORDER = (1, 3, 2)
ROWS = 16 * RING
WIDE = 640
VMEM_LIMIT = 56 * 1024 * 1024


def gid(z, x):
    return (z % NZ) * NX + x % NX


def sid(y, c):
    return (y % NY) * 2 + c % 2


CORE_SWAP = [(s, s ^ 1) for s in range(8)]


def along_z(dz):
    return [(gid(z, x), gid(z + dz, x)) for z in range(NZ) for x in range(NX)]


def along_x(dx):
    return [(gid(z, x), gid(z, x + dx)) for z in range(NZ) for x in range(NX)]


def along_y(dy):
    return [(sid(y, c), sid(y + dy, c)) for y in range(NY) for c in range(2)]


def along_z_by_plane(sign):
    return [
        (gid(z, x) * 8 + sid(y, c), gid(z + sign * (3 + y), x) * 8 + sid(y, c))
        for z in range(NZ)
        for x in range(NX)
        for y in range(NY)
        for c in range(2)
    ]


def row_table():
    n = np.arange(ROWS)
    half, n = n // (ROWS // 2), n % (ROWS // 2)
    ring, n = n // (4 * RING), n % (4 * RING)
    step, n = n // RING, n % RING
    part = n // HALF
    kz = np.where(ring == 0, np.array(KZ)[part], 0)
    kx = np.where(ring == 0, step, part)
    row = half * HALF + n % HALF
    zero = np.zeros_like(n)
    return np.stack([ring, step, kz, kx, row, zero, zero, zero]).astype(np.int32)


def position():
    g = lax.axis_index("grp")
    s = lax.axis_index("seq")
    return g & 3, s >> 1, g >> 2, s & 1


def pack_kernel(wq_ref, wp_ref, out_ref, buf):
    _, _, _, c = position()
    buf[0:36, :] = wq_ref[...].astype(F32)
    wp = wp_ref[...].astype(F32)
    buf[36:48, 0:D] = wp[0:12, :]
    tail = wp[12:18, :]
    buf[36:42, D:QKV] = tail[:, 0:INNER]
    buf[42:48, D:QKV] = pltpu.roll(tail[:, 512:D], 640 - 64, 1)[:, 0:INNER]
    out_ref[...] = buf[pl.ds(pl.multiple_of(c * HALF, 8), HALF), :].astype(BF)


def pack(w_qkv, w_proj):
    return pl.pallas_call(
        pack_kernel,
        out_shape=jax.ShapeDtypeStruct((HALF, QKV), BF),
        scratch_shapes=[pltpu.VMEM((48, QKV), F32)],
        name="pack_weights",
    )(w_qkv, w_proj)


def split_kernel(tok_ref, dy_ref, *outs):
    _, y, _, c = position()
    for k in range(4):
        base = ((y + k) & 3) * 64
        for part, core in ((0, c), (1, 1 - c)):
            off = pl.multiple_of(base + core * 32, 32)
            outs[k][part * 64 : part * 64 + 32, :] = tok_ref[pl.ds(off, 32), :]
            outs[k][part * 64 + 32 : part * 64 + 64, :] = dy_ref[pl.ds(off, 32), :]


def split_tokens(x, dy):
    return pl.pallas_call(
        split_kernel,
        out_shape=[jax.ShapeDtypeStruct((128, D), BF)] * 4,
        name="split_tokens",
    )(x, dy)


def join_kernel(g0, g1, g2, g3, swapped, out_ref):
    _, y, _, c = position()
    for k, g in enumerate((g0, g1, g2, g3)):
        base = ((y + k) & 3) * 64
        out_ref[pl.ds(pl.multiple_of(base + c * 32, 32), 32), :] = g[0:32, :]
        out_ref[pl.ds(pl.multiple_of(base + (1 - c) * 32, 32), 32), :] = swapped[
            k * 32 : k * 32 + 32, :
        ]


def join_tokens(parts, swapped):
    return pl.pallas_call(
        join_kernel,
        out_shape=jax.ShapeDtypeStruct((256, D), BF),
        name="join_tokens",
    )(*parts, swapped)


def dot(a, b, ca, cb):
    return lax.dot_general(a, b, (((ca,), (cb,)), ((), ())), preferred_element_type=F32)


def main_kernel(*refs):
    count_ref, tab_ref, mods_ref = refs[0:3]
    td = refs[3:7]
    tsw = refs[7]
    own_w = refs[8:16]
    other_w = refs[16:24]
    gt = refs[24:28]
    keep = refs[28:36]
    send = refs[36:44]
    wbuf, g, perm, nrm, modp, q_s, k_s, v_s, h_s, o_s, dq_s, dk_s, dv_s, rows_s, in_sem, out_sem = refs[44:]
    x, y, z, c = position()
    count = count_ref[0]
    half_rows = ROWS // 2

    loads = []
    for i in range(8):
        for side, src in ((c, own_w[i]), (1 - c, other_w[i])):
            off = pl.multiple_of(side * half_rows + i * RING, 32)
            copy = pltpu.make_async_copy(src, wbuf.at[pl.ds(off, RING), :], in_sem.at[len(loads)])
            copy.start()
            loads.append(copy)

    ring = tab_ref[0:1, :]
    step = tab_ref[1:2, :]
    kz = jnp.where(ring == 0, tab_ref[2:3, :], 3 + ((y + step) & 3))
    kx = tab_ref[3:4, :]
    row = tab_ref[4:5, :]
    shard = ((z + kz) & 7) * 4 + ((x + kx) & 3)
    natural = jnp.where(row < 36, shard * 36 + row, -1)
    for i in range(0, D, 128):
        ids = lax.broadcasted_iota(jnp.int32, (128, ROWS), 0) + i
        perm[i : i + 128, :] = jnp.where(ids == natural, 1.0, 0.0).astype(BF)

    xf = jnp.concatenate(
        [t[0:32, :].astype(F32) for t in td]
        + [tsw[64 * k : 64 * k + 32, :].astype(F32) for k in range(4)],
        axis=0,
    )
    mean = jnp.mean(xf, axis=-1, keepdims=True)
    cent = xf - mean
    rstd = lax.rsqrt(jnp.mean(cent * cent, axis=-1, keepdims=True) + 1e-06)
    normed = cent * rstd
    nrm[...] = normed
    modded = (normed * (1.0 + mods_ref[1:2, :]) + mods_ref[0:1, :]).astype(BF)
    modp[...] = dot(modded, perm[...], 1, 0).astype(BF)

    for copy in loads:
        copy.wait()

    lane = lax.broadcasted_iota(jnp.int32, (1, WIDE), 1)
    inner_lane = lane < INNER
    mp = modp[...]
    front = dot(mp, wbuf[:, 0:D], 1, 0)
    q_s[...] = jnp.where(inner_lane, front[:, 0:WIDE], 0.0).astype(BF)
    k_s[...] = jnp.where(inner_lane, pltpu.roll(front[:, 512:D], WIDE - 64, 1), 0.0).astype(BF)
    v_s[:, 512:WIDE] = jnp.zeros((256, 128), BF)
    v_s[:, 0:INNER] = dot(mp, wbuf[:, D:QKV], 1, 0).astype(BF)

    r = lax.broadcasted_iota(jnp.int32, (256, 1), 0)
    rf = (((y - (r >> 5)) & 3) * 2) + (c ^ (r >> 7))
    col = lax.broadcasted_iota(jnp.int32, (1, 256), 1)
    cf = (((y - (col >> 5)) & 3) * 2) + (c ^ (col >> 7))
    live = jnp.where(rf < count, 1.0, 0.0)
    dyf = jnp.concatenate(
        [t[32:64, :].astype(F32) for t in td]
        + [tsw[64 * k + 32 : 64 * k + 64, :].astype(F32) for k in range(4)],
        axis=0,
    )
    gated_f = mods_ref[2:3, :] * live * dyf
    gated = gated_f.astype(BF)
    gated_lo = gated[:, 0:INNER]
    gated_hi = pltpu.roll(gated_f[:, 512:D], WIDE - 64, 1)[:, 0:INNER].astype(BF)

    row1 = row[:, half_rows:]
    shard1 = shard[:, half_rows:]
    ids = lax.broadcasted_iota(jnp.int32, (INNER, half_rows), 0)
    pick_main = jnp.where(ids == jnp.where(row1 >= 36, shard1 * 18 + row1 - 36, -1), 1.0, 0.0).astype(BF)
    pick_lo = jnp.where(
        ids == jnp.where((row1 >= 36) & (row1 < 42), shard1 * 18 + row1 - 24, -1), 1.0, 0.0
    ).astype(BF)
    pick_hi = jnp.where(ids == jnp.where(row1 >= 42, shard1 * 18 + row1 - 30, -1), 1.0, 0.0).astype(BF)
    w1 = wbuf[half_rows:, :]
    gh_main = dot(gated, w1[:, 0:D], 1, 1).astype(BF)
    gh_lo = dot(gated_lo, w1[:, D:QKV], 1, 1).astype(BF)
    gh_hi = dot(gated_hi, w1[:, D:QKV], 1, 1).astype(BF)
    gh = dot(gh_main, pick_main, 1, 1) + dot(gh_lo, pick_lo, 1, 1) + dot(gh_hi, pick_hi, 1, 1)
    h_s[:, 512:WIDE] = jnp.zeros((256, 128), BF)
    h_s[:, 0:INNER] = gh.astype(BF)

    same = ((r & 31) == (col & 31)) & (cf < count)
    factor = HEAD ** (-0.5)
    for ref in (o_s, dq_s, dk_s, dv_s):
        ref[...] = jnp.zeros_like(ref)
    for h in range(HEADS):
        lo = h * HEAD
        start = lo // 128 * 128
        stop = -(-(lo + HEAD) // 128) * 128
        win = slice(start, stop)
        lanes = lax.broadcasted_iota(jnp.int32, (1, stop - start), 1) + start
        inside = (lanes >= lo) & (lanes < lo + HEAD)
        zero = jnp.zeros((), BF)
        qm = jnp.where(inside, q_s[:, win], zero)
        km = jnp.where(inside, k_s[:, win], zero)
        vm = jnp.where(inside, v_s[:, win], zero)
        gm = jnp.where(inside, h_s[:, win], zero)
        scores = jnp.where(same, dot(qm, km, 1, 1) * factor, -1e30)
        top = jnp.max(scores, axis=-1, keepdims=True)
        expd = jnp.exp(scores - top)
        probs = expd / jnp.sum(expd, axis=-1, keepdims=True)
        probs_b = probs.astype(BF)
        o_s[:, win] += dot(probs_b, vm, 1, 0)
        dprobs = dot(gm, vm, 1, 1)
        dv_s[:, win] += dot(probs_b, gm, 0, 0)
        delta = jnp.sum(probs * dprobs, axis=-1, keepdims=True)
        ds = (probs * (dprobs - delta) * factor).astype(BF)
        dq_s[:, win] += dot(ds, km, 1, 0)
        dk_s[:, win] += dot(ds, qm, 0, 0)

    dkr = pltpu.roll(dk_s[...], 64, 1)
    rows_s[:, 0:512] = dq_s[:, 0:512].astype(BF)
    rows_s[:, 512:640] = (dq_s[:, 512:640] + dkr[:, 0:128]).astype(BF)
    rows_s[:, 640:D] = dkr[:, 128:640].astype(BF)
    rows_s[:, D:QKV] = dv_s[:, 0:INNER].astype(BF)

    heads_out = o_s[:, 0:INNER].astype(BF)
    h_main = dot(heads_out, pick_main, 1, 0).astype(BF)
    h_lo = dot(heads_out, pick_lo, 1, 0).astype(BF)
    h_hi = dot(heads_out, pick_hi, 1, 0).astype(BF)
    rows = rows_s[...]
    for i in range(0, half_rows, 256):
        g[i : i + 256, :] = dot(modp[:, i : i + 256], rows, 0, 0).astype(BF)
    for i in range(0, half_rows, 256):
        m = modp[:, half_rows + i : half_rows + i + 256]
        at = slice(half_rows + i, half_rows + i + 256)
        g[at, 0:D] = (dot(m, rows[:, 0:D], 0, 0) + dot(h_main[:, i : i + 256], gated, 0, 0)).astype(BF)
        g[at, D:QKV] = (
            dot(m, rows[:, D:QKV], 0, 0)
            + dot(h_lo[:, i : i + 256], gated_lo, 0, 0)
            + dot(h_hi[:, i : i + 256], gated_hi, 0, 0)
        ).astype(BF)
    stores = []
    for side, dst in ((1 - c, send), (c, keep)):
        for i in range(8):
            off = pl.multiple_of(side * half_rows + i * RING, 32)
            copy = pltpu.make_async_copy(g.at[pl.ds(off, RING), :], dst[i], out_sem.at[len(stores)])
            copy.start()
            stores.append(copy)

    gmp = dot(rows, wbuf[...], 1, 1).astype(BF)
    grad_modded = dot(gmp, perm[...], 1, 1)
    dn = grad_modded * (1.0 + mods_ref[1:2, :])
    normed = nrm[...]
    mean_dn = jnp.mean(dn, axis=-1, keepdims=True)
    mean_dnn = jnp.mean(dn * normed, axis=-1, keepdims=True)
    grad_x = (dyf + rstd * (dn - mean_dn - normed * mean_dnn)).astype(BF)
    for k in range(4):
        gt[k][0:32, :] = grad_x[32 * k : 32 * k + 32, :]
        gt[k][32:64, :] = grad_x[128 + 32 * k : 128 + 32 * k + 32, :]
    for copy in stores:
        copy.wait()


def compute(count, table, mods, td, tsw, own_w, other_w):
    vmem = pl.BlockSpec(memory_space=pltpu.VMEM)
    smem = pl.BlockSpec(memory_space=pltpu.SMEM)
    hbm = pl.BlockSpec(memory_space=pl.ANY)
    wide = pltpu.VMEM((256, WIDE), F32)
    wide_b = pltpu.VMEM((256, WIDE), BF)
    outs = pl.pallas_call(
        main_kernel,
        in_specs=[smem, vmem, vmem] + [vmem] * 5 + [hbm] * 16,
        out_specs=[vmem] * 4 + [hbm] * 16,
        out_shape=[jax.ShapeDtypeStruct((64, D), BF)] * 4
        + [jax.ShapeDtypeStruct((RING, QKV), BF)] * 16,
        scratch_shapes=[
            pltpu.VMEM((ROWS, QKV), BF),
            pltpu.VMEM((ROWS, QKV), BF),
            pltpu.VMEM((D, ROWS), BF),
            pltpu.VMEM((256, D), F32),
            pltpu.VMEM((256, ROWS), BF),
            wide_b,
            wide_b,
            wide_b,
            wide_b,
            wide,
            wide,
            wide,
            wide,
            pltpu.VMEM((256, QKV), BF),
            pltpu.SemaphoreType.DMA((16,)),
            pltpu.SemaphoreType.DMA((16,)),
        ],
        compiler_params=pltpu.CompilerParams(vmem_limit_bytes=VMEM_LIMIT),
        cost_estimate=pl.CostEstimate(
            flops=10_000_000_000, bytes_accessed=14_000_000, transcendentals=600_000
        ),
        name="block",
    )(count, table, mods, *td, tsw, *own_w, *other_w)
    return outs[0:4], outs[4:12], outs[12:20]


def add(*parts):
    total = parts[0].astype(F32)
    for part in parts[1:]:
        total = total + part.astype(F32)
    return total.astype(BF)


def sum_kernel(*refs):
    parts, outs = refs[:4], refs[4:]
    total = parts[0][...].astype(F32)
    for part in parts[1:]:
        total = total + part[...].astype(F32)
    for k, out in enumerate(outs):
        out[...] = total[HALF * k : HALF * k + HALF, :].astype(BF)


def sum_blocks(parts):
    return pl.pallas_call(
        sum_kernel,
        out_shape=[jax.ShapeDtypeStruct((HALF, QKV), BF)] * 4,
        name="sum_blocks",
    )(*parts)


def local(tokens, grad_out, modulation, frame_counts, w_qkv, w_proj):
    both = ("grp", "seq")
    barrier = lax.optimization_barrier
    mine = pack(w_qkv, w_proj)
    plane = lax.ppermute(mine, both, along_z_by_plane(-1))
    zs = [lax.ppermute(mine, "grp", along_z(-kz)) for kz in KZ[1:]]
    td = split_tokens(tokens[0, 0], grad_out[0, 0])
    tdr = {k: lax.ppermute(td[k], "seq", along_y(k)) for k in ORDER}
    tdr[0] = td[0]
    plane_x = dict(zip(ORDER, barrier([lax.ppermute(plane, "grp", along_x(-k)) for k in ORDER])))
    xs = {0: jnp.concatenate([mine, *zs], axis=0)}
    ys = {0: jnp.concatenate([plane, plane_x[1], plane_x[2], plane_x[3]], axis=0)}
    for k in ORDER:
        xs[k] = lax.ppermute(xs[0], "grp", along_x(-k))
        ys[k] = lax.ppermute(ys[0], "seq", along_y(-k))
    own = barrier([xs[k] for k in range(4)] + [ys[k] for k in range(4)])
    other = [lax.ppermute(w, "seq", CORE_SWAP) for w in own]
    tsw = lax.ppermute(
        jnp.concatenate([tdr[k][64:128] for k in range(4)], axis=0), "seq", CORE_SWAP
    )

    gt, keep, send = compute(
        frame_counts, jnp.asarray(row_table()), modulation[0], [tdr[k] for k in range(4)], tsw, own, other
    )

    part = [None] * 8
    for i in (1, 5, 3, 7, 2, 6, 0, 4):
        part[i] = add(keep[i], lax.ppermute(send[i], "seq", CORE_SWAP))
    x_in = [lax.ppermute(part[k], "grp", along_x(k)) for k in ORDER]
    y_in = [lax.ppermute(part[4 + k], "seq", along_y(k)) for k in ORDER]
    heavy = barrier(x_in + y_in)
    y_sums = sum_blocks([part[4], *heavy[3:]])
    x_sums = sum_blocks([part[0], *heavy[:3]])
    plane_in = [lax.ppermute(y_sums[k], "grp", along_x(k)) for k in ORDER]
    z_in = [lax.ppermute(x_sums[i], "grp", along_z(KZ[i])) for i in (1, 2, 3)]
    *plane_in, z1, z2, z3 = barrier(plane_in + z_in)
    z_in = [z1, z2, z3]
    plane_sum = add(y_sums[0], *plane_in)
    plane_home = lax.ppermute(plane_sum, both, along_z_by_plane(1))
    block = add(x_sums[0], *z_in, plane_home)
    r1, r3, r2 = [lax.ppermute(block, "seq", along_y(k)) for k in ORDER]
    total = (block.astype(F32) + r2.astype(F32)) + (r1.astype(F32) + r3.astype(F32))
    other_total = lax.ppermute(total, "seq", CORE_SWAP)
    first = (lax.axis_index("seq") & 1) == 0
    lower = jnp.where(first, total, other_total)
    upper = jnp.where(first, other_total, total)
    grad_qkv = jnp.concatenate([lower, upper[0:12]], axis=0)
    tail = jnp.concatenate([upper[12:18, D:QKV], upper[18:24, D:QKV]], axis=1)
    grad_proj = jnp.concatenate([upper[12:24, 0:D], tail], axis=0)

    gtr = [gt[0]] + [lax.ppermute(gt[k], "seq", along_y(-k)) for k in range(1, 4)]
    gsw = lax.ppermute(jnp.concatenate([t[32:64] for t in gtr], axis=0), "seq", CORE_SWAP)
    grad_x = join_tokens(gtr, gsw)
    return (grad_x[None, None], grad_qkv, grad_proj)


def solution(mesh):
    in_specs = (
        P("grp", "seq", None, None),
        P("grp", "seq", None, None),
        P("grp", None, None),
        P("grp"),
        P("grp", None),
        P("grp", None),
    )
    out_specs = (P("grp", "seq", None, None), P("grp", None), P("grp", None))
    return jax.shard_map(local, mesh=mesh, in_specs=in_specs, out_specs=out_specs, check_vma=False)
```

```python
import jax
import jax.numpy as jnp
import numpy as np
from jax import lax
from jax.experimental import pallas as pl
from jax.experimental.pallas import tpu as pltpu
from jax.sharding import PartitionSpec as P

BF = jnp.bfloat16
F32 = jnp.float32
HEAD = 72
D = 1152
INNER = 576
QKV = 1728
OWN = 288
LANES = 896
NX, NY, NZ = 4, 4, 8
MSG = 64
PAIR = 96
RING = 2 * PAIR
ROWS = 8 * RING
PROJ = 512
KZ = ((0, 1), (7, 2))
ORDER = (1, 3, 2)
TOK = 512
WIDE = 384
VMEM_LIMIT = 40 * 1024 * 1024


def gid(z, x):
    return (z % NZ) * NX + x % NX


def sid(y, c):
    return (y % NY) * 2 + c % 2


CORE_SWAP = [(s, s ^ 1) for s in range(8)]


def along_z(dz):
    return [(gid(z, x), gid(z + dz, x)) for z in range(NZ) for x in range(NX)]


def along_x(dx):
    return [(gid(z, x), gid(z, x + dx)) for z in range(NZ) for x in range(NX)]


def along_y(dy):
    return [(sid(y, c), sid(y + dy, c)) for y in range(NY) for c in range(2)]


def slanted(sign, dz):
    return [
        (gid(z, x) * 8 + sid(y, c), gid(z + dz, x + sign * y) * 8 + sid(y, c))
        for z in range(NZ)
        for x in range(NX)
        for y in range(NY)
        for c in range(2)
    ]


def row_table(per_pair):
    n = np.arange(16 * per_pair)
    pair, r = n // per_pair, n % per_pair + PAIR - per_pair
    ring, step, part = pair // 8, pair // 2 % 4, pair % 2
    zero = np.zeros_like(n)
    kz = np.array(KZ)[ring, part]
    return np.stack([ring, step, kz, r, zero, zero, zero, zero]).astype(np.int32)


def position():
    g = lax.axis_index("grp")
    s = lax.axis_index("seq")
    return g & 3, s >> 1, g >> 2, s & 1


def dot(a, b, ca, cb):
    return lax.dot_general(a, b, (((ca,), (cb,)), ((), ())), preferred_element_type=F32)


def places(tab):
    x, y, z, _ = position()
    step = tab[1:2, :]
    xs = (x + jnp.where(tab[0:1, :] == 0, step, y + step)) & 3
    return xs, (z + tab[2:3, :]) & 7, tab[3:4, :]


def fill_perm(tab, perm):
    xs, a, r = places(tab)
    first = (a * 4 + xs) * 36 + r
    second = (((a + 4) & 7) * 4 + xs) * 36 + r - 36
    natural = jnp.where(r < 36, first, jnp.where(r < 72, second, -1))
    for i in range(0, D, 128):
        ids = lax.broadcasted_iota(jnp.int32, (128, ROWS), 0) + i
        perm[i : i + 128, :] = jnp.where(ids == natural, 1.0, 0.0).astype(BF)


def pack_kernel(wq_ref, wp_ref, out_ref, buf):
    _, _, _, c = position()
    wq = wq_ref[...].astype(F32)
    pad = jnp.zeros((36, LANES - 3 * OWN), F32)

    def part(core):
        cols = [wq[:, b * INNER + core * OWN : b * INNER + core * OWN + OWN] for b in range(3)]
        return jnp.concatenate(cols + [pad], axis=1)

    buf[...] = jnp.zeros_like(buf)
    buf[0:36, :] = jnp.where(c == 0, part(0), part(1))
    wp = wp_ref[...].astype(F32)
    buf[40:58, :] = wp[:, 0:LANES]
    for u in range(3):
        buf[58:64, 256 * u : 256 * u + 256] = wp[6 * u : 6 * u + 6, LANES:D]
    out_ref[...] = buf[...].astype(BF)


def pack(w_qkv, w_proj):
    return pl.pallas_call(
        pack_kernel,
        out_shape=jax.ShapeDtypeStruct((MSG, LANES), BF),
        scratch_shapes=[pltpu.VMEM((MSG, LANES), F32)],
        name="pack_weights",
    )(w_qkv, w_proj)


def pair_kernel(mine_ref, far_ref, out_ref, buf):
    _, _, z, c = position()
    mine = mine_ref[...].astype(F32)
    far = far_ref[...].astype(F32)
    buf[0:36, :] = mine[0:36, :]
    buf[36:72, :] = far[0:36, :]
    buf[72:96, :] = jnp.where((z >> 2) == c, mine[40:64, :], far[40:64, :])
    out_ref[...] = buf[...].astype(BF)


def make_pair(mine, far):
    return pl.pallas_call(
        pair_kernel,
        out_shape=jax.ShapeDtypeStruct((PAIR, LANES), BF),
        scratch_shapes=[pltpu.VMEM((PAIR, LANES), F32)],
        name="pair_weights",
    )(mine, far)


def split_kernel(tok_ref, dy_ref, *outs):
    _, y, _, _ = position()
    for k in range(4):
        off = pl.multiple_of(((y + k) & 3) * 64, 64)
        outs[k][0:64, :] = tok_ref[pl.ds(off, 64), :]
        outs[k][64:128, :] = dy_ref[pl.ds(off, 64), :]


def split_tokens(x, dy):
    return pl.pallas_call(
        split_kernel,
        out_shape=[jax.ShapeDtypeStruct((128, D), BF)] * 4,
        name="split_tokens",
    )(x, dy)


def join_kernel(g0, g1, g2, g3, out_ref):
    _, y, _, _ = position()
    for k, g in enumerate((g0, g1, g2, g3)):
        out_ref[pl.ds(pl.multiple_of(((y + k) & 3) * 64, 64), 64), :] = g[...]


def join_tokens(parts):
    return pl.pallas_call(
        join_kernel,
        out_shape=jax.ShapeDtypeStruct((256, D), BF),
        name="join_tokens",
    )(*parts)


def normalize(xf):
    mean = jnp.mean(xf, axis=-1, keepdims=True)
    cent = xf - mean
    rstd = lax.rsqrt(jnp.mean(cent * cent, axis=-1, keepdims=True) + 1e-06)
    return cent * rstd, rstd


def gather_rows(parts, base):
    return jnp.concatenate(
        [p[base + 32 * s : base + 32 * s + 32, :].astype(F32) for s in range(2) for p in parts], axis=0
    )


def frames_of(index, y, c):
    return (((y - (index >> 5)) & 3) * 2) + (c ^ ((index >> 7) & 1))


def prepare_kernel(count_ref, tab_ref, mods_ref, *refs):
    td, (modp_ref, gated_ref, perm) = refs[0:8], refs[8:]
    _, y, _, c = position()
    fill_perm(tab_ref[...], perm)
    normed, _ = normalize(gather_rows(td, 0))
    modded = (normed * (1.0 + mods_ref[1:2, :]) + mods_ref[0:1, :]).astype(BF)
    modp_ref[...] = dot(modded, perm[...], 1, 0).astype(BF)
    index = lax.broadcasted_iota(jnp.int32, (TOK, 1), 0)
    live = jnp.where(frames_of(index, y, c) < count_ref[0], 1.0, 0.0)
    gated_ref[...] = (mods_ref[2:3, :] * live * gather_rows(td, 64)).astype(BF)


def specs(kinds):
    of = {"s": pltpu.SMEM, "v": pltpu.VMEM, "a": pl.ANY}
    return [pl.BlockSpec(memory_space=of[k]) for k in kinds]


def prepare(count, table, mods, td):
    return pl.pallas_call(
        prepare_kernel,
        in_specs=specs("s" + "v" * 10),
        out_specs=specs("vv"),
        out_shape=[jax.ShapeDtypeStruct((TOK, ROWS), BF), jax.ShapeDtypeStruct((TOK, D), BF)],
        scratch_shapes=[pltpu.VMEM((D, ROWS), BF)],
        compiler_params=pltpu.CompilerParams(vmem_limit_bytes=VMEM_LIMIT),
        cost_estimate=pl.CostEstimate(
            flops=2_000_000_000, bytes_accessed=6_000_000, transcendentals=512
        ),
        name="prepare",
    )(count, table, mods, *td)


def load_weights(w, wbuf, sem):
    loads = []
    for i in range(8):
        copy = pltpu.make_async_copy(w[i], wbuf.at[pl.ds(i * RING, RING), :], sem.at[i])
        copy.start()
        loads.append(copy)
    return loads


def main_kernel(count_ref, tab_ref, modp, gated, *refs):
    w = refs[0:8]
    rows_ref = refs[8]
    g_out = refs[9:17]
    wbuf, g, gf, gp, q_s, k_s, v_s, h_s, o_s, dq_s, dk_s, dv_s, in_sem, out_sem = refs[17:]
    _, y, _, c = position()
    loads = load_weights(w, wbuf, in_sem)

    xs, a, r = places(tab_ref[...])
    inner = jnp.where((r >= 72) & (r < 90), ((a & 3) * 4 + xs) * 18 + r - 72, -1)
    pick = jnp.where(
        lax.broadcasted_iota(jnp.int32, (WIDE, PROJ), 0) == inner, 1.0, 0.0
    ).astype(BF)
    main_lane = (r >= 72) & (r < 90)
    tail_lane = r >= 90

    for copy in loads:
        copy.wait()

    lane = lax.broadcasted_iota(jnp.int32, (1, WIDE), 1)
    own_lane = lane < OWN
    qkv = dot(modp[...], wbuf[...], 1, 0)
    q_s[...] = jnp.where(own_lane, qkv[:, 0:384], 0.0).astype(BF)
    k_s[...] = jnp.where(own_lane, pltpu.roll(qkv[:, 256:640], WIDE - 32, 1), 0.0).astype(BF)
    v_s[...] = jnp.where(own_lane, pltpu.roll(qkv[:, 512:896], WIDE - 64, 1), 0.0).astype(BF)

    wp = jnp.concatenate([wbuf[PAIR * p + 64 : PAIR * p + 96, :] for p in range(16)], axis=0)
    g_lo = gated[:, 0:LANES]
    g_hi = gated[:, LANES:D]
    ghp = jnp.where(main_lane, dot(g_lo, wp, 1, 1), 0.0)
    for u in range(3):
        tail = dot(g_hi, wp[:, 256 * u : 256 * u + 256], 1, 1)
        ghp += pltpu.roll(jnp.where(tail_lane, tail, 0.0), PROJ + 6 * u - 18, 1)
    h_s[...] = dot(ghp.astype(BF), pick, 1, 1).astype(BF)

    row = lax.broadcasted_iota(jnp.int32, (256, 1), 0)
    col = lax.broadcasted_iota(jnp.int32, (1, 256), 1)
    same = ((row & 31) == (col & 31)) & (frames_of(col, y, c) < count_ref[0])
    factor = HEAD ** (-0.5)
    for ref in (o_s, dq_s, dk_s, dv_s):
        ref[...] = jnp.zeros_like(ref)
    zero = jnp.zeros((), BF)
    for s in range(2):
        at = slice(256 * s, 256 * s + 256)
        for h in range(4):
            lo = h * HEAD
            start = lo // 128 * 128
            stop = -(-(lo + HEAD) // 128) * 128
            win = slice(start, stop)
            lanes = lax.broadcasted_iota(jnp.int32, (1, stop - start), 1) + start
            inside = (lanes >= lo) & (lanes < lo + HEAD)
            qm = jnp.where(inside, q_s[at, win], zero)
            km = jnp.where(inside, k_s[at, win], zero)
            vm = jnp.where(inside, v_s[at, win], zero)
            gm = jnp.where(inside, h_s[at, win], zero)
            scores = jnp.where(same, dot(qm, km, 1, 1) * factor, -1e30)
            top = jnp.max(scores, axis=-1, keepdims=True)
            expd = jnp.exp(scores - top)
            probs = expd / jnp.sum(expd, axis=-1, keepdims=True)
            probs_b = probs.astype(BF)
            o_s[at, win] += dot(probs_b, vm, 1, 0)
            dprobs = dot(gm, vm, 1, 1)
            dv_s[at, win] += dot(probs_b, gm, 0, 0)
            delta = jnp.sum(probs * dprobs, axis=-1, keepdims=True)
            ds = (probs * (dprobs - delta) * factor).astype(BF)
            dq_s[at, win] += dot(ds, km, 1, 0)
            dk_s[at, win] += dot(ds, qm, 0, 0)

    dkr = pltpu.roll(dk_s[...], 32, 1)
    dvr = pltpu.roll(dv_s[...], 64, 1)
    rows_ref[:, 0:256] = dq_s[:, 0:256].astype(BF)
    rows_ref[:, 256:384] = (dq_s[:, 256:384] + dkr[:, 0:128]).astype(BF)
    rows_ref[:, 384:512] = dkr[:, 128:256].astype(BF)
    rows_ref[:, 512:640] = (dkr[:, 256:384] + dvr[:, 0:128]).astype(BF)
    rows_ref[:, 640:896] = dvr[:, 128:384].astype(BF)

    hmf = dot(o_s[...].astype(BF), pick, 1, 0)
    gp[...] = dot(hmf.astype(BF), g_lo, 0, 0)
    for u in range(3):
        h_u = jnp.where(tail_lane, pltpu.roll(hmf, 18 - 6 * u, 1), 0.0).astype(BF)
        gp[:, 256 * u : 256 * u + 256] += dot(h_u, g_hi, 0, 0)
    rows = rows_ref[...]
    stores = []
    for j in range(4):
        gf[...] = dot(modp[:, 384 * j : 384 * j + 384], rows, 0, 0)
        for p in range(4):
            n = 4 * j + p
            gf[PAIR * p + 64 : PAIR * p + 96, :] += gp[32 * n : 32 * n + 32, :]
        g[384 * j : 384 * j + 384, :] = gf[...].astype(BF)
        for i in (2 * j, 2 * j + 1):
            copy = pltpu.make_async_copy(g.at[pl.ds(i * RING, RING), :], g_out[i], out_sem.at[i])
            copy.start()
            stores.append(copy)
    for copy in stores:
        copy.wait()


def compute(count, table, modp, gated, w):
    wide = pltpu.VMEM((TOK, WIDE), F32)
    wide_b = pltpu.VMEM((TOK, WIDE), BF)
    outs = pl.pallas_call(
        main_kernel,
        in_specs=specs("svvv" + "a" * 8),
        out_specs=specs("v" + "a" * 8),
        out_shape=[jax.ShapeDtypeStruct((TOK, LANES), BF)]
        + [jax.ShapeDtypeStruct((RING, LANES), BF)] * 8,
        scratch_shapes=[
            pltpu.VMEM((ROWS, LANES), BF),
            pltpu.VMEM((ROWS, LANES), BF),
            pltpu.VMEM((384, LANES), F32),
            pltpu.VMEM((PROJ, LANES), F32),
            wide_b,
            wide_b,
            wide_b,
            wide_b,
            wide,
            wide,
            wide,
            wide,
            pltpu.SemaphoreType.DMA((8,)),
            pltpu.SemaphoreType.DMA((8,)),
        ],
        compiler_params=pltpu.CompilerParams(vmem_limit_bytes=VMEM_LIMIT),
        cost_estimate=pl.CostEstimate(
            flops=7_000_000_000, bytes_accessed=9_000_000, transcendentals=600_000
        ),
        name="block",
    )(count, table, modp, gated, *w)
    return outs[0], outs[1:]


def back_kernel(tab_ref, rows, *refs):
    w = refs[0:8]
    own_ref, other_ref, wbuf, perm, sem = refs[8:]
    loads = load_weights(w, wbuf, sem)
    fill_perm(tab_ref[...], perm)
    for copy in loads:
        copy.wait()
    packed = dot(rows[...], wbuf[...], 1, 1).astype(BF)
    part = dot(packed, perm[...], 1, 1).astype(BF)
    for s in range(2):
        own_ref[128 * s : 128 * s + 128, :] = part[256 * s : 256 * s + 128, :]
        other_ref[128 * s : 128 * s + 128, :] = part[256 * s + 128 : 256 * s + 256, :]


def back(table, rows, w):
    return pl.pallas_call(
        back_kernel,
        in_specs=specs("vv" + "a" * 8),
        out_specs=specs("vv"),
        out_shape=[jax.ShapeDtypeStruct((256, D), BF)] * 2,
        scratch_shapes=[
            pltpu.VMEM((ROWS, LANES), BF),
            pltpu.VMEM((D, ROWS), BF),
            pltpu.SemaphoreType.DMA((8,)),
        ],
        compiler_params=pltpu.CompilerParams(vmem_limit_bytes=VMEM_LIMIT),
        cost_estimate=pl.CostEstimate(
            flops=3_400_000_000, bytes_accessed=6_000_000, transcendentals=0
        ),
        name="back",
    )(table, rows, *w)


def final_kernel(mods_ref, own_ref, other_ref, *refs):
    td, gt = refs[0:4], refs[4:]
    normed, rstd = normalize(gather_rows(td, 0))
    grad_modded = (own_ref[...].astype(F32) + other_ref[...].astype(F32)).astype(BF).astype(F32)
    dn = grad_modded * (1.0 + mods_ref[1:2, :])
    mean_dn = jnp.mean(dn, axis=-1, keepdims=True)
    mean_dnn = jnp.mean(dn * normed, axis=-1, keepdims=True)
    grad_x = (gather_rows(td, 64) + rstd * (dn - mean_dn - normed * mean_dnn)).astype(BF)
    for s in range(2):
        for k in range(4):
            gt[k][32 * s : 32 * s + 32, :] = grad_x[128 * s + 32 * k : 128 * s + 32 * k + 32, :]


def finish(mods, own, other, td):
    return pl.pallas_call(
        final_kernel,
        out_shape=[jax.ShapeDtypeStruct((64, D), BF)] * 4,
        compiler_params=pltpu.CompilerParams(vmem_limit_bytes=VMEM_LIMIT),
        name="finish",
    )(mods, own, other, *td)


def sum_kernel(*refs):
    parts, outs = refs[:4], refs[4:]
    total = parts[0][...].astype(F32)
    for part in parts[1:]:
        total = total + part[...].astype(F32)
    for k, out in enumerate(outs):
        out[...] = total[PAIR * k : PAIR * k + PAIR, :].astype(BF)


def sum_ring(parts):
    return pl.pallas_call(
        sum_kernel,
        out_shape=[jax.ShapeDtypeStruct((PAIR, LANES), BF)] * 2,
        name="sum_ring",
    )(*parts)


def fold_kernel(*refs):
    parts, (keep, send, buf) = refs[:4], refs[4:]
    total = parts[0][...].astype(F32)
    for part in parts[1:]:
        total = total + part[...].astype(F32)
    gap = jnp.zeros((4, LANES), F32)
    for out, lo in ((keep, 0), (send, 36)):
        buf[0:36, :] = total[lo : lo + 36, :]
        buf[36:40, :] = gap
        buf[40:64, :] = total[72:96, :]
        out[...] = buf[...].astype(BF)


def fold(parts):
    return pl.pallas_call(
        fold_kernel,
        out_shape=[jax.ShapeDtypeStruct((MSG, LANES), BF)] * 2,
        scratch_shapes=[pltpu.VMEM((MSG, LANES), F32)],
        name="fold",
    )(*parts)


def unpack_kernel(own_ref, other_ref, gq_ref, gp_ref):
    _, _, z, c = position()
    own, other = own_ref[...], other_ref[...]
    first = jnp.where(c == 0, own, other)[0:36, :]
    second = jnp.where(c == 0, other, own)[0:36, :]
    cols = []
    for b in range(3):
        cols += [first[:, b * OWN : b * OWN + OWN], second[:, b * OWN : b * OWN + OWN]]
    gq_ref[...] = jnp.concatenate(cols, axis=1)
    proj = jnp.where((z >> 2) == c, own, other)
    gp_ref[:, 0:LANES] = proj[40:58, :]
    for u in range(3):
        gp_ref[6 * u : 6 * u + 6, LANES:D] = proj[58:64, 256 * u : 256 * u + 256]


def unpack(own, other):
    return pl.pallas_call(
        unpack_kernel,
        out_shape=[jax.ShapeDtypeStruct((36, QKV), F32), jax.ShapeDtypeStruct((18, D), F32)],
        name="unpack_grads",
    )(own, other)


def add(*parts):
    total = parts[0].astype(F32)
    for part in parts[1:]:
        total = total + part.astype(F32)
    return total.astype(BF)


def local(tokens, grad_out, modulation, frame_counts, w_qkv, w_proj):
    both = ("grp", "seq")
    barrier = lax.optimization_barrier
    mods = modulation[0]
    table = jnp.asarray(row_table(PAIR))
    mine = pack(w_qkv, w_proj)
    far = lax.ppermute(mine, "grp", along_z(4))
    td = split_tokens(tokens[0, 0], grad_out[0, 0])
    tdr = {k: lax.ppermute(td[k], "seq", along_y(k)) for k in ORDER}
    tdr[0] = td[0]
    pair = make_pair(mine, far)
    y_a = lax.ppermute(pair, both, slanted(-1, 1))
    y_b = lax.ppermute(pair, both, slanted(-1, -2))
    x_b = lax.ppermute(pair, "grp", along_z(-1))
    xs = {0: jnp.concatenate([pair, x_b], axis=0)}
    ys = {0: jnp.concatenate([y_a, y_b], axis=0)}
    for k in ORDER:
        xs[k] = lax.ppermute(xs[0], "grp", along_x(-k))
        ys[k] = lax.ppermute(ys[0], "seq", along_y(-k))
    w = [xs[k] for k in range(4)] + [ys[k] for k in range(4)]
    own_td = [tdr[k] for k in range(4)]
    other_td = [lax.ppermute(t, "seq", CORE_SWAP) for t in own_td]
    modp, gated = prepare(frame_counts, table, mods, own_td + other_td)

    rows, grads = compute(frame_counts, jnp.asarray(row_table(32)), modp, gated, w)

    x_in = [lax.ppermute(grads[k], "grp", along_x(k)) for k in ORDER]
    y_in = [lax.ppermute(grads[4 + k], "seq", along_y(k)) for k in ORDER]
    x_near, x_next = sum_ring([grads[0], *x_in])
    y_a, y_b = sum_ring([grads[4], *y_in])
    z_in = barrier(
        [
            lax.ppermute(y_a, both, slanted(1, -1)),
            lax.ppermute(y_b, both, slanted(1, 2)),
            lax.ppermute(x_next, "grp", along_z(1)),
        ]
    )
    keep, send = fold([x_near, *z_in])
    block = add(keep, lax.ppermute(send, "grp", along_z(4)))
    r1, r3, r2 = [lax.ppermute(block, "seq", along_y(k)) for k in ORDER]
    total = (block.astype(F32) + r2.astype(F32)) + (r1.astype(F32) + r3.astype(F32))
    grad_qkv, grad_proj = unpack(total, lax.ppermute(total, "seq", CORE_SWAP))

    own_part, other_part = back(table, rows, w)
    gt = finish(mods, own_part, lax.ppermute(other_part, "seq", CORE_SWAP), own_td)
    grad_x = join_tokens([gt[0]] + [lax.ppermute(gt[k], "seq", along_y(-k)) for k in range(1, 4)])
    return (grad_x[None, None], grad_qkv, grad_proj)


def solution(mesh):
    in_specs = (
        P("grp", "seq", None, None),
        P("grp", "seq", None, None),
        P("grp", None, None),
        P("grp"),
        P("grp", None),
        P("grp", None),
    )
    out_specs = (P("grp", "seq", None, None), P("grp", None), P("grp", None))
    return jax.shard_map(local, mesh=mesh, in_specs=in_specs, out_specs=out_specs, check_vma=False)
```

```python
import jax
import jax.numpy as jnp
import numpy as np
from jax import lax
from jax.experimental import pallas as pl
from jax.experimental.pallas import tpu as pltpu
from jax.sharding import PartitionSpec as P

BF = jnp.bfloat16
F32 = jnp.float32
HEAD = 72
D = 1152
INNER = 576
QKV = 1728
OWN = 288
LANES = 896
NX, NY, NZ = 4, 4, 8
MSG = 64
PAIR = 96
RING = 2 * PAIR
ROWS = 8 * RING
PROJ = 512
KZ = ((0, 1), (7, 2))
ORDER = (1, 3, 2)
TOK = 512
WIDE = 384
VMEM_LIMIT = 40 * 1024 * 1024


def gid(z, x):
    return (z % NZ) * NX + x % NX


def sid(y, c):
    return (y % NY) * 2 + c % 2


CORE_SWAP = [(s, s ^ 1) for s in range(8)]


def along_z(dz):
    return [(gid(z, x), gid(z + dz, x)) for z in range(NZ) for x in range(NX)]


def along_x(dx):
    return [(gid(z, x), gid(z, x + dx)) for z in range(NZ) for x in range(NX)]


def along_y(dy):
    return [(sid(y, c), sid(y + dy, c)) for y in range(NY) for c in range(2)]


def slanted(sign, dz):
    return [
        (gid(z, x) * 8 + sid(y, c), gid(z + dz, x + sign * y) * 8 + sid(y, c))
        for z in range(NZ)
        for x in range(NX)
        for y in range(NY)
        for c in range(2)
    ]


def row_table(per_pair):
    n = np.arange(16 * per_pair)
    pair, r = n // per_pair, n % per_pair + PAIR - per_pair
    ring, step, part = pair // 8, pair // 2 % 4, pair % 2
    zero = np.zeros_like(n)
    kz = np.array(KZ)[ring, part]
    return np.stack([ring, step, kz, r, zero, zero, zero, zero]).astype(np.int32)


def position():
    g = lax.axis_index("grp")
    s = lax.axis_index("seq")
    return g & 3, s >> 1, g >> 2, s & 1


def dot(a, b, ca, cb):
    return lax.dot_general(a, b, (((ca,), (cb,)), ((), ())), preferred_element_type=F32)


def places(tab):
    x, y, z, _ = position()
    step = tab[1:2, :]
    xs = (x + jnp.where(tab[0:1, :] == 0, step, y + step)) & 3
    return xs, (z + tab[2:3, :]) & 7, tab[3:4, :]


def fill_perm(tab, perm):
    xs, a, r = places(tab)
    first = (a * 4 + xs) * 36 + r
    second = (((a + 4) & 7) * 4 + xs) * 36 + r - 36
    natural = jnp.where(r < 36, first, jnp.where(r < 72, second, -1))
    for i in range(0, D, 128):
        ids = lax.broadcasted_iota(jnp.int32, (128, ROWS), 0) + i
        perm[i : i + 128, :] = jnp.where(ids == natural, 1.0, 0.0).astype(BF)


def pack_kernel(wq_ref, wp_ref, out_ref, buf):
    _, _, _, c = position()
    wq = wq_ref[...].astype(F32)
    pad = jnp.zeros((36, LANES - 3 * OWN), F32)

    def part(core):
        cols = [wq[:, b * INNER + core * OWN : b * INNER + core * OWN + OWN] for b in range(3)]
        return jnp.concatenate(cols + [pad], axis=1)

    buf[...] = jnp.zeros_like(buf)
    buf[0:36, :] = jnp.where(c == 0, part(0), part(1))
    wp = wp_ref[...].astype(F32)
    buf[40:58, :] = wp[:, 0:LANES]
    for u in range(3):
        buf[58:64, 256 * u : 256 * u + 256] = wp[6 * u : 6 * u + 6, LANES:D]
    out_ref[...] = buf[...].astype(BF)


def pack(w_qkv, w_proj):
    return pl.pallas_call(
        pack_kernel,
        out_shape=jax.ShapeDtypeStruct((MSG, LANES), BF),
        scratch_shapes=[pltpu.VMEM((MSG, LANES), F32)],
        name="pack_weights",
    )(w_qkv, w_proj)


def pair_kernel(mine_ref, far_ref, out_ref, buf):
    _, _, z, c = position()
    mine = mine_ref[...].astype(F32)
    far = far_ref[...].astype(F32)
    buf[0:36, :] = mine[0:36, :]
    buf[36:72, :] = far[0:36, :]
    buf[72:96, :] = jnp.where((z >> 2) == c, mine[40:64, :], far[40:64, :])
    out_ref[...] = buf[...].astype(BF)


def make_pair(mine, far):
    return pl.pallas_call(
        pair_kernel,
        out_shape=jax.ShapeDtypeStruct((PAIR, LANES), BF),
        scratch_shapes=[pltpu.VMEM((PAIR, LANES), F32)],
        name="pair_weights",
    )(mine, far)


def split_kernel(tok_ref, dy_ref, *outs):
    _, y, _, _ = position()
    for k in range(4):
        off = pl.multiple_of(((y + k) & 3) * 64, 64)
        outs[k][0:64, :] = tok_ref[pl.ds(off, 64), :]
        outs[k][64:128, :] = dy_ref[pl.ds(off, 64), :]


def split_tokens(x, dy):
    return pl.pallas_call(
        split_kernel,
        out_shape=[jax.ShapeDtypeStruct((128, D), BF)] * 4,
        name="split_tokens",
    )(x, dy)


def join_kernel(g0, g1, g2, g3, out_ref):
    _, y, _, _ = position()
    for k, g in enumerate((g0, g1, g2, g3)):
        out_ref[pl.ds(pl.multiple_of(((y + k) & 3) * 64, 64), 64), :] = g[...]


def join_tokens(parts):
    return pl.pallas_call(
        join_kernel,
        out_shape=jax.ShapeDtypeStruct((256, D), BF),
        name="join_tokens",
    )(*parts)


def normalize(xf):
    mean = jnp.mean(xf, axis=-1, keepdims=True)
    cent = xf - mean
    rstd = lax.rsqrt(jnp.mean(cent * cent, axis=-1, keepdims=True) + 1e-06)
    return cent * rstd, rstd


def gather_rows(parts, base):
    return jnp.concatenate(
        [p[base + 32 * s : base + 32 * s + 32, :].astype(F32) for s in range(2) for p in parts], axis=0
    )


def frames_of(index, y, c):
    return (((y - (index >> 5)) & 3) * 2) + (c ^ ((index >> 7) & 1))


def prepare_kernel(count_ref, tab_ref, mods_ref, *refs):
    td, (modp_ref, gated_ref, perm) = refs[0:8], refs[8:]
    _, y, _, c = position()
    fill_perm(tab_ref[...], perm)
    normed, _ = normalize(gather_rows(td, 0))
    modded = (normed * (1.0 + mods_ref[1:2, :]) + mods_ref[0:1, :]).astype(BF)
    modp_ref[...] = dot(modded, perm[...], 1, 0).astype(BF)
    index = lax.broadcasted_iota(jnp.int32, (TOK, 1), 0)
    live = jnp.where(frames_of(index, y, c) < count_ref[0], 1.0, 0.0)
    gated_ref[...] = (mods_ref[2:3, :] * live * gather_rows(td, 64)).astype(BF)


def specs(kinds):
    of = {"s": pltpu.SMEM, "v": pltpu.VMEM, "a": pl.ANY}
    return [pl.BlockSpec(memory_space=of[k]) for k in kinds]


def prepare(count, table, mods, td):
    return pl.pallas_call(
        prepare_kernel,
        in_specs=specs("s" + "v" * 10),
        out_specs=specs("vv"),
        out_shape=[jax.ShapeDtypeStruct((TOK, ROWS), BF), jax.ShapeDtypeStruct((TOK, D), BF)],
        scratch_shapes=[pltpu.VMEM((D, ROWS), BF)],
        compiler_params=pltpu.CompilerParams(vmem_limit_bytes=VMEM_LIMIT),
        cost_estimate=pl.CostEstimate(
            flops=2_000_000_000, bytes_accessed=6_000_000, transcendentals=512
        ),
        name="prepare",
    )(count, table, mods, *td)


def load_weights(w, wbuf, sem):
    loads = []
    for i in range(8):
        copy = pltpu.make_async_copy(w[i], wbuf.at[pl.ds(i * RING, RING), :], sem.at[i])
        copy.start()
        loads.append(copy)
    return loads


def main_kernel(count_ref, tab_ref, modp, gated, *refs):
    w = refs[0:8]
    rows_ref = refs[8]
    g_out = refs[9:17]
    wbuf, g, gf, gp, q_s, k_s, v_s, h_s, o_s, dq_s, dk_s, dv_s, in_sem, out_sem = refs[17:]
    _, y, _, c = position()
    loads = load_weights(w, wbuf, in_sem)

    xs, a, r = places(tab_ref[...])
    inner = jnp.where((r >= 72) & (r < 90), ((a & 3) * 4 + xs) * 18 + r - 72, -1)
    pick = jnp.where(
        lax.broadcasted_iota(jnp.int32, (WIDE, PROJ), 0) == inner, 1.0, 0.0
    ).astype(BF)
    main_lane = (r >= 72) & (r < 90)
    tail_lane = r >= 90

    for copy in loads:
        copy.wait()

    lane = lax.broadcasted_iota(jnp.int32, (1, WIDE), 1)
    own_lane = lane < OWN
    qkv = dot(modp[...], wbuf[...], 1, 0)
    q_s[...] = jnp.where(own_lane, qkv[:, 0:384], 0.0).astype(BF)
    k_s[...] = jnp.where(own_lane, pltpu.roll(qkv[:, 256:640], WIDE - 32, 1), 0.0).astype(BF)
    v_s[...] = jnp.where(own_lane, pltpu.roll(qkv[:, 512:896], WIDE - 64, 1), 0.0).astype(BF)

    wp = jnp.concatenate([wbuf[PAIR * p + 64 : PAIR * p + 96, :] for p in range(16)], axis=0)
    g_lo = gated[:, 0:LANES]
    g_hi = gated[:, LANES:D]
    ghp = jnp.where(main_lane, dot(g_lo, wp, 1, 1), 0.0)
    for u in range(3):
        tail = dot(g_hi, wp[:, 256 * u : 256 * u + 256], 1, 1)
        ghp += pltpu.roll(jnp.where(tail_lane, tail, 0.0), PROJ + 6 * u - 18, 1)
    h_s[...] = dot(ghp.astype(BF), pick, 1, 1).astype(BF)

    row = lax.broadcasted_iota(jnp.int32, (256, 1), 0)
    col = lax.broadcasted_iota(jnp.int32, (1, 256), 1)
    same = ((row & 31) == (col & 31)) & (frames_of(col, y, c) < count_ref[0])
    factor = HEAD ** (-0.5)
    for ref in (o_s, dq_s, dk_s, dv_s):
        ref[...] = jnp.zeros_like(ref)
    zero = jnp.zeros((), BF)
    for s in range(2):
        at = slice(256 * s, 256 * s + 256)
        for h in range(4):
            lo = h * HEAD
            start = lo // 128 * 128
            stop = -(-(lo + HEAD) // 128) * 128
            win = slice(start, stop)
            lanes = lax.broadcasted_iota(jnp.int32, (1, stop - start), 1) + start
            inside = (lanes >= lo) & (lanes < lo + HEAD)
            qm = jnp.where(inside, q_s[at, win], zero)
            km = jnp.where(inside, k_s[at, win], zero)
            vm = jnp.where(inside, v_s[at, win], zero)
            gm = jnp.where(inside, h_s[at, win], zero)
            scores = jnp.where(same, dot(qm, km, 1, 1) * factor, -1e30)
            top = jnp.max(scores, axis=-1, keepdims=True)
            expd = jnp.exp(scores - top)
            probs = expd / jnp.sum(expd, axis=-1, keepdims=True)
            probs_b = probs.astype(BF)
            o_s[at, win] += dot(probs_b, vm, 1, 0)
            dprobs = dot(gm, vm, 1, 1)
            dv_s[at, win] += dot(probs_b, gm, 0, 0)
            delta = jnp.sum(probs * dprobs, axis=-1, keepdims=True)
            ds = (probs * (dprobs - delta) * factor).astype(BF)
            dq_s[at, win] += dot(ds, km, 1, 0)
            dk_s[at, win] += dot(ds, qm, 0, 0)

    dkr = pltpu.roll(dk_s[...], 32, 1)
    dvr = pltpu.roll(dv_s[...], 64, 1)
    rows_ref[:, 0:256] = dq_s[:, 0:256].astype(BF)
    rows_ref[:, 256:384] = (dq_s[:, 256:384] + dkr[:, 0:128]).astype(BF)
    rows_ref[:, 384:512] = dkr[:, 128:256].astype(BF)
    rows_ref[:, 512:640] = (dkr[:, 256:384] + dvr[:, 0:128]).astype(BF)
    rows_ref[:, 640:896] = dvr[:, 128:384].astype(BF)

    hmf = dot(o_s[...].astype(BF), pick, 1, 0)
    gp[...] = dot(hmf.astype(BF), g_lo, 0, 0)
    for u in range(3):
        h_u = jnp.where(tail_lane, pltpu.roll(hmf, 18 - 6 * u, 1), 0.0).astype(BF)
        gp[:, 256 * u : 256 * u + 256] += dot(h_u, g_hi, 0, 0)
    rows = rows_ref[...]
    stores = []
    for j in range(4):
        gf[...] = dot(modp[:, 384 * j : 384 * j + 384], rows, 0, 0)
        for p in range(4):
            n = 4 * j + p
            gf[PAIR * p + 64 : PAIR * p + 96, :] += gp[32 * n : 32 * n + 32, :]
        g[384 * j : 384 * j + 384, :] = gf[...].astype(BF)
        for i in (2 * j, 2 * j + 1):
            copy = pltpu.make_async_copy(g.at[pl.ds(i * RING, RING), :], g_out[i], out_sem.at[i])
            copy.start()
            stores.append(copy)
    for copy in stores:
        copy.wait()


def compute(count, table, modp, gated, w):
    wide = pltpu.VMEM((TOK, WIDE), F32)
    wide_b = pltpu.VMEM((TOK, WIDE), BF)
    outs = pl.pallas_call(
        main_kernel,
        in_specs=specs("svvv" + "a" * 8),
        out_specs=specs("v" + "a" * 8),
        out_shape=[jax.ShapeDtypeStruct((TOK, LANES), BF)]
        + [jax.ShapeDtypeStruct((RING, LANES), BF)] * 8,
        scratch_shapes=[
            pltpu.VMEM((ROWS, LANES), BF),
            pltpu.VMEM((ROWS, LANES), BF),
            pltpu.VMEM((384, LANES), F32),
            pltpu.VMEM((PROJ, LANES), F32),
            wide_b,
            wide_b,
            wide_b,
            wide_b,
            wide,
            wide,
            wide,
            wide,
            pltpu.SemaphoreType.DMA((8,)),
            pltpu.SemaphoreType.DMA((8,)),
        ],
        compiler_params=pltpu.CompilerParams(vmem_limit_bytes=VMEM_LIMIT),
        cost_estimate=pl.CostEstimate(
            flops=7_000_000_000, bytes_accessed=9_000_000, transcendentals=600_000
        ),
        name="block",
    )(count, table, modp, gated, *w)
    return outs[0], outs[1:]


def back_kernel(tab_ref, rows, *refs):
    w = refs[0:8]
    own_ref, other_ref, wbuf, perm, sem = refs[8:]
    loads = load_weights(w, wbuf, sem)
    fill_perm(tab_ref[...], perm)
    for copy in loads:
        copy.wait()
    packed = dot(rows[...], wbuf[...], 1, 1).astype(BF)
    part = dot(packed, perm[...], 1, 1).astype(BF)
    for s in range(2):
        own_ref[128 * s : 128 * s + 128, :] = part[256 * s : 256 * s + 128, :]
        other_ref[128 * s : 128 * s + 128, :] = part[256 * s + 128 : 256 * s + 256, :]


def back(table, rows, w):
    return pl.pallas_call(
        back_kernel,
        in_specs=specs("vv" + "a" * 8),
        out_specs=specs("vv"),
        out_shape=[jax.ShapeDtypeStruct((256, D), BF)] * 2,
        scratch_shapes=[
            pltpu.VMEM((ROWS, LANES), BF),
            pltpu.VMEM((D, ROWS), BF),
            pltpu.SemaphoreType.DMA((8,)),
        ],
        compiler_params=pltpu.CompilerParams(vmem_limit_bytes=VMEM_LIMIT),
        cost_estimate=pl.CostEstimate(
            flops=3_400_000_000, bytes_accessed=6_000_000, transcendentals=0
        ),
        name="back",
    )(table, rows, *w)


def final_kernel(mods_ref, own_ref, other_ref, *refs):
    td, gt = refs[0:4], refs[4:]
    normed, rstd = normalize(gather_rows(td, 0))
    grad_modded = (own_ref[...].astype(F32) + other_ref[...].astype(F32)).astype(BF).astype(F32)
    dn = grad_modded * (1.0 + mods_ref[1:2, :])
    mean_dn = jnp.mean(dn, axis=-1, keepdims=True)
    mean_dnn = jnp.mean(dn * normed, axis=-1, keepdims=True)
    grad_x = (gather_rows(td, 64) + rstd * (dn - mean_dn - normed * mean_dnn)).astype(BF)
    for s in range(2):
        for k in range(4):
            gt[k][32 * s : 32 * s + 32, :] = grad_x[128 * s + 32 * k : 128 * s + 32 * k + 32, :]


def finish(mods, own, other, td):
    return pl.pallas_call(
        final_kernel,
        out_shape=[jax.ShapeDtypeStruct((64, D), BF)] * 4,
        compiler_params=pltpu.CompilerParams(vmem_limit_bytes=VMEM_LIMIT),
        name="finish",
    )(mods, own, other, *td)


def sum_kernel(*refs):
    parts, outs = refs[:4], refs[4:]
    total = parts[0][...].astype(F32)
    for part in parts[1:]:
        total = total + part[...].astype(F32)
    for k, out in enumerate(outs):
        out[...] = total[PAIR * k : PAIR * k + PAIR, :].astype(BF)


def sum_ring(parts):
    return pl.pallas_call(
        sum_kernel,
        out_shape=[jax.ShapeDtypeStruct((PAIR, LANES), BF)] * 2,
        name="sum_ring",
    )(*parts)


def fold_kernel(*refs):
    parts, (keep, send, buf) = refs[:4], refs[4:]
    total = parts[0][...].astype(F32)
    for part in parts[1:]:
        total = total + part[...].astype(F32)
    gap = jnp.zeros((4, LANES), F32)
    for out, lo in ((keep, 0), (send, 36)):
        buf[0:36, :] = total[lo : lo + 36, :]
        buf[36:40, :] = gap
        buf[40:64, :] = total[72:96, :]
        out[...] = buf[...].astype(BF)


def fold(parts):
    return pl.pallas_call(
        fold_kernel,
        out_shape=[jax.ShapeDtypeStruct((MSG, LANES), BF)] * 2,
        scratch_shapes=[pltpu.VMEM((MSG, LANES), F32)],
        name="fold",
    )(*parts)


def unpack_kernel(own_ref, other_ref, gq_ref, gp_ref):
    _, _, z, c = position()
    own, other = own_ref[...], other_ref[...]
    first = jnp.where(c == 0, own, other)[0:36, :]
    second = jnp.where(c == 0, other, own)[0:36, :]
    cols = []
    for b in range(3):
        cols += [first[:, b * OWN : b * OWN + OWN], second[:, b * OWN : b * OWN + OWN]]
    gq_ref[...] = jnp.concatenate(cols, axis=1)
    proj = jnp.where((z >> 2) == c, own, other)
    gp_ref[:, 0:LANES] = proj[40:58, :]
    for u in range(3):
        gp_ref[6 * u : 6 * u + 6, LANES:D] = proj[58:64, 256 * u : 256 * u + 256]


def unpack(own, other):
    return pl.pallas_call(
        unpack_kernel,
        out_shape=[jax.ShapeDtypeStruct((36, QKV), F32), jax.ShapeDtypeStruct((18, D), F32)],
        name="unpack_grads",
    )(own, other)


def add(*parts):
    total = parts[0].astype(F32)
    for part in parts[1:]:
        total = total + part.astype(F32)
    return total.astype(BF)


def local(tokens, grad_out, modulation, frame_counts, w_qkv, w_proj):
    both = ("grp", "seq")
    barrier = lax.optimization_barrier
    mods = modulation[0]
    table = jnp.asarray(row_table(PAIR))
    mine = pack(w_qkv, w_proj)
    far = lax.ppermute(mine, "grp", along_z(4))
    td = split_tokens(tokens[0, 0], grad_out[0, 0])
    td_in = [lax.ppermute(td[k], "seq", along_y(k)) for k in ORDER]
    far, own0, td_in[0], td_in[1] = barrier((far, td[0], td_in[0], td_in[1]))
    pair = make_pair(mine, far)
    x_b = lax.ppermute(pair, "grp", along_z(-1))
    y_a = lax.ppermute(pair, both, slanted(-1, 1))
    y_b = lax.ppermute(pair, both, slanted(-1, -2))
    x_b, y_a, y_b, *td_in = barrier([x_b, y_a, y_b] + td_in)
    tdr = dict(zip(ORDER, td_in))
    tdr[0] = own0
    xs = {0: jnp.concatenate([pair, x_b], axis=0)}
    ys = {0: jnp.concatenate([y_a, y_b], axis=0)}
    for k in ORDER:
        xs[k] = lax.ppermute(xs[0], "grp", along_x(-k))
        ys[k] = lax.ppermute(ys[0], "seq", along_y(-k))
    own_td = [tdr[k] for k in range(4)]
    other_td = [lax.ppermute(t, "seq", CORE_SWAP) for t in own_td]
    modp, gated = prepare(frame_counts, table, mods, own_td + other_td)
    *w, modp, gated = barrier([xs[k] for k in range(4)] + [ys[k] for k in range(4)] + [modp, gated])

    rows, grads = compute(frame_counts, jnp.asarray(row_table(32)), modp, gated, w)

    x_in = [lax.ppermute(grads[k], "grp", along_x(k)) for k in ORDER]
    y_in = [lax.ppermute(grads[4 + k], "seq", along_y(k)) for k in ORDER]
    own_part, other_part = back(table, rows, w)
    *ring_in, own_part, other_part = barrier(x_in + y_in + [own_part, other_part])
    other_in = lax.ppermute(other_part, "seq", CORE_SWAP)
    x_next = add(grads[0][PAIR:], *[t[PAIR:] for t in ring_in[:3]])
    y_a = add(grads[4][:PAIR], *[t[:PAIR] for t in ring_in[3:]])
    y_b = add(grads[4][PAIR:], *[t[PAIR:] for t in ring_in[3:]])
    x_near = add(grads[0][:PAIR], *[t[:PAIR] for t in ring_in[:3]])
    z_in = [
        lax.ppermute(x_next, "grp", along_z(1)),
        lax.ppermute(y_a, both, slanted(1, -1)),
        lax.ppermute(y_b, both, slanted(1, 2)),
    ]
    gt = finish(mods, own_part, other_in, own_td)
    *z_in, g0, g1, g2, g3 = barrier(z_in + list(gt))
    keep, send = fold([x_near, *z_in])
    send, g1, g2, g3 = barrier((send, g1, g2, g3))
    far = lax.ppermute(send, "grp", along_z(4))
    g_in = [lax.ppermute(g, "seq", along_y(-k)) for k, g in ((1, g1), (2, g2), (3, g3))]
    far, *g_in = barrier([far] + g_in)
    block = add(keep, far)
    r_in = [lax.ppermute(block, "seq", along_y(k)) for k in ORDER]
    grad_x = join_tokens([g0] + g_in)
    r1, r3, r2, grad_x = barrier(r_in + [grad_x])
    total = (block.astype(F32) + r2.astype(F32)) + (r1.astype(F32) + r3.astype(F32))
    grad_qkv, grad_proj = unpack(total, lax.ppermute(total, "seq", CORE_SWAP))
    return (grad_x[None, None], grad_qkv, grad_proj)


def solution(mesh):
    in_specs = (
        P("grp", "seq", None, None),
        P("grp", "seq", None, None),
        P("grp", None, None),
        P("grp"),
        P("grp", None),
        P("grp", None),
    )
    out_specs = (P("grp", "seq", None, None), P("grp", None), P("grp", None))
    return jax.shard_map(local, mesh=mesh, in_specs=in_specs, out_specs=out_specs, check_vma=False)
```

```python
import jax
import jax.numpy as jnp
import numpy as np
from jax import lax
from jax.experimental import pallas as pl
from jax.experimental.pallas import tpu as pltpu
from jax.sharding import PartitionSpec as P

BF = jnp.bfloat16
F32 = jnp.float32
HEAD = 72
D = 1152
INNER = 576
QKV = 1728
OWN = 288
LANES = 896
NX, NY, NZ = 4, 4, 8
XMSG = 64
YMSG = 40
XR = 4 * XMSG
YR = 4 * YMSG
YBASE = 4 * XR
ROWS = YBASE + 4 * YR
PROJ = 512
ORDER = (2, 1, 3)
TOK = 512
WIDE = 384
VMEM_LIMIT = 40 * 1024 * 1024


def gid(z, x):
    return (z % NZ) * NX + x % NX


def sid(y, c):
    return (y % NY) * 2 + c % 2


CORE_SWAP = [(s, s ^ 1) for s in range(8)]


def along_z(dz):
    return [(gid(z, x), gid(z + dz, x)) for z in range(NZ) for x in range(NX)]


def along_x(dx):
    return [(gid(z, x), gid(z, x + dx)) for z in range(NZ) for x in range(NX)]


def along_y(dy):
    return [(sid(y, c), sid(y + dy, c)) for y in range(NY) for c in range(2)]


def flat(z, x, y, c):
    return gid(z, x) * 8 + sid(y, c)


def x_homes(m):
    pairs = []
    for z in range(NZ):
        c = z % 2
        for x in range(NX):
            for y in range(NY):
                pairs.append((flat(z, x, y, c), flat(z - 2 * m, x, y, c)))
                pairs.append((flat(z, x, y, 1 - c), flat(z - 2 * m - 1, x, y, c)))
    return pairs


def y_homes():
    pairs = []
    for z in range(NZ):
        c = 1 - z % 2
        for x in range(NX):
            for y in range(NY):
                pairs.append((flat(z, x, y, c), flat(z - 2 * y, x, y, c)))
                pairs.append((flat(z, x, y, 1 - c), flat(z - 2 * y - 1, x, y, c)))
    return pairs


def back_home(pairs):
    return [(user, home) for home, user in pairs]


def row_table():
    n = np.arange(YBASE)
    m = np.arange(4 * YR)
    zero, one = np.zeros_like(n), np.ones_like(m)
    xt = np.stack([zero, n // XR, n // XMSG % 4, n % XMSG] + [zero] * 4)
    yt = np.stack([one, m // YR, m // YMSG % 4, m % YMSG] + [0 * one] * 4)
    return np.concatenate([xt, yt], axis=1).astype(np.int32)


def proj_table():
    t = row_table()[:, :YBASE]
    return t[:, t[3] >= 32]


def position():
    g = lax.axis_index("grp")
    s = lax.axis_index("seq")
    return g & 3, s >> 1, g >> 2, s & 1


def dot(a, b, ca, cb):
    return lax.dot_general(a, b, (((ca,), (cb,)), ((), ())), preferred_element_type=F32)


def places(tab):
    x, y, z, c = position()
    in_x, step, part = tab[0:1, :] == 0, tab[1:2, :], tab[2:3, :]
    odd = (z ^ c) & 1
    xs = (x + jnp.where(in_x, step, part)) & 3
    zs = (z + jnp.where(in_x, 2 * part + odd, 2 * ((y + step) & 3) + 1 - odd)) & 7
    return xs, zs, tab[3:4, :]


def fill_perm(tab, perm):
    xs, zs, r = places(tab)
    natural = jnp.where(r < 36, (zs * 4 + xs) * 36 + r, -1)
    for i in range(0, D, 128):
        ids = lax.broadcasted_iota(jnp.int32, (128, ROWS), 0) + i
        perm[i : i + 128, :] = jnp.where(ids == natural, 1.0, 0.0).astype(BF)


def head_columns(parity):
    return [b * INNER + (2 * i + parity) * HEAD for b in range(3) for i in range(4)]


def pack_kernel(wq_ref, wp_ref, xm_ref, ym_ref, buf):
    _, _, z, _ = position()
    wq = wq_ref[...].astype(F32)
    pad = jnp.zeros((36, LANES - 3 * OWN), F32)
    even, odd = [
        jnp.concatenate([wq[:, lo : lo + HEAD] for lo in head_columns(p)] + [pad], axis=1)
        for p in range(2)
    ]
    is_even = (z & 1) == 0
    buf[...] = jnp.zeros_like(buf)
    buf[0:36, :] = jnp.where(is_even, odd, even)
    ym_ref[...] = buf[0:YMSG, :].astype(BF)
    buf[0:36, :] = jnp.where(is_even, even, odd)
    wp = wp_ref[...].astype(F32)
    buf[40:58, :] = wp[:, 0:LANES]
    for u in range(3):
        buf[58:64, 256 * u : 256 * u + 256] = wp[6 * u : 6 * u + 6, LANES:D]
    xm_ref[...] = buf[...].astype(BF)


def pack(w_qkv, w_proj):
    return pl.pallas_call(
        pack_kernel,
        out_shape=[
            jax.ShapeDtypeStruct((XMSG, LANES), BF),
            jax.ShapeDtypeStruct((YMSG, LANES), BF),
        ],
        scratch_shapes=[pltpu.VMEM((XMSG, LANES), F32)],
        name="pack_weights",
    )(w_qkv, w_proj)


def split_kernel(tok_ref, dy_ref, *outs):
    _, y, _, _ = position()
    for k in range(4):
        off = pl.multiple_of(((y + k) & 3) * 64, 64)
        outs[k][0:64, :] = tok_ref[pl.ds(off, 64), :]
        outs[k][64:128, :] = dy_ref[pl.ds(off, 64), :]


def split_tokens(x, dy):
    return pl.pallas_call(
        split_kernel,
        out_shape=[jax.ShapeDtypeStruct((128, D), BF)] * 4,
        name="split_tokens",
    )(x, dy)


def join_kernel(g0, g1, g2, g3, out_ref):
    _, y, _, _ = position()
    for k, g in enumerate((g0, g1, g2, g3)):
        out_ref[pl.ds(pl.multiple_of(((y + k) & 3) * 64, 64), 64), :] = g[...]


def join_tokens(parts):
    return pl.pallas_call(
        join_kernel,
        out_shape=jax.ShapeDtypeStruct((256, D), BF),
        name="join_tokens",
    )(*parts)


def normalize(xf):
    mean = jnp.mean(xf, axis=-1, keepdims=True)
    cent = xf - mean
    rstd = lax.rsqrt(jnp.mean(cent * cent, axis=-1, keepdims=True) + 1e-06)
    return cent * rstd, rstd


def gather_rows(parts, base):
    return jnp.concatenate(
        [p[base + 32 * s : base + 32 * s + 32, :].astype(F32) for s in range(2) for p in parts], axis=0
    )


def frames_of(index, y, c):
    return (((y - (index >> 5)) & 3) * 2) + (c ^ ((index >> 7) & 1))


def prepare_kernel(count_ref, tab_ref, mods_ref, *refs):
    td, (modp_ref, gated_ref, perm) = refs[0:8], refs[8:]
    _, y, _, c = position()
    fill_perm(tab_ref[...], perm)
    normed, _ = normalize(gather_rows(td, 0))
    modded = (normed * (1.0 + mods_ref[1:2, :]) + mods_ref[0:1, :]).astype(BF)
    modp_ref[...] = dot(modded, perm[...], 1, 0).astype(BF)
    index = lax.broadcasted_iota(jnp.int32, (TOK, 1), 0)
    live = jnp.where(frames_of(index, y, c) < count_ref[0], 1.0, 0.0)
    gated_ref[...] = (mods_ref[2:3, :] * live * gather_rows(td, 64)).astype(BF)


def specs(kinds):
    of = {"s": pltpu.SMEM, "v": pltpu.VMEM, "a": pl.ANY}
    return [pl.BlockSpec(memory_space=of[k]) for k in kinds]


def prepare(count, table, mods, td):
    return pl.pallas_call(
        prepare_kernel,
        in_specs=specs("s" + "v" * 10),
        out_specs=specs("vv"),
        out_shape=[jax.ShapeDtypeStruct((TOK, ROWS), BF), jax.ShapeDtypeStruct((TOK, D), BF)],
        scratch_shapes=[pltpu.VMEM((D, ROWS), BF)],
        compiler_params=pltpu.CompilerParams(vmem_limit_bytes=VMEM_LIMIT),
        cost_estimate=pl.CostEstimate(
            flops=2_000_000_000, bytes_accessed=6_000_000, transcendentals=512
        ),
        name="prepare",
    )(count, table, mods, *td)


def span(i):
    return (i * XR, XR) if i < 4 else (YBASE + (i - 4) * YR, YR)


def load_weights(w, wbuf, sem):
    loads = []
    for i in range(8):
        copy = pltpu.make_async_copy(w[i], wbuf.at[pl.ds(*span(i)), :], sem.at[i])
        copy.start()
        loads.append(copy)
    return loads


def main_kernel(count_ref, tab_ref, modp, gated, *refs):
    w = refs[0:8]
    rows_ref = refs[8]
    g_out = refs[9:17]
    wbuf, g, gf, gp, q_s, k_s, v_s, h_s, o_s, dq_s, dk_s, dv_s, in_sem, out_sem = refs[17:]
    _, y, _, c = position()
    loads = load_weights(w, wbuf, in_sem)

    xs, zs, r = places(tab_ref[...])
    main_lane = (r >= 40) & (r < 58)
    tail_lane = r >= 58
    inner = jnp.where(main_lane, (zs >> 1) * HEAD + xs * 18 + r - 40, -1)
    pick = jnp.where(
        lax.broadcasted_iota(jnp.int32, (WIDE, PROJ), 0) == inner, 1.0, 0.0
    ).astype(BF)

    for copy in loads:
        copy.wait()

    lane = lax.broadcasted_iota(jnp.int32, (1, WIDE), 1)
    own_lane = lane < OWN
    qkv = dot(modp[...], wbuf[...], 1, 0)
    q_s[...] = jnp.where(own_lane, qkv[:, 0:384], 0.0).astype(BF)
    k_s[...] = jnp.where(own_lane, pltpu.roll(qkv[:, 256:640], WIDE - 32, 1), 0.0).astype(BF)
    v_s[...] = jnp.where(own_lane, pltpu.roll(qkv[:, 512:896], WIDE - 64, 1), 0.0).astype(BF)

    wp = jnp.concatenate([wbuf[XMSG * p + 32 : XMSG * p + 64, :] for p in range(16)], axis=0)
    g_lo = gated[:, 0:LANES]
    g_hi = gated[:, LANES:D]
    ghp = jnp.where(main_lane, dot(g_lo, wp, 1, 1), 0.0)
    for u in range(3):
        tail = dot(g_hi, wp[:, 256 * u : 256 * u + 256], 1, 1)
        ghp += pltpu.roll(jnp.where(tail_lane, tail, 0.0), PROJ + 6 * u - 18, 1)
    h_s[...] = dot(ghp.astype(BF), pick, 1, 1).astype(BF)

    row = lax.broadcasted_iota(jnp.int32, (256, 1), 0)
    col = lax.broadcasted_iota(jnp.int32, (1, 256), 1)
    same = ((row & 31) == (col & 31)) & (frames_of(col, y, c) < count_ref[0])
    factor = HEAD ** (-0.5)
    for ref in (o_s, dq_s, dk_s, dv_s):
        ref[...] = jnp.zeros_like(ref)
    zero = jnp.zeros((), BF)
    for s in range(2):
        at = slice(256 * s, 256 * s + 256)
        for h in range(4):
            lo = h * HEAD
            start = lo // 128 * 128
            stop = -(-(lo + HEAD) // 128) * 128
            win = slice(start, stop)
            lanes = lax.broadcasted_iota(jnp.int32, (1, stop - start), 1) + start
            inside = (lanes >= lo) & (lanes < lo + HEAD)
            qm = jnp.where(inside, q_s[at, win], zero)
            km = jnp.where(inside, k_s[at, win], zero)
            vm = jnp.where(inside, v_s[at, win], zero)
            gm = jnp.where(inside, h_s[at, win], zero)
            scores = jnp.where(same, dot(qm, km, 1, 1) * factor, -1e30)
            top = jnp.max(scores, axis=-1, keepdims=True)
            expd = jnp.exp(scores - top)
            probs = expd / jnp.sum(expd, axis=-1, keepdims=True)
            probs_b = probs.astype(BF)
            o_s[at, win] += dot(probs_b, vm, 1, 0)
            dprobs = dot(gm, vm, 1, 1)
            dv_s[at, win] += dot(probs_b, gm, 0, 0)
            delta = jnp.sum(probs * dprobs, axis=-1, keepdims=True)
            ds = (probs * (dprobs - delta) * factor).astype(BF)
            dq_s[at, win] += dot(ds, km, 1, 0)
            dk_s[at, win] += dot(ds, qm, 0, 0)

    dkr = pltpu.roll(dk_s[...], 32, 1)
    dvr = pltpu.roll(dv_s[...], 64, 1)
    rows_ref[:, 0:256] = dq_s[:, 0:256].astype(BF)
    rows_ref[:, 256:384] = (dq_s[:, 256:384] + dkr[:, 0:128]).astype(BF)
    rows_ref[:, 384:512] = dkr[:, 128:256].astype(BF)
    rows_ref[:, 512:640] = (dkr[:, 256:384] + dvr[:, 0:128]).astype(BF)
    rows_ref[:, 640:896] = dvr[:, 128:384].astype(BF)

    hmf = dot(o_s[...].astype(BF), pick, 1, 0)
    gp[...] = dot(hmf.astype(BF), g_lo, 0, 0)
    for u in range(3):
        h_u = jnp.where(tail_lane, pltpu.roll(hmf, 18 - 6 * u, 1), 0.0).astype(BF)
        gp[:, 256 * u : 256 * u + 256] += dot(h_u, g_hi, 0, 0)
    rows = rows_ref[...]
    stores = []
    for lo, size in ((0, 256), (256, 256), (512, 256), (768, 256), (1024, 256), (1280, 384)):
        gf[0:size, :] = dot(modp[:, lo : lo + size], rows, 0, 0)
        for n in range(lo // XMSG, (lo + size) // XMSG):
            if lo < YBASE:
                at = XMSG * n - lo + 32
                gf[at : at + 32, :] += gp[32 * n : 32 * n + 32, :]
        g[lo : lo + size, :] = gf[0:size, :].astype(BF)
        for i in range(8):
            start, length = span(i)
            if lo < start + length <= lo + size:
                copy = pltpu.make_async_copy(g.at[pl.ds(start, length), :], g_out[i], out_sem.at[i])
                copy.start()
                stores.append(copy)
    for copy in stores:
        copy.wait()


def compute(count, table, modp, gated, w):
    wide = pltpu.VMEM((TOK, WIDE), F32)
    wide_b = pltpu.VMEM((TOK, WIDE), BF)
    outs = pl.pallas_call(
        main_kernel,
        in_specs=specs("svvv" + "a" * 8),
        out_specs=specs("v" + "a" * 8),
        out_shape=[jax.ShapeDtypeStruct((TOK, LANES), BF)]
        + [jax.ShapeDtypeStruct((span(i)[1], LANES), BF) for i in range(8)],
        scratch_shapes=[
            pltpu.VMEM((ROWS, LANES), BF),
            pltpu.VMEM((ROWS, LANES), BF),
            pltpu.VMEM((384, LANES), F32),
            pltpu.VMEM((PROJ, LANES), F32),
            wide_b,
            wide_b,
            wide_b,
            wide_b,
            wide,
            wide,
            wide,
            wide,
            pltpu.SemaphoreType.DMA((8,)),
            pltpu.SemaphoreType.DMA((8,)),
        ],
        compiler_params=pltpu.CompilerParams(vmem_limit_bytes=VMEM_LIMIT),
        cost_estimate=pl.CostEstimate(
            flops=7_000_000_000, bytes_accessed=9_000_000, transcendentals=600_000
        ),
        name="block",
    )(count, table, modp, gated, *w)
    return outs[0], outs[1:]


def back_kernel(tab_ref, rows, *refs):
    w = refs[0:8]
    own_ref, other_ref, wbuf, perm, sem = refs[8:]
    loads = load_weights(w, wbuf, sem)
    fill_perm(tab_ref[...], perm)
    for copy in loads:
        copy.wait()
    packed = dot(rows[...], wbuf[...], 1, 1).astype(BF)
    part = dot(packed, perm[...], 1, 1).astype(BF)
    for s in range(2):
        own_ref[128 * s : 128 * s + 128, :] = part[256 * s : 256 * s + 128, :]
        other_ref[128 * s : 128 * s + 128, :] = part[256 * s + 128 : 256 * s + 256, :]


def back(table, rows, w):
    return pl.pallas_call(
        back_kernel,
        in_specs=specs("vv" + "a" * 8),
        out_specs=specs("vv"),
        out_shape=[jax.ShapeDtypeStruct((256, D), BF)] * 2,
        scratch_shapes=[
            pltpu.VMEM((ROWS, LANES), BF),
            pltpu.VMEM((D, ROWS), BF),
            pltpu.SemaphoreType.DMA((8,)),
        ],
        compiler_params=pltpu.CompilerParams(vmem_limit_bytes=VMEM_LIMIT),
        cost_estimate=pl.CostEstimate(
            flops=3_400_000_000, bytes_accessed=6_000_000, transcendentals=0
        ),
        name="back",
    )(table, rows, *w)


def final_kernel(mods_ref, own_ref, other_ref, *refs):
    td, gt = refs[0:4], refs[4:]
    normed, rstd = normalize(gather_rows(td, 0))
    grad_modded = (own_ref[...].astype(F32) + other_ref[...].astype(F32)).astype(BF).astype(F32)
    dn = grad_modded * (1.0 + mods_ref[1:2, :])
    mean_dn = jnp.mean(dn, axis=-1, keepdims=True)
    mean_dnn = jnp.mean(dn * normed, axis=-1, keepdims=True)
    grad_x = (gather_rows(td, 64) + rstd * (dn - mean_dn - normed * mean_dnn)).astype(BF)
    for s in range(2):
        for k in range(4):
            gt[k][32 * s : 32 * s + 32, :] = grad_x[128 * s + 32 * k : 128 * s + 32 * k + 32, :]


def finish(mods, own, other, td):
    return pl.pallas_call(
        final_kernel,
        out_shape=[jax.ShapeDtypeStruct((64, D), BF)] * 4,
        compiler_params=pltpu.CompilerParams(vmem_limit_bytes=VMEM_LIMIT),
        name="finish",
    )(mods, own, other, *td)


def unpack_kernel(own_ref, other_ref, gq_ref, gp_ref):
    _, _, z, _ = position()
    total = own_ref[...] + other_ref[...]
    mine, rest = total[0:36, :], total[XMSG : XMSG + 36, :]
    is_even = (z & 1) == 0
    even, odd = jnp.where(is_even, mine, rest), jnp.where(is_even, rest, mine)
    cols = []
    for n in range(12):
        cols += [even[:, n * HEAD : n * HEAD + HEAD], odd[:, n * HEAD : n * HEAD + HEAD]]
    gq_ref[...] = jnp.concatenate(cols, axis=1)
    gp_ref[:, 0:LANES] = total[40:58, :]
    for u in range(3):
        gp_ref[6 * u : 6 * u + 6, LANES:D] = total[58:64, 256 * u : 256 * u + 256]


def unpack(own, other):
    return pl.pallas_call(
        unpack_kernel,
        out_shape=[jax.ShapeDtypeStruct((36, QKV), F32), jax.ShapeDtypeStruct((18, D), F32)],
        name="unpack_grads",
    )(own, other)


def add(*parts):
    total = parts[0].astype(F32)
    for part in parts[1:]:
        total = total + part.astype(F32)
    return total.astype(BF)


def local(tokens, grad_out, modulation, frame_counts, w_qkv, w_proj):
    both = ("grp", "seq")
    barrier = lax.optimization_barrier
    mods = modulation[0]
    table = jnp.asarray(row_table())
    x_msg, y_msg = pack(w_qkv, w_proj)
    plane = lax.ppermute(y_msg, both, y_homes())
    x_parts = [lax.ppermute(x_msg, both, x_homes(m)) for m in range(4)]
    td = split_tokens(tokens[0, 0], grad_out[0, 0])
    td_in = [lax.ppermute(td[k], "seq", along_y(k)) for k in ORDER]
    plane, own0 = barrier((plane, td[0]))
    small = dict(zip(ORDER, barrier([lax.ppermute(plane, "grp", along_x(-k)) for k in ORDER])))
    xs = {0: jnp.concatenate(barrier(x_parts), axis=0)}
    ys = {0: jnp.concatenate([plane, small[1], small[2], small[3]], axis=0)}
    for k in ORDER:
        xs[k] = lax.ppermute(xs[0], "grp", along_x(-k))
        ys[k] = lax.ppermute(ys[0], "seq", along_y(-k))
    tdr = dict(zip(ORDER, td_in))
    tdr[0] = own0
    own_td = [tdr[k] for k in range(4)]
    other_td = [lax.ppermute(t, "seq", CORE_SWAP) for t in own_td]
    modp, gated = prepare(frame_counts, table, mods, own_td + other_td)
    *w, modp, gated = barrier([xs[k] for k in range(4)] + [ys[k] for k in range(4)] + [modp, gated])

    rows, grads = compute(frame_counts, jnp.asarray(proj_table()), modp, gated, w)

    ring_in = []
    for k in ORDER:
        ring_in.append(lax.ppermute(grads[k], "grp", along_x(k)))
        ring_in.append(lax.ppermute(grads[4 + k], "seq", along_y(k)))
    own_part, other_part = back(table, rows, w)
    *ring_in, own_part, other_part = barrier(ring_in + [own_part, other_part])
    other_in = lax.ppermute(other_part, "seq", CORE_SWAP)
    y_all, x_all = [grads[4], *ring_in[1::2]], [grads[0], *ring_in[0::2]]
    y_sum = [add(*[t[YMSG * m : YMSG * m + YMSG] for t in y_all]) for m in range(4)]
    x_sum = [add(*[t[XMSG * m : XMSG * m + XMSG] for t in x_all]) for m in range(4)]
    small = [lax.ppermute(y_sum[k], "grp", along_x(k)) for k in ORDER]
    z_in = [lax.ppermute(x_sum[m], both, back_home(x_homes(m))) for m in range(4)]
    gt = finish(mods, own_part, other_in, own_td)
    *small, g0, g1, g2, g3 = barrier(small + list(gt))
    plane = lax.ppermute(add(y_sum[0], *small), both, back_home(y_homes()))
    *z_in, plane = barrier(z_in + [plane])
    block = jnp.concatenate([add(*z_in), plane], axis=0)
    r_in = [lax.ppermute(block, "seq", along_y(k)) for k in ORDER]
    g_in = [lax.ppermute(g, "seq", along_y(-k)) for k, g in ((1, g1), (2, g2), (3, g3))]
    r2, r1, r3, *g_in = barrier(r_in + g_in)
    total = (block.astype(F32) + r2.astype(F32)) + (r1.astype(F32) + r3.astype(F32))
    other_total = lax.ppermute(total, "seq", CORE_SWAP)
    grad_x, other_total = barrier((join_tokens([g0] + g_in), other_total))
    grad_qkv, grad_proj = unpack(total, other_total)
    return (grad_x[None, None], grad_qkv, grad_proj)


def solution(mesh):
    in_specs = (
        P("grp", "seq", None, None),
        P("grp", "seq", None, None),
        P("grp", None, None),
        P("grp"),
        P("grp", None),
        P("grp", None),
    )
    out_specs = (P("grp", "seq", None, None), P("grp", None), P("grp", None))
    return jax.shard_map(local, mesh=mesh, in_specs=in_specs, out_specs=out_specs, check_vma=False)
```

```python
import jax
import jax.numpy as jnp
import numpy as np
from jax import lax
from jax.experimental import pallas as pl
from jax.experimental.pallas import tpu as pltpu
from jax.sharding import PartitionSpec as P

BF = jnp.bfloat16
F32 = jnp.float32
HEAD = 72
D = 1152
INNER = 576
QKV = 1728
OWN = 288
LANES = 896
NX, NY, NZ = 4, 4, 8
MSG = 64
PAIR = 96
RING = 2 * PAIR
ROWS = 8 * RING
PROJ = 512
KZ = ((0, 1), (7, 2))
ORDER = (1, 2, 3)
TOK = 512
WIDE = 384
VMEM_LIMIT = 40 * 1024 * 1024


def gid(z, x):
    return (z % NZ) * NX + x % NX


def sid(y, c):
    return (y % NY) * 2 + c % 2


CORE_SWAP = [(s, s ^ 1) for s in range(8)]


def along_z(dz):
    return [(gid(z, x), gid(z + dz, x)) for z in range(NZ) for x in range(NX)]


def along_x(dx):
    return [(gid(z, x), gid(z, x + dx)) for z in range(NZ) for x in range(NX)]


def along_y(dy):
    return [(sid(y, c), sid(y + dy, c)) for y in range(NY) for c in range(2)]


def slanted(sign, dz):
    return [
        (gid(z, x) * 8 + sid(y, c), gid(z + dz, x + sign * y) * 8 + sid(y, c))
        for z in range(NZ)
        for x in range(NX)
        for y in range(NY)
        for c in range(2)
    ]


def row_table(per_pair):
    n = np.arange(16 * per_pair)
    pair, r = n // per_pair, n % per_pair + PAIR - per_pair
    ring, step, part = pair // 8, pair // 2 % 4, pair % 2
    zero = np.zeros_like(n)
    kz = np.array(KZ)[ring, part]
    return np.stack([ring, step, kz, r, zero, zero, zero, zero]).astype(np.int32)


def position():
    g = lax.axis_index("grp")
    s = lax.axis_index("seq")
    return g & 3, s >> 1, g >> 2, s & 1


def dot(a, b, ca, cb):
    return lax.dot_general(a, b, (((ca,), (cb,)), ((), ())), preferred_element_type=F32)


def places(tab):
    x, y, z, _ = position()
    step = tab[1:2, :]
    xs = (x + jnp.where(tab[0:1, :] == 0, step, y + step)) & 3
    return xs, (z + tab[2:3, :]) & 7, tab[3:4, :]


def fill_perm(tab, perm):
    xs, a, r = places(tab)
    first = (a * 4 + xs) * 36 + r
    second = (((a + 4) & 7) * 4 + xs) * 36 + r - 36
    natural = jnp.where(r < 36, first, jnp.where(r < 72, second, -1))
    for i in range(0, D, 128):
        ids = lax.broadcasted_iota(jnp.int32, (128, ROWS), 0) + i
        perm[i : i + 128, :] = jnp.where(ids == natural, 1.0, 0.0).astype(BF)


def pack_kernel(wq_ref, wp_ref, out_ref, buf):
    _, _, _, c = position()
    wq = wq_ref[...].astype(F32)
    pad = jnp.zeros((36, LANES - 3 * OWN), F32)

    def part(core):
        cols = [wq[:, b * INNER + core * OWN : b * INNER + core * OWN + OWN] for b in range(3)]
        return jnp.concatenate(cols + [pad], axis=1)

    buf[...] = jnp.zeros_like(buf)
    buf[0:36, :] = jnp.where(c == 0, part(0), part(1))
    wp = wp_ref[...].astype(F32)
    buf[40:58, :] = wp[:, 0:LANES]
    for u in range(3):
        buf[58:64, 256 * u : 256 * u + 256] = wp[6 * u : 6 * u + 6, LANES:D]
    out_ref[...] = buf[...].astype(BF)


def pack(w_qkv, w_proj):
    return pl.pallas_call(
        pack_kernel,
        out_shape=jax.ShapeDtypeStruct((MSG, LANES), BF),
        scratch_shapes=[pltpu.VMEM((MSG, LANES), F32)],
        name="pack_weights",
    )(w_qkv, w_proj)


def pair_kernel(mine_ref, far_ref, out_ref, buf):
    _, _, z, c = position()
    mine = mine_ref[...].astype(F32)
    far = far_ref[...].astype(F32)
    buf[0:36, :] = mine[0:36, :]
    buf[36:72, :] = far[0:36, :]
    buf[72:96, :] = jnp.where((z >> 2) == c, mine[40:64, :], far[40:64, :])
    out_ref[...] = buf[...].astype(BF)


def make_pair(mine, far):
    return pl.pallas_call(
        pair_kernel,
        out_shape=jax.ShapeDtypeStruct((PAIR, LANES), BF),
        scratch_shapes=[pltpu.VMEM((PAIR, LANES), F32)],
        name="pair_weights",
    )(mine, far)


def split_kernel(tok_ref, dy_ref, *outs):
    _, y, _, _ = position()
    for k in range(4):
        off = pl.multiple_of(((y + k) & 3) * 64, 64)
        outs[k][0:64, :] = tok_ref[pl.ds(off, 64), :]
        outs[k][64:128, :] = dy_ref[pl.ds(off, 64), :]


def split_tokens(x, dy):
    return pl.pallas_call(
        split_kernel,
        out_shape=[jax.ShapeDtypeStruct((128, D), BF)] * 4,
        name="split_tokens",
    )(x, dy)


def join_kernel(g0, g1, g2, g3, out_ref):
    _, y, _, _ = position()
    for k, g in enumerate((g0, g1, g2, g3)):
        out_ref[pl.ds(pl.multiple_of(((y + k) & 3) * 64, 64), 64), :] = g[...]


def join_tokens(parts):
    return pl.pallas_call(
        join_kernel,
        out_shape=jax.ShapeDtypeStruct((256, D), BF),
        name="join_tokens",
    )(*parts)


def normalize(xf):
    mean = jnp.mean(xf, axis=-1, keepdims=True)
    cent = xf - mean
    rstd = lax.rsqrt(jnp.mean(cent * cent, axis=-1, keepdims=True) + 1e-06)
    return cent * rstd, rstd


def gather_rows(parts, base):
    return jnp.concatenate(
        [p[base + 32 * s : base + 32 * s + 32, :].astype(F32) for s in range(2) for p in parts], axis=0
    )


def frames_of(index, y, c):
    return (((y - (index >> 5)) & 3) * 2) + (c ^ ((index >> 7) & 1))


def prepare_kernel(count_ref, tab_ref, mods_ref, *refs):
    td, (modp_ref, gated_ref, perm) = refs[0:8], refs[8:]
    _, y, _, c = position()
    fill_perm(tab_ref[...], perm)
    normed, _ = normalize(gather_rows(td, 0))
    modded = (normed * (1.0 + mods_ref[1:2, :]) + mods_ref[0:1, :]).astype(BF)
    modp_ref[...] = dot(modded, perm[...], 1, 0).astype(BF)
    index = lax.broadcasted_iota(jnp.int32, (TOK, 1), 0)
    live = jnp.where(frames_of(index, y, c) < count_ref[0], 1.0, 0.0)
    gated_ref[...] = (mods_ref[2:3, :] * live * gather_rows(td, 64)).astype(BF)


def specs(kinds):
    of = {"s": pltpu.SMEM, "v": pltpu.VMEM, "a": pl.ANY}
    return [pl.BlockSpec(memory_space=of[k]) for k in kinds]


def prepare(count, table, mods, td):
    return pl.pallas_call(
        prepare_kernel,
        in_specs=specs("s" + "v" * 10),
        out_specs=specs("vv"),
        out_shape=[jax.ShapeDtypeStruct((TOK, ROWS), BF), jax.ShapeDtypeStruct((TOK, D), BF)],
        scratch_shapes=[pltpu.VMEM((D, ROWS), BF)],
        compiler_params=pltpu.CompilerParams(vmem_limit_bytes=VMEM_LIMIT),
        cost_estimate=pl.CostEstimate(
            flops=2_000_000_000, bytes_accessed=6_000_000, transcendentals=512
        ),
        name="prepare",
    )(count, table, mods, *td)


def load_weights(w, wbuf, sem):
    loads = []
    for i in range(8):
        copy = pltpu.make_async_copy(w[i], wbuf.at[pl.ds(i * RING, RING), :], sem.at[i])
        copy.start()
        loads.append(copy)
    return loads


def main_kernel(count_ref, tab_ref, modp, gated, *refs):
    w = refs[0:8]
    rows_ref = refs[8]
    g_out = refs[9:17]
    wbuf, g, gf, gp, q_s, k_s, v_s, h_s, o_s, dq_s, dk_s, dv_s, in_sem, out_sem = refs[17:]
    _, y, _, c = position()
    loads = load_weights(w, wbuf, in_sem)

    xs, a, r = places(tab_ref[...])
    inner = jnp.where((r >= 72) & (r < 90), ((a & 3) * 4 + xs) * 18 + r - 72, -1)
    pick = jnp.where(
        lax.broadcasted_iota(jnp.int32, (WIDE, PROJ), 0) == inner, 1.0, 0.0
    ).astype(BF)
    main_lane = (r >= 72) & (r < 90)
    tail_lane = r >= 90

    for copy in loads:
        copy.wait()

    lane = lax.broadcasted_iota(jnp.int32, (1, WIDE), 1)
    own_lane = lane < OWN
    qkv = dot(modp[...], wbuf[...], 1, 0)
    q_s[...] = jnp.where(own_lane, qkv[:, 0:384], 0.0).astype(BF)
    k_s[...] = jnp.where(own_lane, pltpu.roll(qkv[:, 256:640], WIDE - 32, 1), 0.0).astype(BF)
    v_s[...] = jnp.where(own_lane, pltpu.roll(qkv[:, 512:896], WIDE - 64, 1), 0.0).astype(BF)

    wp = jnp.concatenate([wbuf[PAIR * p + 64 : PAIR * p + 96, :] for p in range(16)], axis=0)
    g_lo = gated[:, 0:LANES]
    g_hi = gated[:, LANES:D]
    ghp = jnp.where(main_lane, dot(g_lo, wp, 1, 1), 0.0)
    for u in range(3):
        tail = dot(g_hi, wp[:, 256 * u : 256 * u + 256], 1, 1)
        ghp += pltpu.roll(jnp.where(tail_lane, tail, 0.0), PROJ + 6 * u - 18, 1)
    h_s[...] = dot(ghp.astype(BF), pick, 1, 1).astype(BF)

    row = lax.broadcasted_iota(jnp.int32, (256, 1), 0)
    col = lax.broadcasted_iota(jnp.int32, (1, 256), 1)
    same = ((row & 31) == (col & 31)) & (frames_of(col, y, c) < count_ref[0])
    factor = HEAD ** (-0.5)
    for ref in (o_s, dq_s, dk_s, dv_s):
        ref[...] = jnp.zeros_like(ref)
    zero = jnp.zeros((), BF)
    for s in range(2):
        at = slice(256 * s, 256 * s + 256)
        for h in range(4):
            lo = h * HEAD
            start = lo // 128 * 128
            stop = -(-(lo + HEAD) // 128) * 128
            win = slice(start, stop)
            lanes = lax.broadcasted_iota(jnp.int32, (1, stop - start), 1) + start
            inside = (lanes >= lo) & (lanes < lo + HEAD)
            qm = jnp.where(inside, q_s[at, win], zero)
            km = jnp.where(inside, k_s[at, win], zero)
            vm = jnp.where(inside, v_s[at, win], zero)
            gm = jnp.where(inside, h_s[at, win], zero)
            scores = jnp.where(same, dot(qm, km, 1, 1) * factor, -1e30)
            top = jnp.max(scores, axis=-1, keepdims=True)
            expd = jnp.exp(scores - top)
            probs = expd / jnp.sum(expd, axis=-1, keepdims=True)
            probs_b = probs.astype(BF)
            o_s[at, win] += dot(probs_b, vm, 1, 0)
            dprobs = dot(gm, vm, 1, 1)
            dv_s[at, win] += dot(probs_b, gm, 0, 0)
            delta = jnp.sum(probs * dprobs, axis=-1, keepdims=True)
            ds = (probs * (dprobs - delta) * factor).astype(BF)
            dq_s[at, win] += dot(ds, km, 1, 0)
            dk_s[at, win] += dot(ds, qm, 0, 0)

    dkr = pltpu.roll(dk_s[...], 32, 1)
    dvr = pltpu.roll(dv_s[...], 64, 1)
    rows_ref[:, 0:256] = dq_s[:, 0:256].astype(BF)
    rows_ref[:, 256:384] = (dq_s[:, 256:384] + dkr[:, 0:128]).astype(BF)
    rows_ref[:, 384:512] = dkr[:, 128:256].astype(BF)
    rows_ref[:, 512:640] = (dkr[:, 256:384] + dvr[:, 0:128]).astype(BF)
    rows_ref[:, 640:896] = dvr[:, 128:384].astype(BF)

    hmf = dot(o_s[...].astype(BF), pick, 1, 0)
    gp[...] = dot(hmf.astype(BF), g_lo, 0, 0)
    for u in range(3):
        h_u = jnp.where(tail_lane, pltpu.roll(hmf, 18 - 6 * u, 1), 0.0).astype(BF)
        gp[:, 256 * u : 256 * u + 256] += dot(h_u, g_hi, 0, 0)
    rows = rows_ref[...]
    stores = []
    for j in range(4):
        gf[...] = dot(modp[:, 384 * j : 384 * j + 384], rows, 0, 0)
        for p in range(4):
            n = 4 * j + p
            gf[PAIR * p + 64 : PAIR * p + 96, :] += gp[32 * n : 32 * n + 32, :]
        g[384 * j : 384 * j + 384, :] = gf[...].astype(BF)
        for i in (2 * j, 2 * j + 1):
            copy = pltpu.make_async_copy(g.at[pl.ds(i * RING, RING), :], g_out[i], out_sem.at[i])
            copy.start()
            stores.append(copy)
    for copy in stores:
        copy.wait()


def compute(count, table, modp, gated, w):
    wide = pltpu.VMEM((TOK, WIDE), F32)
    wide_b = pltpu.VMEM((TOK, WIDE), BF)
    outs = pl.pallas_call(
        main_kernel,
        in_specs=specs("svvv" + "a" * 8),
        out_specs=specs("v" + "a" * 8),
        out_shape=[jax.ShapeDtypeStruct((TOK, LANES), BF)]
        + [jax.ShapeDtypeStruct((RING, LANES), BF)] * 8,
        scratch_shapes=[
            pltpu.VMEM((ROWS, LANES), BF),
            pltpu.VMEM((ROWS, LANES), BF),
            pltpu.VMEM((384, LANES), F32),
            pltpu.VMEM((PROJ, LANES), F32),
            wide_b,
            wide_b,
            wide_b,
            wide_b,
            wide,
            wide,
            wide,
            wide,
            pltpu.SemaphoreType.DMA((8,)),
            pltpu.SemaphoreType.DMA((8,)),
        ],
        compiler_params=pltpu.CompilerParams(vmem_limit_bytes=VMEM_LIMIT),
        cost_estimate=pl.CostEstimate(
            flops=7_000_000_000, bytes_accessed=9_000_000, transcendentals=600_000
        ),
        name="block",
    )(count, table, modp, gated, *w)
    return outs[0], outs[1:]


def back_kernel(tab_ref, rows, *refs):
    w = refs[0:8]
    own_ref, other_ref, wbuf, perm, sem = refs[8:]
    loads = load_weights(w, wbuf, sem)
    fill_perm(tab_ref[...], perm)
    for copy in loads:
        copy.wait()
    packed = dot(rows[...], wbuf[...], 1, 1).astype(BF)
    part = dot(packed, perm[...], 1, 1).astype(BF)
    for s in range(2):
        own_ref[128 * s : 128 * s + 128, :] = part[256 * s : 256 * s + 128, :]
        other_ref[128 * s : 128 * s + 128, :] = part[256 * s + 128 : 256 * s + 256, :]


def back(table, rows, w):
    return pl.pallas_call(
        back_kernel,
        in_specs=specs("vv" + "a" * 8),
        out_specs=specs("vv"),
        out_shape=[jax.ShapeDtypeStruct((256, D), BF)] * 2,
        scratch_shapes=[
            pltpu.VMEM((ROWS, LANES), BF),
            pltpu.VMEM((D, ROWS), BF),
            pltpu.SemaphoreType.DMA((8,)),
        ],
        compiler_params=pltpu.CompilerParams(vmem_limit_bytes=VMEM_LIMIT),
        cost_estimate=pl.CostEstimate(
            flops=3_400_000_000, bytes_accessed=6_000_000, transcendentals=0
        ),
        name="back",
    )(table, rows, *w)


def final_kernel(mods_ref, own_ref, other_ref, *refs):
    td, gt = refs[0:4], refs[4:]
    normed, rstd = normalize(gather_rows(td, 0))
    grad_modded = (own_ref[...].astype(F32) + other_ref[...].astype(F32)).astype(BF).astype(F32)
    dn = grad_modded * (1.0 + mods_ref[1:2, :])
    mean_dn = jnp.mean(dn, axis=-1, keepdims=True)
    mean_dnn = jnp.mean(dn * normed, axis=-1, keepdims=True)
    grad_x = (gather_rows(td, 64) + rstd * (dn - mean_dn - normed * mean_dnn)).astype(BF)
    for s in range(2):
        for k in range(4):
            gt[k][32 * s : 32 * s + 32, :] = grad_x[128 * s + 32 * k : 128 * s + 32 * k + 32, :]


def finish(mods, own, other, td):
    return pl.pallas_call(
        final_kernel,
        out_shape=[jax.ShapeDtypeStruct((64, D), BF)] * 4,
        compiler_params=pltpu.CompilerParams(vmem_limit_bytes=VMEM_LIMIT),
        name="finish",
    )(mods, own, other, *td)


def sum_kernel(*refs):
    parts, outs = refs[:4], refs[4:]
    total = parts[0][...].astype(F32)
    for part in parts[1:]:
        total = total + part[...].astype(F32)
    for k, out in enumerate(outs):
        out[...] = total[PAIR * k : PAIR * k + PAIR, :].astype(BF)


def sum_ring(parts):
    return pl.pallas_call(
        sum_kernel,
        out_shape=[jax.ShapeDtypeStruct((PAIR, LANES), BF)] * 2,
        name="sum_ring",
    )(*parts)


def fold_kernel(*refs):
    parts, (keep, send, buf) = refs[:4], refs[4:]
    total = parts[0][...].astype(F32)
    for part in parts[1:]:
        total = total + part[...].astype(F32)
    gap = jnp.zeros((4, LANES), F32)
    for out, lo in ((keep, 0), (send, 36)):
        buf[0:36, :] = total[lo : lo + 36, :]
        buf[36:40, :] = gap
        buf[40:64, :] = total[72:96, :]
        out[...] = buf[...].astype(BF)


def fold(parts):
    return pl.pallas_call(
        fold_kernel,
        out_shape=[jax.ShapeDtypeStruct((MSG, LANES), BF)] * 2,
        scratch_shapes=[pltpu.VMEM((MSG, LANES), F32)],
        name="fold",
    )(*parts)


def unpack_kernel(own_ref, other_ref, gq_ref, gp_ref):
    _, _, z, c = position()
    own, other = own_ref[...], other_ref[...]
    first = jnp.where(c == 0, own, other)[0:36, :]
    second = jnp.where(c == 0, other, own)[0:36, :]
    cols = []
    for b in range(3):
        cols += [first[:, b * OWN : b * OWN + OWN], second[:, b * OWN : b * OWN + OWN]]
    gq_ref[...] = jnp.concatenate(cols, axis=1)
    proj = jnp.where((z >> 2) == c, own, other)
    gp_ref[:, 0:LANES] = proj[40:58, :]
    for u in range(3):
        gp_ref[6 * u : 6 * u + 6, LANES:D] = proj[58:64, 256 * u : 256 * u + 256]


def unpack(own, other):
    return pl.pallas_call(
        unpack_kernel,
        out_shape=[jax.ShapeDtypeStruct((36, QKV), F32), jax.ShapeDtypeStruct((18, D), F32)],
        name="unpack_grads",
    )(own, other)


def add(*parts):
    total = parts[0].astype(F32)
    for part in parts[1:]:
        total = total + part.astype(F32)
    return total.astype(BF)


def local(tokens, grad_out, modulation, frame_counts, w_qkv, w_proj):
    both = ("grp", "seq")
    barrier = lax.optimization_barrier
    mods = modulation[0]
    table = jnp.asarray(row_table(PAIR))
    mine = pack(w_qkv, w_proj)
    far = lax.ppermute(mine, "grp", along_z(4))
    mine, x, dy = barrier((mine, tokens[0, 0], grad_out[0, 0]))
    td = split_tokens(x, dy)
    td_in = {k: lax.ppermute(td[k], "seq", along_y(k)) for k in ORDER}
    far, td_in[1], td_in[3] = barrier((far, td_in[1], td_in[3]))
    own_td = [td[0], td_in[1], td_in[2], td_in[3]]
    pair = make_pair(mine, far)
    y_b = lax.ppermute(pair, both, slanted(-1, -2))
    y_a = lax.ppermute(pair, both, slanted(-1, 1))
    x_b = lax.ppermute(pair, "grp", along_z(-1))
    other_td = [lax.ppermute(t, "seq", CORE_SWAP) for t in own_td]
    x_b, y_a, y_b, *other_td = barrier([x_b, y_a, y_b] + other_td)
    xs, ys = {}, {}
    xs[0], ys[0] = barrier(
        (jnp.concatenate([pair, x_b], axis=0), jnp.concatenate([y_a, y_b], axis=0))
    )
    for k in ORDER:
        xs[k] = lax.ppermute(xs[0], "grp", along_x(-k))
        ys[k] = lax.ppermute(ys[0], "seq", along_y(-k))
    modp, gated = prepare(frame_counts, table, mods, own_td + other_td)
    *w, modp, gated = barrier([xs[k] for k in range(4)] + [ys[k] for k in range(4)] + [modp, gated])

    rows, grads = compute(frame_counts, jnp.asarray(row_table(32)), modp, gated, w)

    ring_in = []
    for k in ORDER:
        ring_in.append(lax.ppermute(grads[k], "grp", along_x(k)))
        ring_in.append(lax.ppermute(grads[4 + k], "seq", along_y(k)))
    own_part, other_part = back(table, rows, w)
    *ring_in, own_part, other_part = barrier(ring_in + [own_part, other_part])
    other_in = lax.ppermute(other_part, "seq", CORE_SWAP)
    x_all, y_all = [grads[0], *ring_in[0::2]], [grads[4], *ring_in[1::2]]
    y_a = add(*[t[:PAIR] for t in y_all])
    y_b = add(*[t[PAIR:] for t in y_all])
    x_next = add(*[t[PAIR:] for t in x_all])
    x_near = add(*[t[:PAIR] for t in x_all])
    z_in = [
        lax.ppermute(y_b, both, slanted(1, 2)),
        lax.ppermute(y_a, both, slanted(1, -1)),
        lax.ppermute(x_next, "grp", along_z(1)),
    ]
    gt = finish(mods, own_part, other_in, own_td)
    g_in = [lax.ppermute(gt[k], "seq", along_y(-k)) for k in ORDER]
    *z_in, g1, g2, g3 = barrier(z_in + g_in)
    keep, send = fold([x_near, *z_in])
    far = lax.ppermute(send, "grp", along_z(4))
    far, grad_x = barrier((far, join_tokens([gt[0], g1, g2, g3])))
    block = add(keep, far)
    r1, r2, r3 = barrier([lax.ppermute(block, "seq", along_y(k)) for k in ORDER])
    total = (block.astype(F32) + r2.astype(F32)) + (r1.astype(F32) + r3.astype(F32))
    grad_qkv, grad_proj = unpack(total, lax.ppermute(total, "seq", CORE_SWAP))
    return (grad_x[None, None], grad_qkv, grad_proj)


def solution(mesh):
    in_specs = (
        P("grp", "seq", None, None),
        P("grp", "seq", None, None),
        P("grp", None, None),
        P("grp"),
        P("grp", None),
        P("grp", None),
    )
    out_specs = (P("grp", "seq", None, None), P("grp", None), P("grp", None))
    return jax.shard_map(local, mesh=mesh, in_specs=in_specs, out_specs=out_specs, check_vma=False)
```

```python
import jax
import jax.numpy as jnp
import numpy as np
from jax import lax
from jax.experimental import pallas as pl
from jax.experimental.pallas import tpu as pltpu
from jax.sharding import PartitionSpec as P

BF = jnp.bfloat16
F32 = jnp.float32
HEAD = 72
D = 1152
INNER = 576
QKV = 1728
OWN = 288
LANES = 896
NX, NY, NZ = 4, 4, 8
XMSG = 64
YMSG = 40
XR = 4 * XMSG
YR = 4 * YMSG
YBASE = 4 * XR
ROWS = YBASE + 4 * YR
PROJ = 512
ORDER = (1, 2, 3)
TOK = 512
WIDE = 384
VMEM_LIMIT = 40 * 1024 * 1024


def gid(z, x):
    return (z % NZ) * NX + x % NX


def sid(y, c):
    return (y % NY) * 2 + c % 2


CORE_SWAP = [(s, s ^ 1) for s in range(8)]


def along_z(dz):
    return [(gid(z, x), gid(z + dz, x)) for z in range(NZ) for x in range(NX)]


def along_x(dx):
    return [(gid(z, x), gid(z, x + dx)) for z in range(NZ) for x in range(NX)]


def along_y(dy):
    return [(sid(y, c), sid(y + dy, c)) for y in range(NY) for c in range(2)]


def flat(z, x, y, c):
    return gid(z, x) * 8 + sid(y, c)


def x_homes(m):
    pairs = []
    for z in range(NZ):
        c = z % 2
        for x in range(NX):
            for y in range(NY):
                pairs.append((flat(z, x, y, c), flat(z - 2 * m, x, y, c)))
                pairs.append((flat(z, x, y, 1 - c), flat(z - 2 * m - 1, x, y, c)))
    return pairs


def y_homes():
    pairs = []
    for z in range(NZ):
        c = 1 - z % 2
        for x in range(NX):
            for y in range(NY):
                pairs.append((flat(z, x, y, c), flat(z - 2 * y, x, y, c)))
                pairs.append((flat(z, x, y, 1 - c), flat(z - 2 * y - 1, x, y, c)))
    return pairs


def back_home(pairs):
    return [(user, home) for home, user in pairs]


def row_table():
    n = np.arange(YBASE)
    m = np.arange(4 * YR)
    zero, one = np.zeros_like(n), np.ones_like(m)
    xt = np.stack([zero, n // XR, n // XMSG % 4, n % XMSG] + [zero] * 4)
    yt = np.stack([one, m // YR, m // YMSG % 4, m % YMSG] + [0 * one] * 4)
    return np.concatenate([xt, yt], axis=1).astype(np.int32)


def proj_table():
    t = row_table()[:, :YBASE]
    return t[:, t[3] >= 32]


def position():
    g = lax.axis_index("grp")
    s = lax.axis_index("seq")
    return g & 3, s >> 1, g >> 2, s & 1


def dot(a, b, ca, cb):
    return lax.dot_general(a, b, (((ca,), (cb,)), ((), ())), preferred_element_type=F32)


def places(tab):
    x, y, z, c = position()
    in_x, step, part = tab[0:1, :] == 0, tab[1:2, :], tab[2:3, :]
    odd = (z ^ c) & 1
    xs = (x + jnp.where(in_x, step, part)) & 3
    zs = (z + jnp.where(in_x, 2 * part + odd, 2 * ((y + step) & 3) + 1 - odd)) & 7
    return xs, zs, tab[3:4, :]


def fill_perm(tab, perm):
    xs, zs, r = places(tab)
    natural = jnp.where(r < 36, (zs * 4 + xs) * 36 + r, -1)
    for i in range(0, D, 128):
        ids = lax.broadcasted_iota(jnp.int32, (128, ROWS), 0) + i
        perm[i : i + 128, :] = jnp.where(ids == natural, 1.0, 0.0).astype(BF)


def head_columns(parity):
    return [b * INNER + (2 * i + parity) * HEAD for b in range(3) for i in range(4)]


def pack_kernel(wq_ref, wp_ref, xm_ref, ym_ref, buf):
    _, _, z, _ = position()
    wq = wq_ref[...].astype(F32)
    pad = jnp.zeros((36, LANES - 3 * OWN), F32)
    even, odd = [
        jnp.concatenate([wq[:, lo : lo + HEAD] for lo in head_columns(p)] + [pad], axis=1)
        for p in range(2)
    ]
    is_even = (z & 1) == 0
    buf[...] = jnp.zeros_like(buf)
    buf[0:36, :] = jnp.where(is_even, odd, even)
    ym_ref[...] = buf[0:YMSG, :].astype(BF)
    buf[0:36, :] = jnp.where(is_even, even, odd)
    wp = wp_ref[...].astype(F32)
    buf[40:58, :] = wp[:, 0:LANES]
    for u in range(3):
        buf[58:64, 256 * u : 256 * u + 256] = wp[6 * u : 6 * u + 6, LANES:D]
    xm_ref[...] = buf[...].astype(BF)


def pack(w_qkv, w_proj):
    return pl.pallas_call(
        pack_kernel,
        out_shape=[
            jax.ShapeDtypeStruct((XMSG, LANES), BF),
            jax.ShapeDtypeStruct((YMSG, LANES), BF),
        ],
        scratch_shapes=[pltpu.VMEM((XMSG, LANES), F32)],
        name="pack_weights",
    )(w_qkv, w_proj)


def split_kernel(tok_ref, dy_ref, *outs):
    _, y, _, _ = position()
    for k in range(4):
        off = pl.multiple_of(((y + k) & 3) * 64, 64)
        outs[k][0:64, :] = tok_ref[pl.ds(off, 64), :]
        outs[k][64:128, :] = dy_ref[pl.ds(off, 64), :]


def split_tokens(x, dy):
    return pl.pallas_call(
        split_kernel,
        out_shape=[jax.ShapeDtypeStruct((128, D), BF)] * 4,
        name="split_tokens",
    )(x, dy)


def join_kernel(g0, g1, g2, g3, out_ref):
    _, y, _, _ = position()
    for k, g in enumerate((g0, g1, g2, g3)):
        out_ref[pl.ds(pl.multiple_of(((y + k) & 3) * 64, 64), 64), :] = g[0:64, :]


def join_tokens(parts):
    return pl.pallas_call(
        join_kernel,
        out_shape=jax.ShapeDtypeStruct((256, D), BF),
        name="join_tokens",
    )(*parts)


def normalize(xf):
    mean = jnp.mean(xf, axis=-1, keepdims=True)
    cent = xf - mean
    rstd = lax.rsqrt(jnp.mean(cent * cent, axis=-1, keepdims=True) + 1e-06)
    return cent * rstd, rstd


def gather_rows(parts, base):
    return jnp.concatenate(
        [p[base + 32 * s : base + 32 * s + 32, :].astype(F32) for s in range(2) for p in parts], axis=0
    )


def frames_of(index, y, c):
    return (((y - (index >> 5)) & 3) * 2) + (c ^ ((index >> 7) & 1))


def prepare_kernel(count_ref, tab_ref, mods_ref, *refs):
    td, (modp_ref, gated_ref, perm) = refs[0:8], refs[8:]
    _, y, _, c = position()
    fill_perm(tab_ref[...], perm)
    normed, _ = normalize(gather_rows(td, 0))
    modded = (normed * (1.0 + mods_ref[1:2, :]) + mods_ref[0:1, :]).astype(BF)
    modp_ref[...] = dot(modded, perm[...], 1, 0).astype(BF)
    index = lax.broadcasted_iota(jnp.int32, (TOK, 1), 0)
    live = jnp.where(frames_of(index, y, c) < count_ref[0], 1.0, 0.0)
    gated_ref[...] = (mods_ref[2:3, :] * live * gather_rows(td, 64)).astype(BF)


def specs(kinds):
    of = {"s": pltpu.SMEM, "v": pltpu.VMEM, "a": pl.ANY}
    return [pl.BlockSpec(memory_space=of[k]) for k in kinds]


def prepare(count, table, mods, td):
    return pl.pallas_call(
        prepare_kernel,
        in_specs=specs("s" + "v" * 10),
        out_specs=specs("vv"),
        out_shape=[jax.ShapeDtypeStruct((TOK, ROWS), BF), jax.ShapeDtypeStruct((TOK, D), BF)],
        scratch_shapes=[pltpu.VMEM((D, ROWS), BF)],
        compiler_params=pltpu.CompilerParams(vmem_limit_bytes=VMEM_LIMIT),
        cost_estimate=pl.CostEstimate(
            flops=1000, bytes_accessed=1000, transcendentals=0
        ),
        name="prepare",
    )(count, table, mods, *td)


def span(i):
    return (i * XR, XR) if i < 4 else (YBASE + (i - 4) * YR, YR)


def load_weights(w, wbuf, sem):
    loads = []
    for i in range(8):
        copy = pltpu.make_async_copy(w[i], wbuf.at[pl.ds(*span(i)), :], sem.at[i])
        copy.start()
        loads.append(copy)
    return loads


def main_kernel(count_ref, tab_ref, modp, gated, *refs):
    w = refs[0:8]
    rows_ref = refs[8]
    g_out = refs[9:17]
    wbuf, g, gf, gp, q_s, k_s, v_s, h_s, o_s, dq_s, dk_s, dv_s, in_sem, out_sem = refs[17:]
    _, y, _, c = position()
    loads = load_weights(w, wbuf, in_sem)

    xs, zs, r = places(tab_ref[...])
    main_lane = (r >= 40) & (r < 58)
    tail_lane = r >= 58
    inner = jnp.where(main_lane, (zs >> 1) * HEAD + xs * 18 + r - 40, -1)
    pick = jnp.where(
        lax.broadcasted_iota(jnp.int32, (WIDE, PROJ), 0) == inner, 1.0, 0.0
    ).astype(BF)

    for copy in loads:
        copy.wait()

    lane = lax.broadcasted_iota(jnp.int32, (1, WIDE), 1)
    own_lane = lane < OWN
    qkv = dot(modp[...], wbuf[...], 1, 0)
    q_s[...] = jnp.where(own_lane, qkv[:, 0:384], 0.0).astype(BF)
    k_s[...] = jnp.where(own_lane, pltpu.roll(qkv[:, 256:640], WIDE - 32, 1), 0.0).astype(BF)
    v_s[...] = jnp.where(own_lane, pltpu.roll(qkv[:, 512:896], WIDE - 64, 1), 0.0).astype(BF)

    wp = jnp.concatenate([wbuf[XMSG * p + 32 : XMSG * p + 64, :] for p in range(16)], axis=0)
    g_lo = gated[:, 0:LANES]
    g_hi = gated[:, LANES:D]
    ghp = jnp.where(main_lane, dot(g_lo, wp, 1, 1), 0.0)
    for u in range(3):
        tail = dot(g_hi, wp[:, 256 * u : 256 * u + 256], 1, 1)
        ghp += pltpu.roll(jnp.where(tail_lane, tail, 0.0), PROJ + 6 * u - 18, 1)
    h_s[...] = dot(ghp.astype(BF), pick, 1, 1).astype(BF)

    row = lax.broadcasted_iota(jnp.int32, (256, 1), 0)
    col = lax.broadcasted_iota(jnp.int32, (1, 256), 1)
    same = ((row & 31) == (col & 31)) & (frames_of(col, y, c) < count_ref[0])
    factor = HEAD ** (-0.5)
    for ref in (o_s, dq_s, dk_s, dv_s):
        ref[...] = jnp.zeros_like(ref)
    zero = jnp.zeros((), BF)
    for s in range(2):
        at = slice(256 * s, 256 * s + 256)
        for h in range(4):
            lo = h * HEAD
            start = lo // 128 * 128
            stop = -(-(lo + HEAD) // 128) * 128
            win = slice(start, stop)
            lanes = lax.broadcasted_iota(jnp.int32, (1, stop - start), 1) + start
            inside = (lanes >= lo) & (lanes < lo + HEAD)
            qm = jnp.where(inside, q_s[at, win], zero)
            km = jnp.where(inside, k_s[at, win], zero)
            vm = jnp.where(inside, v_s[at, win], zero)
            gm = jnp.where(inside, h_s[at, win], zero)
            scores = jnp.where(same, dot(qm, km, 1, 1) * factor, -1e30)
            top = jnp.max(scores, axis=-1, keepdims=True)
            expd = jnp.exp(scores - top)
            probs = expd / jnp.sum(expd, axis=-1, keepdims=True)
            probs_b = probs.astype(BF)
            o_s[at, win] += dot(probs_b, vm, 1, 0)
            dprobs = dot(gm, vm, 1, 1)
            dv_s[at, win] += dot(probs_b, gm, 0, 0)
            delta = jnp.sum(probs * dprobs, axis=-1, keepdims=True)
            ds = (probs * (dprobs - delta) * factor).astype(BF)
            dq_s[at, win] += dot(ds, km, 1, 0)
            dk_s[at, win] += dot(ds, qm, 0, 0)

    dkr = pltpu.roll(dk_s[...], 32, 1)
    dvr = pltpu.roll(dv_s[...], 64, 1)
    rows_ref[:, 0:256] = dq_s[:, 0:256].astype(BF)
    rows_ref[:, 256:384] = (dq_s[:, 256:384] + dkr[:, 0:128]).astype(BF)
    rows_ref[:, 384:512] = dkr[:, 128:256].astype(BF)
    rows_ref[:, 512:640] = (dkr[:, 256:384] + dvr[:, 0:128]).astype(BF)
    rows_ref[:, 640:896] = dvr[:, 128:384].astype(BF)

    hmf = dot(o_s[...].astype(BF), pick, 1, 0)
    gp[...] = dot(hmf.astype(BF), g_lo, 0, 0)
    for u in range(3):
        h_u = jnp.where(tail_lane, pltpu.roll(hmf, 18 - 6 * u, 1), 0.0).astype(BF)
        gp[:, 256 * u : 256 * u + 256] += dot(h_u, g_hi, 0, 0)
    rows = rows_ref[...]
    stores = []
    for lo, size in ((0, 256), (256, 256), (512, 256), (768, 256), (1024, 256), (1280, 384)):
        gf[0:size, :] = dot(modp[:, lo : lo + size], rows, 0, 0)
        for n in range(lo // XMSG, (lo + size) // XMSG):
            if lo < YBASE:
                at = XMSG * n - lo + 32
                gf[at : at + 32, :] += gp[32 * n : 32 * n + 32, :]
        g[lo : lo + size, :] = gf[0:size, :].astype(BF)
        for i in range(8):
            start, length = span(i)
            if lo < start + length <= lo + size:
                copy = pltpu.make_async_copy(g.at[pl.ds(start, length), :], g_out[i], out_sem.at[i])
                copy.start()
                stores.append(copy)
    for copy in stores:
        copy.wait()


def compute(count, table, modp, gated, w):
    wide = pltpu.VMEM((TOK, WIDE), F32)
    wide_b = pltpu.VMEM((TOK, WIDE), BF)
    outs = pl.pallas_call(
        main_kernel,
        in_specs=specs("svvv" + "a" * 8),
        out_specs=specs("v" + "a" * 8),
        out_shape=[jax.ShapeDtypeStruct((TOK, LANES), BF)]
        + [jax.ShapeDtypeStruct((span(i)[1], LANES), BF) for i in range(8)],
        scratch_shapes=[
            pltpu.VMEM((ROWS, LANES), BF),
            pltpu.VMEM((ROWS, LANES), BF),
            pltpu.VMEM((384, LANES), F32),
            pltpu.VMEM((PROJ, LANES), F32),
            wide_b,
            wide_b,
            wide_b,
            wide_b,
            wide,
            wide,
            wide,
            wide,
            pltpu.SemaphoreType.DMA((8,)),
            pltpu.SemaphoreType.DMA((8,)),
        ],
        compiler_params=pltpu.CompilerParams(vmem_limit_bytes=VMEM_LIMIT),
        cost_estimate=pl.CostEstimate(
            flops=7_000_000_000, bytes_accessed=9_000_000, transcendentals=600_000
        ),
        name="block",
    )(count, table, modp, gated, *w)
    return outs[0], outs[1:]


def back_kernel(tab_ref, rows, *refs):
    w = refs[0:8]
    own_ref, other_ref, wbuf, perm, sem = refs[8:]
    loads = load_weights(w, wbuf, sem)
    fill_perm(tab_ref[...], perm)
    for copy in loads:
        copy.wait()
    packed = dot(rows[...], wbuf[...], 1, 1).astype(BF)
    part = dot(packed, perm[...], 1, 1).astype(BF)
    for s in range(2):
        own_ref[128 * s : 128 * s + 128, :] = part[256 * s : 256 * s + 128, :]
        other_ref[128 * s : 128 * s + 128, :] = part[256 * s + 128 : 256 * s + 256, :]


def back(table, rows, w):
    return pl.pallas_call(
        back_kernel,
        in_specs=specs("vv" + "a" * 8),
        out_specs=specs("vv"),
        out_shape=[jax.ShapeDtypeStruct((256, D), BF)] * 2,
        scratch_shapes=[
            pltpu.VMEM((ROWS, LANES), BF),
            pltpu.VMEM((D, ROWS), BF),
            pltpu.SemaphoreType.DMA((8,)),
        ],
        compiler_params=pltpu.CompilerParams(vmem_limit_bytes=VMEM_LIMIT),
        cost_estimate=pl.CostEstimate(
            flops=3_400_000_000, bytes_accessed=6_000_000, transcendentals=0
        ),
        name="back",
    )(table, rows, *w)


def final_kernel(mods_ref, own_ref, other_ref, *refs):
    td, gt = refs[0:4], refs[4:]
    normed, rstd = normalize(gather_rows(td, 0))
    grad_modded = (own_ref[...].astype(F32) + other_ref[...].astype(F32)).astype(BF).astype(F32)
    dn = grad_modded * (1.0 + mods_ref[1:2, :])
    mean_dn = jnp.mean(dn, axis=-1, keepdims=True)
    mean_dnn = jnp.mean(dn * normed, axis=-1, keepdims=True)
    grad_x = (gather_rows(td, 64) + rstd * (dn - mean_dn - normed * mean_dnn)).astype(BF)
    for s in range(2):
        for k in range(4):
            gt[k][32 * s : 32 * s + 32, :] = grad_x[128 * s + 32 * k : 128 * s + 32 * k + 32, :]


def finish(mods, own, other, td):
    return pl.pallas_call(
        final_kernel,
        out_shape=[jax.ShapeDtypeStruct((64, D), BF)] * 4,
        compiler_params=pltpu.CompilerParams(vmem_limit_bytes=VMEM_LIMIT),
        name="finish",
    )(mods, own, other, *td)


def unpack_kernel(own_ref, other_ref, gq_ref, gp_ref):
    _, _, z, _ = position()
    total = own_ref[...] + other_ref[...]
    mine, rest = total[0:36, :], total[XMSG : XMSG + 36, :]
    is_even = (z & 1) == 0
    even, odd = jnp.where(is_even, mine, rest), jnp.where(is_even, rest, mine)
    cols = []
    for n in range(12):
        cols += [even[:, n * HEAD : n * HEAD + HEAD], odd[:, n * HEAD : n * HEAD + HEAD]]
    gq_ref[...] = jnp.concatenate(cols, axis=1)
    gp_ref[:, 0:LANES] = total[40:58, :]
    for u in range(3):
        gp_ref[6 * u : 6 * u + 6, LANES:D] = total[58:64, 256 * u : 256 * u + 256]


def unpack(own, other):
    return pl.pallas_call(
        unpack_kernel,
        out_shape=[jax.ShapeDtypeStruct((36, QKV), F32), jax.ShapeDtypeStruct((18, D), F32)],
        name="unpack_grads",
    )(own, other)


def add(*parts):
    total = parts[0].astype(F32)
    for part in parts[1:]:
        total = total + part.astype(F32)
    return total.astype(BF)


def local(tokens, grad_out, modulation, frame_counts, w_qkv, w_proj):
    both = ("grp", "seq")
    barrier = lax.optimization_barrier
    mods = modulation[0]
    table = jnp.asarray(row_table())
    x_msg, y_msg = pack(w_qkv, w_proj)
    plane = lax.ppermute(y_msg, both, y_homes())
    x_parts = [lax.ppermute(x_msg, both, x_homes(m)) for m in range(4)]
    td = split_tokens(tokens[0, 0], grad_out[0, 0])
    td_in = {k: lax.ppermute(td[k], "seq", along_y(k)) for k in ORDER}
    small = [lax.ppermute(plane, "grp", along_x(-k)) for k in ORDER]
    xs, ys = {}, {}
    *x_parts, td_in[1], td_in[3] = barrier(x_parts + [td_in[1], td_in[3]])
    xs[0], plane, *small = barrier([jnp.concatenate(x_parts, axis=0), plane] + small)
    own_td = [td[0]] + [td_in[k] for k in ORDER]
    other_td = [lax.ppermute(t, "seq", CORE_SWAP) for t in own_td]
    ys[0] = jnp.concatenate([plane] + small, axis=0)
    for k in (3, 2, 1):
        ys[k] = lax.ppermute(ys[0], "seq", along_y(-k))
    for k in (3, 2, 1):
        xs[k] = lax.ppermute(xs[0], "grp", along_x(-k))
    modp, gated = prepare(frame_counts, table, mods, own_td + other_td)
    *w, modp, gated = barrier([ys[k] for k in (3, 2, 1, 0)] + [xs[k] for k in (3, 2, 1, 0)] + [modp, gated])
    w = [w[7], w[6], w[5], w[4], w[3], w[2], w[1], w[0]]

    rows, grads = compute(frame_counts, jnp.asarray(proj_table()), modp, gated, w)

    y_in, x_in = {}, {}
    y_in[1] = lax.ppermute(grads[5], "seq", along_y(1))
    for k in ORDER:
        x_in[k] = lax.ppermute(grads[k], "grp", along_x(k))
    for k in (2, 3):
        y_in[k] = lax.ppermute(grads[4 + k], "seq", along_y(k))
    own_part, other_part = back(table, rows, w)
    x1, x2, x3, y1, y2, y3, own_part, other_part = barrier(
        [x_in[k] for k in ORDER] + [y_in[k] for k in ORDER] + [own_part, other_part]
    )
    gt = finish(mods, own_part, lax.ppermute(other_part, "seq", CORE_SWAP), own_td)
    y_all, x_all = [grads[4], y1, y2, y3], [grads[0], x1, x2, x3]
    y_sum = [add(*[t[YMSG * m : YMSG * m + YMSG] for t in y_all]) for m in range(4)]
    small = [lax.ppermute(y_sum[k], "grp", along_x(k)) for k in ORDER]
    x_sum = [add(*[t[XMSG * m : XMSG * m + XMSG] for t in x_all]) for m in range(4)]
    z_in = [lax.ppermute(x_sum[m], both, back_home(x_homes(m))) for m in range(4)]
    plane = lax.ppermute(add(y_sum[0], *small), both, back_home(y_homes()))
    *z_in, plane, g0, g1, g2, g3 = barrier(z_in + [plane] + list(gt))
    block = jnp.pad(jnp.concatenate([add(*z_in), plane], axis=0), ((0, 0), (0, D - LANES)))
    out = [jnp.concatenate([g, block], axis=0) for g in (g1, g2, g3)]
    r1, r2, r3 = barrier([lax.ppermute(t, "seq", along_y(-k)) for t, k in zip(out, ORDER)])
    own, p1, p2, p3 = [
        t[lo:, :LANES].astype(F32) for t, lo in ((block, 0), (r1, 64), (r2, 64), (r3, 64))
    ]
    total = (own + p2) + (p1 + p3)
    other_total = lax.ppermute(total, "seq", CORE_SWAP)
    grad_x = join_tokens([g0, r1, r2, r3])
    other_total, grad_x = barrier((other_total, grad_x))
    grad_qkv, grad_proj = unpack(total, other_total)
    return (grad_x[None, None], grad_qkv, grad_proj)


def solution(mesh):
    in_specs = (
        P("grp", "seq", None, None),
        P("grp", "seq", None, None),
        P("grp", None, None),
        P("grp"),
        P("grp", None),
        P("grp", None),
    )
    out_specs = (P("grp", "seq", None, None), P("grp", None), P("grp", None))
    return jax.shard_map(local, mesh=mesh, in_specs=in_specs, out_specs=out_specs, check_vma=False)
```

```python
import jax
import jax.numpy as jnp
import numpy as np
from jax import lax
from jax.experimental import pallas as pl
from jax.experimental.pallas import tpu as pltpu
from jax.sharding import PartitionSpec as P

BF = jnp.bfloat16
F32 = jnp.float32
HEAD = 72
D = 1152
INNER = 576
QKV = 1728
OWN = 288
LANES = 896
NX, NY, NZ = 4, 4, 8
MSG = 64
KZ = (0, 1, 7, 2)
XR = 192
YR = 4 * MSG
YBASE = 4 * XR
ROWS = YBASE + 4 * YR
PROJ = 768
ORDER = (1, 3, 2)
TOK = 512
WIDE = 384
VMEM_LIMIT = 40 * 1024 * 1024


def gid(z, x):
    return (z % NZ) * NX + x % NX


def sid(y, c):
    return (y % NY) * 2 + c % 2


CORE_SWAP = [(s, s ^ 1) for s in range(8)]


def along_z(dz):
    return [(gid(z, x), gid(z + dz, x)) for z in range(NZ) for x in range(NX)]


def along_x(dx):
    return [(gid(z, x), gid(z, x + dx)) for z in range(NZ) for x in range(NX)]


def along_y(dy):
    return [(sid(y, c), sid(y + dy, c)) for y in range(NY) for c in range(2)]


def along_z_by_plane(sign):
    return [
        (gid(z, x) * 8 + sid(y, c), gid(z + sign * (3 + y), x) * 8 + sid(y, c))
        for z in range(NZ)
        for x in range(NX)
        for y in range(NY)
        for c in range(2)
    ]


def row_table():
    cols = []
    for step in range(4):
        for part in range(4):
            cols += [(0, step, 0, r, KZ[part], KZ[part], 0, 0) for r in range(36)]
        for even, odd in ((0, 1), (2, 7)):
            cols += [(0, step, 0, 40 + r, even, odd, 0, 0) for r in range(24)]
    for step in range(4):
        for part in range(4):
            cols += [(1, step, part, r, 0, 0, 0, 0) for r in range(MSG)]
    return np.array(cols, np.int32).T


def proj_table():
    t = row_table()
    x, y = t[:, :YBASE].reshape(8, 4, XR), t[:, YBASE:].reshape(8, 16, MSG)
    return np.concatenate([x[:, :, 128:].reshape(8, 256), y[:, :, 32:].reshape(8, 512)], axis=1)


def position():
    g = lax.axis_index("grp")
    s = lax.axis_index("seq")
    return g & 3, s >> 1, g >> 2, s & 1


def dot(a, b, ca, cb):
    return lax.dot_general(a, b, (((ca,), (cb,)), ((), ())), preferred_element_type=F32)


def places(tab):
    x, y, z, c = position()
    in_x, step = tab[0:1, :] == 0, tab[1:2, :]
    xs = (x + jnp.where(in_x, step, tab[2:3, :])) & 3
    near = jnp.where(((z ^ c) & 1) == 0, tab[4:5, :], tab[5:6, :])
    zs = (z + jnp.where(in_x, near, 3 + ((y + step) & 3))) & 7
    return xs, zs, tab[3:4, :]


def fill_perm(tab, perm):
    xs, zs, r = places(tab)
    natural = jnp.where(r < 36, (zs * 4 + xs) * 36 + r, -1)
    for i in range(0, D, 128):
        ids = lax.broadcasted_iota(jnp.int32, (128, ROWS), 0) + i
        perm[i : i + 128, :] = jnp.where(ids == natural, 1.0, 0.0).astype(BF)


def head_columns(parity):
    return [b * INNER + (2 * i + parity) * HEAD for b in range(3) for i in range(4)]


def pack_kernel(wq_ref, wp_ref, out_ref, buf):
    _, _, _, c = position()
    wq = wq_ref[...].astype(F32)
    pad = jnp.zeros((36, LANES - 3 * OWN), F32)
    even, odd = [
        jnp.concatenate([wq[:, lo : lo + HEAD] for lo in head_columns(p)] + [pad], axis=1)
        for p in range(2)
    ]
    buf[...] = jnp.zeros_like(buf)
    buf[0:36, :] = jnp.where(c == 0, even, odd)
    wp = wp_ref[...].astype(F32)
    buf[40:58, :] = wp[:, 0:LANES]
    for u in range(3):
        buf[58:64, 256 * u : 256 * u + 256] = wp[6 * u : 6 * u + 6, LANES:D]
    out_ref[...] = buf[...].astype(BF)


def pack(w_qkv, w_proj):
    return pl.pallas_call(
        pack_kernel,
        out_shape=jax.ShapeDtypeStruct((MSG, LANES), BF),
        scratch_shapes=[pltpu.VMEM((MSG, LANES), F32)],
        name="pack_weights",
    )(w_qkv, w_proj)


def join_x_kernel(own_ref, next_ref, last_ref, far_ref, out_ref, buf):
    _, _, z, c = position()
    own, nxt, last, far = [t[...].astype(F32) for t in (own_ref, next_ref, last_ref, far_ref)]
    for i, t in enumerate((own, nxt, last, far)):
        buf[36 * i : 36 * i + 36, :] = t[0:36, :]
    same = ((z ^ c) & 1) == 0
    buf[144:168, :] = jnp.where(same, own, nxt)[40:64, :]
    buf[168:192, :] = jnp.where(same, far, last)[40:64, :]
    out_ref[...] = buf[...].astype(BF)


def join_x(*parts):
    return pl.pallas_call(
        join_x_kernel,
        out_shape=jax.ShapeDtypeStruct((XR, LANES), BF),
        scratch_shapes=[pltpu.VMEM((XR, LANES), F32)],
        name="join_x",
    )(*parts)


def part_x_kernel(*refs):
    parts, outs, buf = refs[0:4], refs[4:8], refs[8]
    _, _, z, c = position()
    total = parts[0][...].astype(F32)
    for part in parts[1:]:
        total = total + part[...].astype(F32)
    same = ((z ^ c) & 1) == 0
    none = jnp.zeros((24, LANES), F32)
    first, second = total[144:168, :], total[168:192, :]
    buf[36:40, :] = none[0:4, :]
    proj = (
        jnp.where(same, first, none),
        jnp.where(same, none, first),
        jnp.where(same, none, second),
        jnp.where(same, second, none),
    )
    for i in range(4):
        buf[0:36, :] = total[36 * i : 36 * i + 36, :]
        buf[40:64, :] = proj[i]
        outs[i][...] = buf[...].astype(BF)


def part_x(parts):
    return pl.pallas_call(
        part_x_kernel,
        out_shape=[jax.ShapeDtypeStruct((MSG, LANES), BF)] * 4,
        scratch_shapes=[pltpu.VMEM((MSG, LANES), F32)],
        name="part_x",
    )(*parts)


def split_kernel(tok_ref, dy_ref, *outs):
    _, y, _, _ = position()
    for k in range(4):
        off = pl.multiple_of(((y + k) & 3) * 64, 64)
        outs[k][0:64, :] = tok_ref[pl.ds(off, 64), :]
        outs[k][64:128, :] = dy_ref[pl.ds(off, 64), :]


def split_tokens(x, dy):
    return pl.pallas_call(
        split_kernel,
        out_shape=[jax.ShapeDtypeStruct((128, D), BF)] * 4,
        name="split_tokens",
    )(x, dy)


def join_kernel(g0, g1, g2, g3, out_ref):
    _, y, _, _ = position()
    for k, g in enumerate((g0, g1, g2, g3)):
        out_ref[pl.ds(pl.multiple_of(((y + k) & 3) * 64, 64), 64), :] = g[...]


def join_tokens(parts):
    return pl.pallas_call(
        join_kernel,
        out_shape=jax.ShapeDtypeStruct((256, D), BF),
        name="join_tokens",
    )(*parts)


def normalize(xf):
    mean = jnp.mean(xf, axis=-1, keepdims=True)
    cent = xf - mean
    rstd = lax.rsqrt(jnp.mean(cent * cent, axis=-1, keepdims=True) + 1e-06)
    return cent * rstd, rstd


def gather_rows(parts, base):
    return jnp.concatenate(
        [p[base + 32 * s : base + 32 * s + 32, :].astype(F32) for s in range(2) for p in parts], axis=0
    )


def frames_of(index, y, c):
    return (((y - (index >> 5)) & 3) * 2) + (c ^ ((index >> 7) & 1))


def prepare_kernel(count_ref, tab_ref, mods_ref, *refs):
    td, (modp_ref, gated_ref, perm) = refs[0:8], refs[8:]
    _, y, _, c = position()
    fill_perm(tab_ref[...], perm)
    normed, _ = normalize(gather_rows(td, 0))
    modded = (normed * (1.0 + mods_ref[1:2, :]) + mods_ref[0:1, :]).astype(BF)
    modp_ref[...] = dot(modded, perm[...], 1, 0).astype(BF)
    index = lax.broadcasted_iota(jnp.int32, (TOK, 1), 0)
    live = jnp.where(frames_of(index, y, c) < count_ref[0], 1.0, 0.0)
    gated_ref[...] = (mods_ref[2:3, :] * live * gather_rows(td, 64)).astype(BF)


def specs(kinds):
    of = {"s": pltpu.SMEM, "v": pltpu.VMEM, "a": pl.ANY}
    return [pl.BlockSpec(memory_space=of[k]) for k in kinds]


def prepare(count, table, mods, td):
    return pl.pallas_call(
        prepare_kernel,
        in_specs=specs("s" + "v" * 10),
        out_specs=specs("vv"),
        out_shape=[jax.ShapeDtypeStruct((TOK, ROWS), BF), jax.ShapeDtypeStruct((TOK, D), BF)],
        scratch_shapes=[pltpu.VMEM((D, ROWS), BF)],
        compiler_params=pltpu.CompilerParams(vmem_limit_bytes=VMEM_LIMIT),
        cost_estimate=pl.CostEstimate(
            flops=2_000_000_000, bytes_accessed=6_000_000, transcendentals=512
        ),
        name="prepare",
    )(count, table, mods, *td)


def span(i):
    return (i * XR, XR) if i < 4 else (YBASE + (i - 4) * YR, YR)


def load_weights(w, wbuf, sem):
    loads = []
    for i in range(8):
        copy = pltpu.make_async_copy(w[i], wbuf.at[pl.ds(*span(i)), :], sem.at[i])
        copy.start()
        loads.append(copy)
    return loads


def main_kernel(count_ref, tab_ref, modp, gated, *refs):
    w = refs[0:8]
    rows_ref = refs[8]
    g_out = refs[9:17]
    wbuf, g, gf, gp, q_s, k_s, v_s, h_s, o_s, dq_s, dk_s, dv_s, in_sem, out_sem = refs[17:]
    _, y, _, c = position()
    loads = load_weights(w, wbuf, in_sem)

    xs, zs, r = places(tab_ref[...])
    mine = (zs & 1) == c
    main_lane = mine & (r >= 40) & (r < 58)
    tail_lane = mine & (r >= 58)
    inner = jnp.where(main_lane, (zs >> 1) * HEAD + xs * 18 + r - 40, -1)
    pick = jnp.where(
        lax.broadcasted_iota(jnp.int32, (WIDE, PROJ), 0) == inner, 1.0, 0.0
    ).astype(BF)

    for copy in loads:
        copy.wait()

    lane = lax.broadcasted_iota(jnp.int32, (1, WIDE), 1)
    own_lane = lane < OWN
    qkv = dot(modp[...], wbuf[...], 1, 0)
    q_s[...] = jnp.where(own_lane, qkv[:, 0:384], 0.0).astype(BF)
    k_s[...] = jnp.where(own_lane, pltpu.roll(qkv[:, 256:640], WIDE - 32, 1), 0.0).astype(BF)
    v_s[...] = jnp.where(own_lane, pltpu.roll(qkv[:, 512:896], WIDE - 64, 1), 0.0).astype(BF)

    wp = jnp.concatenate(
        [wbuf[XR * k + 128 : XR * k + XR, :] for k in range(4)]
        + [wbuf[YBASE + MSG * n + 32 : YBASE + MSG * n + MSG, :] for n in range(16)],
        axis=0,
    )
    g_lo = gated[:, 0:LANES]
    g_hi = gated[:, LANES:D]
    ghp = jnp.where(main_lane, dot(g_lo, wp, 1, 1), 0.0)
    for u in range(3):
        tail = dot(g_hi, wp[:, 256 * u : 256 * u + 256], 1, 1)
        ghp += pltpu.roll(jnp.where(tail_lane, tail, 0.0), PROJ + 6 * u - 18, 1)
    h_s[...] = dot(ghp.astype(BF), pick, 1, 1).astype(BF)

    row = lax.broadcasted_iota(jnp.int32, (256, 1), 0)
    col = lax.broadcasted_iota(jnp.int32, (1, 256), 1)
    same = ((row & 31) == (col & 31)) & (frames_of(col, y, c) < count_ref[0])
    factor = HEAD ** (-0.5)
    for ref in (o_s, dq_s, dk_s, dv_s):
        ref[...] = jnp.zeros_like(ref)
    zero = jnp.zeros((), BF)
    for s in range(2):
        at = slice(256 * s, 256 * s + 256)
        for h in range(4):
            lo = h * HEAD
            start = lo // 128 * 128
            stop = -(-(lo + HEAD) // 128) * 128
            win = slice(start, stop)
            lanes = lax.broadcasted_iota(jnp.int32, (1, stop - start), 1) + start
            inside = (lanes >= lo) & (lanes < lo + HEAD)
            qm = jnp.where(inside, q_s[at, win], zero)
            km = jnp.where(inside, k_s[at, win], zero)
            vm = jnp.where(inside, v_s[at, win], zero)
            gm = jnp.where(inside, h_s[at, win], zero)
            scores = jnp.where(same, dot(qm, km, 1, 1) * factor, -1e30)
            top = jnp.max(scores, axis=-1, keepdims=True)
            expd = jnp.exp(scores - top)
            probs = expd / jnp.sum(expd, axis=-1, keepdims=True)
            probs_b = probs.astype(BF)
            o_s[at, win] += dot(probs_b, vm, 1, 0)
            dprobs = dot(gm, vm, 1, 1)
            dv_s[at, win] += dot(probs_b, gm, 0, 0)
            delta = jnp.sum(probs * dprobs, axis=-1, keepdims=True)
            ds = (probs * (dprobs - delta) * factor).astype(BF)
            dq_s[at, win] += dot(ds, km, 1, 0)
            dk_s[at, win] += dot(ds, qm, 0, 0)

    dkr = pltpu.roll(dk_s[...], 32, 1)
    dvr = pltpu.roll(dv_s[...], 64, 1)
    rows_ref[:, 0:256] = dq_s[:, 0:256].astype(BF)
    rows_ref[:, 256:384] = (dq_s[:, 256:384] + dkr[:, 0:128]).astype(BF)
    rows_ref[:, 384:512] = dkr[:, 128:256].astype(BF)
    rows_ref[:, 512:640] = (dkr[:, 256:384] + dvr[:, 0:128]).astype(BF)
    rows_ref[:, 640:896] = dvr[:, 128:384].astype(BF)

    hmf = dot(o_s[...].astype(BF), pick, 1, 0)
    gp[...] = dot(hmf.astype(BF), g_lo, 0, 0)
    for u in range(3):
        h_u = jnp.where(tail_lane, pltpu.roll(hmf, 18 - 6 * u, 1), 0.0).astype(BF)
        gp[:, 256 * u : 256 * u + 256] += dot(h_u, g_hi, 0, 0)
    rows = rows_ref[...]
    stores = []
    for lo, size in ((0, 384), (384, 384), (768, 256), (1024, 256), (1280, 256), (1536, 256)):
        gf[0:size, :] = dot(modp[:, lo : lo + size], rows, 0, 0)
        if lo < YBASE:
            for k in range(2):
                at = XR * k + 128
                n = 64 * (lo // XR + k)
                gf[at : at + 64, :] += gp[n : n + 64, :]
        else:
            for m in range(4):
                at = MSG * m + 32
                n = 256 + 32 * ((lo - YBASE) // MSG + m)
                gf[at : at + 32, :] += gp[n : n + 32, :]
        g[lo : lo + size, :] = gf[0:size, :].astype(BF)
        for i in range(8):
            start, length = span(i)
            if lo <= start < lo + size:
                copy = pltpu.make_async_copy(g.at[pl.ds(start, length), :], g_out[i], out_sem.at[i])
                copy.start()
                stores.append(copy)
    for copy in stores:
        copy.wait()


def compute(count, table, modp, gated, w):
    wide = pltpu.VMEM((TOK, WIDE), F32)
    wide_b = pltpu.VMEM((TOK, WIDE), BF)
    outs = pl.pallas_call(
        main_kernel,
        in_specs=specs("svvv" + "a" * 8),
        out_specs=specs("v" + "a" * 8),
        out_shape=[jax.ShapeDtypeStruct((TOK, LANES), BF)]
        + [jax.ShapeDtypeStruct((span(i)[1], LANES), BF) for i in range(8)],
        scratch_shapes=[
            pltpu.VMEM((ROWS, LANES), BF),
            pltpu.VMEM((ROWS, LANES), BF),
            pltpu.VMEM((384, LANES), F32),
            pltpu.VMEM((PROJ, LANES), F32),
            wide_b,
            wide_b,
            wide_b,
            wide_b,
            wide,
            wide,
            wide,
            wide,
            pltpu.SemaphoreType.DMA((8,)),
            pltpu.SemaphoreType.DMA((8,)),
        ],
        compiler_params=pltpu.CompilerParams(vmem_limit_bytes=VMEM_LIMIT),
        cost_estimate=pl.CostEstimate(
            flops=7_000_000_000, bytes_accessed=9_000_000, transcendentals=600_000
        ),
        name="block",
    )(count, table, modp, gated, *w)
    return outs[0], outs[1:]


def back_kernel(tab_ref, rows, *refs):
    w = refs[0:8]
    own_ref, other_ref, wbuf, perm, sem = refs[8:]
    loads = load_weights(w, wbuf, sem)
    fill_perm(tab_ref[...], perm)
    for copy in loads:
        copy.wait()
    packed = dot(rows[...], wbuf[...], 1, 1).astype(BF)
    part = dot(packed, perm[...], 1, 1).astype(BF)
    for s in range(2):
        own_ref[128 * s : 128 * s + 128, :] = part[256 * s : 256 * s + 128, :]
        other_ref[128 * s : 128 * s + 128, :] = part[256 * s + 128 : 256 * s + 256, :]


def back(table, rows, w):
    return pl.pallas_call(
        back_kernel,
        in_specs=specs("vv" + "a" * 8),
        out_specs=specs("vv"),
        out_shape=[jax.ShapeDtypeStruct((256, D), BF)] * 2,
        scratch_shapes=[
            pltpu.VMEM((ROWS, LANES), BF),
            pltpu.VMEM((D, ROWS), BF),
            pltpu.SemaphoreType.DMA((8,)),
        ],
        compiler_params=pltpu.CompilerParams(vmem_limit_bytes=VMEM_LIMIT),
        cost_estimate=pl.CostEstimate(
            flops=3_400_000_000, bytes_accessed=6_000_000, transcendentals=0
        ),
        name="back",
    )(table, rows, *w)


def final_kernel(mods_ref, own_ref, other_ref, *refs):
    td, gt = refs[0:4], refs[4:]
    normed, rstd = normalize(gather_rows(td, 0))
    grad_modded = (own_ref[...].astype(F32) + other_ref[...].astype(F32)).astype(BF).astype(F32)
    dn = grad_modded * (1.0 + mods_ref[1:2, :])
    mean_dn = jnp.mean(dn, axis=-1, keepdims=True)
    mean_dnn = jnp.mean(dn * normed, axis=-1, keepdims=True)
    grad_x = (gather_rows(td, 64) + rstd * (dn - mean_dn - normed * mean_dnn)).astype(BF)
    for s in range(2):
        for k in range(4):
            gt[k][32 * s : 32 * s + 32, :] = grad_x[128 * s + 32 * k : 128 * s + 32 * k + 32, :]


def finish(mods, own, other, td):
    return pl.pallas_call(
        final_kernel,
        out_shape=[jax.ShapeDtypeStruct((64, D), BF)] * 4,
        compiler_params=pltpu.CompilerParams(vmem_limit_bytes=VMEM_LIMIT),
        name="finish",
    )(mods, own, other, *td)


def unpack_kernel(own_ref, other_ref, gq_ref, gp_ref):
    _, _, z, c = position()
    own, other = own_ref[...], other_ref[...]
    even, odd = jnp.where(c == 0, own, other), jnp.where(c == 0, other, own)
    cols = []
    for n in range(12):
        at = slice(n * HEAD, n * HEAD + HEAD)
        cols += [even[0:36, at], odd[0:36, at]]
    gq_ref[...] = jnp.concatenate(cols, axis=1)
    proj = jnp.where((z & 1) == 0, even, odd)
    gp_ref[:, 0:LANES] = proj[40:58, :]
    for u in range(3):
        gp_ref[6 * u : 6 * u + 6, LANES:D] = proj[58:64, 256 * u : 256 * u + 256]


def unpack(own, other):
    return pl.pallas_call(
        unpack_kernel,
        out_shape=[jax.ShapeDtypeStruct((36, QKV), F32), jax.ShapeDtypeStruct((18, D), F32)],
        name="unpack_grads",
    )(own, other)


def add(*parts):
    total = parts[0].astype(F32)
    for part in parts[1:]:
        total = total + part.astype(F32)
    return total.astype(BF)


def local(tokens, grad_out, modulation, frame_counts, w_qkv, w_proj):
    both = ("grp", "seq")
    barrier = lax.optimization_barrier
    mods = modulation[0]
    table = jnp.asarray(row_table())
    mine = pack(w_qkv, w_proj)
    plane = lax.ppermute(mine, both, along_z_by_plane(-1))
    near = [lax.ppermute(mine, "grp", along_z(-kz)) for kz in KZ[1:]]
    td = split_tokens(tokens[0, 0], grad_out[0, 0])
    tdr = {k: lax.ppermute(td[k], "seq", along_y(k)) for k in ORDER}
    tdr[0] = td[0]
    small = dict(zip(ORDER, barrier([lax.ppermute(plane, "grp", along_x(-k)) for k in ORDER])))
    xs = {0: join_x(mine, *near)}
    ys = {0: jnp.concatenate([plane, small[1], small[2], small[3]], axis=0)}
    for k in ORDER:
        xs[k] = lax.ppermute(xs[0], "grp", along_x(-k))
        ys[k] = lax.ppermute(ys[0], "seq", along_y(-k))
    own_td = [tdr[k] for k in range(4)]
    other_td = [lax.ppermute(t, "seq", CORE_SWAP) for t in own_td]
    modp, gated = prepare(frame_counts, table, mods, own_td + other_td)
    *w, modp, gated = barrier([xs[k] for k in range(4)] + [ys[k] for k in range(4)] + [modp, gated])

    rows, grads = compute(frame_counts, jnp.asarray(proj_table()), modp, gated, w)

    ring_in = [lax.ppermute(grads[4 + k], "seq", along_y(k)) for k in ORDER]
    ring_in += [lax.ppermute(grads[k], "grp", along_x(k)) for k in ORDER]
    own_part, other_part = back(table, rows, w)
    *ring_in, own_part, other_part = barrier(ring_in + [own_part, other_part])
    other_in = lax.ppermute(other_part, "seq", CORE_SWAP)
    y_all = [grads[4], *ring_in[:3]]
    y_sum = [add(*[t[MSG * m : MSG * m + MSG] for t in y_all]) for m in range(4)]
    small = [lax.ppermute(y_sum[k], "grp", along_x(k)) for k in ORDER]
    x_sum = part_x([grads[0], *ring_in[3:]])
    near = [lax.ppermute(x_sum[i], "grp", along_z(KZ[i])) for i in (1, 2, 3)]
    gt = finish(mods, own_part, other_in, own_td)
    s1, s2, s3, n1, n2, n3, g0, g1, g2, g3 = barrier(small + near + list(gt))
    plane = lax.ppermute(add(y_sum[0], s1, s2, s3), both, along_z_by_plane(1))
    g_in = [lax.ppermute(g, "seq", along_y(-k)) for k, g in ((1, g1), (2, g2), (3, g3))]
    plane, *g_in = barrier([plane] + g_in)
    block = add(x_sum[0], n1, n2, n3, plane)
    r_in = [lax.ppermute(block, "seq", along_y(k)) for k in ORDER]
    r1, r3, r2, grad_x = barrier(r_in + [join_tokens([g0] + g_in)])
    total = (block.astype(F32) + r2.astype(F32)) + (r1.astype(F32) + r3.astype(F32))
    grad_qkv, grad_proj = unpack(total, lax.ppermute(total, "seq", CORE_SWAP))
    return (grad_x[None, None], grad_qkv, grad_proj)


def solution(mesh):
    in_specs = (
        P("grp", "seq", None, None),
        P("grp", "seq", None, None),
        P("grp", None, None),
        P("grp"),
        P("grp", None),
        P("grp", None),
    )
    out_specs = (P("grp", "seq", None, None), P("grp", None), P("grp", None))
    return jax.shard_map(local, mesh=mesh, in_specs=in_specs, out_specs=out_specs, check_vma=False)
```

```python
import jax
import jax.numpy as jnp
import numpy as np
from jax import lax
from jax.experimental import pallas as pl
from jax.experimental.pallas import tpu as pltpu
from jax.sharding import PartitionSpec as P

BF = jnp.bfloat16
F32 = jnp.float32
HEAD = 72
D = 1152
INNER = 576
QKV = 1728
OWN = 288
LANES = 896
NX, NY, NZ = 4, 4, 8
MSG = 64
PAIR = 96
RING = 2 * PAIR
ROWS = 8 * RING
PROJ = 512
KZ = ((0, 1), (7, 2))
ORDER = (1, 3, 2)
RINGS = (("x", 1), ("x", 2), ("y", 2), ("y", 1), ("x", 3), ("y", 3))
TOK = 512
WIDE = 384
VMEM_LIMIT = 40 * 1024 * 1024


def gid(z, x):
    return (z % NZ) * NX + x % NX


def sid(y, c):
    return (y % NY) * 2 + c % 2


CORE_SWAP = [(s, s ^ 1) for s in range(8)]


def along_z(dz):
    return [(gid(z, x), gid(z + dz, x)) for z in range(NZ) for x in range(NX)]


def along_x(dx):
    return [(gid(z, x), gid(z, x + dx)) for z in range(NZ) for x in range(NX)]


def along_y(dy):
    return [(sid(y, c), sid(y + dy, c)) for y in range(NY) for c in range(2)]


def slanted(sign, dz):
    return [
        (gid(z, x) * 8 + sid(y, c), gid(z + dz, x + sign * y) * 8 + sid(y, c))
        for z in range(NZ)
        for x in range(NX)
        for y in range(NY)
        for c in range(2)
    ]


def row_table(per_pair):
    n = np.arange(16 * per_pair)
    pair, r = n // per_pair, n % per_pair + PAIR - per_pair
    ring, step, part = pair // 8, pair // 2 % 4, pair % 2
    zero = np.zeros_like(n)
    kz = np.array(KZ)[ring, part]
    return np.stack([ring, step, kz, r, zero, zero, zero, zero]).astype(np.int32)


def position():
    g = lax.axis_index("grp")
    s = lax.axis_index("seq")
    return g & 3, s >> 1, g >> 2, s & 1


def dot(a, b, ca, cb):
    return lax.dot_general(a, b, (((ca,), (cb,)), ((), ())), preferred_element_type=F32)


def places(tab):
    x, y, z, _ = position()
    step = tab[1:2, :]
    xs = (x + jnp.where(tab[0:1, :] == 0, step, y + step)) & 3
    return xs, (z + tab[2:3, :]) & 7, tab[3:4, :]


def fill_perm(tab, perm):
    xs, a, r = places(tab)
    first = (a * 4 + xs) * 36 + r
    second = (((a + 4) & 7) * 4 + xs) * 36 + r - 36
    natural = jnp.where(r < 36, first, jnp.where(r < 72, second, -1))
    for i in range(0, D, 128):
        ids = lax.broadcasted_iota(jnp.int32, (128, ROWS), 0) + i
        perm[i : i + 128, :] = jnp.where(ids == natural, 1.0, 0.0).astype(BF)


def pack_kernel(wq_ref, wp_ref, out_ref, buf):
    _, _, _, c = position()
    wq = wq_ref[...].astype(F32)
    pad = jnp.zeros((36, LANES - 3 * OWN), F32)

    def part(core):
        cols = [wq[:, b * INNER + core * OWN : b * INNER + core * OWN + OWN] for b in range(3)]
        return jnp.concatenate(cols + [pad], axis=1)

    buf[...] = jnp.zeros_like(buf)
    buf[0:36, :] = jnp.where(c == 0, part(0), part(1))
    wp = wp_ref[...].astype(F32)
    buf[40:58, :] = wp[:, 0:LANES]
    for u in range(3):
        buf[58:64, 256 * u : 256 * u + 256] = wp[6 * u : 6 * u + 6, LANES:D]
    out_ref[...] = buf[...].astype(BF)


def pack(w_qkv, w_proj):
    return pl.pallas_call(
        pack_kernel,
        out_shape=jax.ShapeDtypeStruct((MSG, LANES), BF),
        scratch_shapes=[pltpu.VMEM((MSG, LANES), F32)],
        name="pack_weights",
    )(w_qkv, w_proj)


def pair_kernel(mine_ref, far_ref, out_ref, buf):
    _, _, z, c = position()
    mine = mine_ref[...].astype(F32)
    far = far_ref[...].astype(F32)
    buf[0:36, :] = mine[0:36, :]
    buf[36:72, :] = far[0:36, :]
    buf[72:96, :] = jnp.where((z >> 2) == c, mine[40:64, :], far[40:64, :])
    out_ref[...] = buf[...].astype(BF)


def make_pair(mine, far):
    return pl.pallas_call(
        pair_kernel,
        out_shape=jax.ShapeDtypeStruct((PAIR, LANES), BF),
        scratch_shapes=[pltpu.VMEM((PAIR, LANES), F32)],
        name="pair_weights",
    )(mine, far)


def split_kernel(tok_ref, dy_ref, *outs):
    _, y, _, _ = position()
    for k in range(4):
        off = pl.multiple_of(((y + k) & 3) * 64, 64)
        outs[k][0:64, :] = tok_ref[pl.ds(off, 64), :]
        outs[k][64:128, :] = dy_ref[pl.ds(off, 64), :]


def split_tokens(x, dy):
    return pl.pallas_call(
        split_kernel,
        out_shape=[jax.ShapeDtypeStruct((128, D), BF)] * 4,
        name="split_tokens",
    )(x, dy)


def join_kernel(g0, g1, g2, g3, out_ref):
    _, y, _, _ = position()
    for k, g in enumerate((g0, g1, g2, g3)):
        out_ref[pl.ds(pl.multiple_of(((y + k) & 3) * 64, 64), 64), :] = g[...]


def join_tokens(parts):
    return pl.pallas_call(
        join_kernel,
        out_shape=jax.ShapeDtypeStruct((256, D), BF),
        name="join_tokens",
    )(*parts)


def normalize(xf):
    mean = jnp.mean(xf, axis=-1, keepdims=True)
    cent = xf - mean
    rstd = lax.rsqrt(jnp.mean(cent * cent, axis=-1, keepdims=True) + 1e-06)
    return cent * rstd, rstd


def gather_rows(parts, base):
    return jnp.concatenate(
        [p[base + 32 * s : base + 32 * s + 32, :].astype(F32) for s in range(2) for p in parts], axis=0
    )


def frames_of(index, y, c):
    return (((y - (index >> 5)) & 3) * 2) + (c ^ ((index >> 7) & 1))


def prepare_kernel(count_ref, tab_ref, mods_ref, *refs):
    own, other, (modp_ref, gated_ref, perm) = refs[0:4], refs[4], refs[5:]
    td = list(own) + [other.at[pl.ds(128 * k, 128), :] for k in range(4)]
    _, y, _, c = position()
    fill_perm(tab_ref[...], perm)
    normed, _ = normalize(gather_rows(td, 0))
    modded = (normed * (1.0 + mods_ref[1:2, :]) + mods_ref[0:1, :]).astype(BF)
    modp_ref[...] = dot(modded, perm[...], 1, 0).astype(BF)
    index = lax.broadcasted_iota(jnp.int32, (TOK, 1), 0)
    live = jnp.where(frames_of(index, y, c) < count_ref[0], 1.0, 0.0)
    gated_ref[...] = (mods_ref[2:3, :] * live * gather_rows(td, 64)).astype(BF)


def specs(kinds):
    of = {"s": pltpu.SMEM, "v": pltpu.VMEM, "a": pl.ANY}
    return [pl.BlockSpec(memory_space=of[k]) for k in kinds]


def prepare(count, table, mods, own_td, other_td):
    return pl.pallas_call(
        prepare_kernel,
        in_specs=specs("s" + "v" * 7),
        out_specs=specs("vv"),
        out_shape=[jax.ShapeDtypeStruct((TOK, ROWS), BF), jax.ShapeDtypeStruct((TOK, D), BF)],
        scratch_shapes=[pltpu.VMEM((D, ROWS), BF)],
        compiler_params=pltpu.CompilerParams(vmem_limit_bytes=VMEM_LIMIT),
        cost_estimate=pl.CostEstimate(
            flops=2_000_000_000, bytes_accessed=6_000_000, transcendentals=512
        ),
        name="prepare",
    )(count, table, mods, *own_td, other_td)


def load_weights(w, wbuf, sem):
    loads = []
    for i in range(8):
        copy = pltpu.make_async_copy(w[i], wbuf.at[pl.ds(i * RING, RING), :], sem.at[i])
        copy.start()
        loads.append(copy)
    return loads


def main_kernel(count_ref, tab_ref, modp, gated, *refs):
    w = refs[0:8]
    rows_ref = refs[8]
    g_out = refs[9:17]
    wbuf, g, gf, gp, q_s, k_s, v_s, h_s, o_s, dq_s, dk_s, dv_s, in_sem, out_sem = refs[17:]
    _, y, _, c = position()
    loads = load_weights(w, wbuf, in_sem)

    xs, a, r = places(tab_ref[...])
    inner = jnp.where((r >= 72) & (r < 90), ((a & 3) * 4 + xs) * 18 + r - 72, -1)
    pick = jnp.where(
        lax.broadcasted_iota(jnp.int32, (WIDE, PROJ), 0) == inner, 1.0, 0.0
    ).astype(BF)
    main_lane = (r >= 72) & (r < 90)
    tail_lane = r >= 90

    for copy in loads:
        copy.wait()

    lane = lax.broadcasted_iota(jnp.int32, (1, WIDE), 1)
    own_lane = lane < OWN
    qkv = dot(modp[...], wbuf[...], 1, 0)
    q_s[...] = jnp.where(own_lane, qkv[:, 0:384], 0.0).astype(BF)
    k_s[...] = jnp.where(own_lane, pltpu.roll(qkv[:, 256:640], WIDE - 32, 1), 0.0).astype(BF)
    v_s[...] = jnp.where(own_lane, pltpu.roll(qkv[:, 512:896], WIDE - 64, 1), 0.0).astype(BF)

    wp = jnp.concatenate([wbuf[PAIR * p + 64 : PAIR * p + 96, :] for p in range(16)], axis=0)
    g_lo = gated[:, 0:LANES]
    g_hi = gated[:, LANES:D]
    ghp = jnp.where(main_lane, dot(g_lo, wp, 1, 1), 0.0)
    for u in range(3):
        tail = dot(g_hi, wp[:, 256 * u : 256 * u + 256], 1, 1)
        ghp += pltpu.roll(jnp.where(tail_lane, tail, 0.0), PROJ + 6 * u - 18, 1)
    h_s[...] = dot(ghp.astype(BF), pick, 1, 1).astype(BF)

    row = lax.broadcasted_iota(jnp.int32, (256, 1), 0)
    col = lax.broadcasted_iota(jnp.int32, (1, 256), 1)
    same = ((row & 31) == (col & 31)) & (frames_of(col, y, c) < count_ref[0])
    factor = HEAD ** (-0.5)
    for ref in (o_s, dq_s, dk_s, dv_s):
        ref[...] = jnp.zeros_like(ref)
    zero = jnp.zeros((), BF)
    for s in range(2):
        at = slice(256 * s, 256 * s + 256)
        for h in range(4):
            lo = h * HEAD
            start = lo // 128 * 128
            stop = -(-(lo + HEAD) // 128) * 128
            win = slice(start, stop)
            lanes = lax.broadcasted_iota(jnp.int32, (1, stop - start), 1) + start
            inside = (lanes >= lo) & (lanes < lo + HEAD)
            qm = jnp.where(inside, q_s[at, win], zero)
            km = jnp.where(inside, k_s[at, win], zero)
            vm = jnp.where(inside, v_s[at, win], zero)
            gm = jnp.where(inside, h_s[at, win], zero)
            scores = jnp.where(same, dot(qm, km, 1, 1) * factor, -1e30)
            top = jnp.max(scores, axis=-1, keepdims=True)
            expd = jnp.exp(scores - top)
            probs = expd / jnp.sum(expd, axis=-1, keepdims=True)
            probs_b = probs.astype(BF)
            o_s[at, win] += dot(probs_b, vm, 1, 0)
            dprobs = dot(gm, vm, 1, 1)
            dv_s[at, win] += dot(probs_b, gm, 0, 0)
            delta = jnp.sum(probs * dprobs, axis=-1, keepdims=True)
            ds = (probs * (dprobs - delta) * factor).astype(BF)
            dq_s[at, win] += dot(ds, km, 1, 0)
            dk_s[at, win] += dot(ds, qm, 0, 0)

    dkr = pltpu.roll(dk_s[...], 32, 1)
    dvr = pltpu.roll(dv_s[...], 64, 1)
    rows_ref[:, 0:256] = dq_s[:, 0:256].astype(BF)
    rows_ref[:, 256:384] = (dq_s[:, 256:384] + dkr[:, 0:128]).astype(BF)
    rows_ref[:, 384:512] = dkr[:, 128:256].astype(BF)
    rows_ref[:, 512:640] = (dkr[:, 256:384] + dvr[:, 0:128]).astype(BF)
    rows_ref[:, 640:896] = dvr[:, 128:384].astype(BF)

    hmf = dot(o_s[...].astype(BF), pick, 1, 0)
    gp[...] = dot(hmf.astype(BF), g_lo, 0, 0)
    for u in range(3):
        h_u = jnp.where(tail_lane, pltpu.roll(hmf, 18 - 6 * u, 1), 0.0).astype(BF)
        gp[:, 256 * u : 256 * u + 256] += dot(h_u, g_hi, 0, 0)
    rows = rows_ref[...]
    stores = []
    for j in range(4):
        gf[...] = dot(modp[:, 384 * j : 384 * j + 384], rows, 0, 0)
        for p in range(4):
            n = 4 * j + p
            gf[PAIR * p + 64 : PAIR * p + 96, :] += gp[32 * n : 32 * n + 32, :]
        g[384 * j : 384 * j + 384, :] = gf[...].astype(BF)
        for i in (2 * j, 2 * j + 1):
            copy = pltpu.make_async_copy(g.at[pl.ds(i * RING, RING), :], g_out[i], out_sem.at[i])
            copy.start()
            stores.append(copy)
    for copy in stores:
        copy.wait()


def compute(count, table, modp, gated, w):
    wide = pltpu.VMEM((TOK, WIDE), F32)
    wide_b = pltpu.VMEM((TOK, WIDE), BF)
    outs = pl.pallas_call(
        main_kernel,
        in_specs=specs("svvv" + "a" * 8),
        out_specs=specs("v" + "a" * 8),
        out_shape=[jax.ShapeDtypeStruct((TOK, LANES), BF)]
        + [jax.ShapeDtypeStruct((RING, LANES), BF)] * 8,
        scratch_shapes=[
            pltpu.VMEM((ROWS, LANES), BF),
            pltpu.VMEM((ROWS, LANES), BF),
            pltpu.VMEM((384, LANES), F32),
            pltpu.VMEM((PROJ, LANES), F32),
            wide_b,
            wide_b,
            wide_b,
            wide_b,
            wide,
            wide,
            wide,
            wide,
            pltpu.SemaphoreType.DMA((8,)),
            pltpu.SemaphoreType.DMA((8,)),
        ],
        compiler_params=pltpu.CompilerParams(vmem_limit_bytes=VMEM_LIMIT),
        cost_estimate=pl.CostEstimate(
            flops=7_000_000_000, bytes_accessed=9_000_000, transcendentals=600_000
        ),
        name="block",
    )(count, table, modp, gated, *w)
    return outs[0], outs[1:]


def back_kernel(tab_ref, rows, *refs):
    w = refs[0:8]
    own_ref, other_ref, wbuf, perm, sem = refs[8:]
    loads = load_weights(w, wbuf, sem)
    fill_perm(tab_ref[...], perm)
    for copy in loads:
        copy.wait()
    packed = dot(rows[...], wbuf[...], 1, 1).astype(BF)
    part = dot(packed, perm[...], 1, 1).astype(BF)
    for s in range(2):
        own_ref[128 * s : 128 * s + 128, :] = part[256 * s : 256 * s + 128, :]
        other_ref[128 * s : 128 * s + 128, :] = part[256 * s + 128 : 256 * s + 256, :]


def back(table, rows, w):
    return pl.pallas_call(
        back_kernel,
        in_specs=specs("vv" + "a" * 8),
        out_specs=specs("vv"),
        out_shape=[jax.ShapeDtypeStruct((256, D), BF)] * 2,
        scratch_shapes=[
            pltpu.VMEM((ROWS, LANES), BF),
            pltpu.VMEM((D, ROWS), BF),
            pltpu.SemaphoreType.DMA((8,)),
        ],
        compiler_params=pltpu.CompilerParams(vmem_limit_bytes=VMEM_LIMIT),
        cost_estimate=pl.CostEstimate(
            flops=3_400_000_000, bytes_accessed=6_000_000, transcendentals=0
        ),
        name="back",
    )(table, rows, *w)


def final_kernel(mods_ref, own_ref, other_ref, *refs):
    td, gt = refs[0:4], refs[4:]
    normed, rstd = normalize(gather_rows(td, 0))
    grad_modded = (own_ref[...].astype(F32) + other_ref[...].astype(F32)).astype(BF).astype(F32)
    dn = grad_modded * (1.0 + mods_ref[1:2, :])
    mean_dn = jnp.mean(dn, axis=-1, keepdims=True)
    mean_dnn = jnp.mean(dn * normed, axis=-1, keepdims=True)
    grad_x = (gather_rows(td, 64) + rstd * (dn - mean_dn - normed * mean_dnn)).astype(BF)
    for s in range(2):
        for k in range(4):
            gt[k][32 * s : 32 * s + 32, :] = grad_x[128 * s + 32 * k : 128 * s + 32 * k + 32, :]


def finish(mods, own, other, td):
    return pl.pallas_call(
        final_kernel,
        out_shape=[jax.ShapeDtypeStruct((64, D), BF)] * 4,
        compiler_params=pltpu.CompilerParams(vmem_limit_bytes=VMEM_LIMIT),
        name="finish",
    )(mods, own, other, *td)


def sum_kernel(*refs):
    parts, outs = refs[:4], refs[4:]
    total = parts[0][...].astype(F32)
    for part in parts[1:]:
        total = total + part[...].astype(F32)
    for k, out in enumerate(outs):
        out[...] = total[PAIR * k : PAIR * k + PAIR, :].astype(BF)


def sum_ring(parts):
    return pl.pallas_call(
        sum_kernel,
        out_shape=[jax.ShapeDtypeStruct((PAIR, LANES), BF)] * 2,
        name="sum_ring",
    )(*parts)


def fold_kernel(*refs):
    parts, (keep, send, buf) = refs[:4], refs[4:]
    total = parts[0][...].astype(F32)
    for part in parts[1:]:
        total = total + part[...].astype(F32)
    gap = jnp.zeros((4, LANES), F32)
    for out, lo in ((keep, 0), (send, 36)):
        buf[0:36, :] = total[lo : lo + 36, :]
        buf[36:40, :] = gap
        buf[40:64, :] = total[72:96, :]
        out[...] = buf[...].astype(BF)


def fold(parts):
    return pl.pallas_call(
        fold_kernel,
        out_shape=[jax.ShapeDtypeStruct((MSG, LANES), BF)] * 2,
        scratch_shapes=[pltpu.VMEM((MSG, LANES), F32)],
        name="fold",
    )(*parts)


def unpack_kernel(own_ref, other_ref, gq_ref, gp_ref):
    _, _, z, c = position()
    own, other = own_ref[...], other_ref[...]
    first = jnp.where(c == 0, own, other)[0:36, :]
    second = jnp.where(c == 0, other, own)[0:36, :]
    cols = []
    for b in range(3):
        cols += [first[:, b * OWN : b * OWN + OWN], second[:, b * OWN : b * OWN + OWN]]
    gq_ref[...] = jnp.concatenate(cols, axis=1)
    proj = jnp.where((z >> 2) == c, own, other)
    gp_ref[:, 0:LANES] = proj[40:58, :]
    for u in range(3):
        gp_ref[6 * u : 6 * u + 6, LANES:D] = proj[58:64, 256 * u : 256 * u + 256]


def unpack(own, other):
    return pl.pallas_call(
        unpack_kernel,
        out_shape=[jax.ShapeDtypeStruct((36, QKV), F32), jax.ShapeDtypeStruct((18, D), F32)],
        name="unpack_grads",
    )(own, other)


def add(*parts):
    total = parts[0].astype(F32)
    for part in parts[1:]:
        total = total + part.astype(F32)
    return total.astype(BF)


def local(tokens, grad_out, modulation, frame_counts, w_qkv, w_proj):
    both = ("grp", "seq")
    barrier = lax.optimization_barrier
    mods = modulation[0]
    table = jnp.asarray(row_table(PAIR))
    mine = pack(w_qkv, w_proj)
    far = lax.ppermute(mine, "grp", along_z(4))
    td = split_tokens(tokens[0, 0], grad_out[0, 0])
    td_in = [lax.ppermute(td[k], "seq", along_y(k)) for k in ORDER]
    far, own0, td_in[0], td_in[1] = barrier((far, td[0], td_in[0], td_in[1]))
    pair = make_pair(mine, far)
    x_b = lax.ppermute(pair, "grp", along_z(-1))
    y_a = lax.ppermute(pair, both, slanted(-1, 1))
    y_b = lax.ppermute(pair, both, slanted(-1, -2))
    own_td = [own0, td_in[0], td_in[2], td_in[1]]
    other_td = lax.ppermute(jnp.concatenate(own_td, axis=0), "seq", CORE_SWAP)
    x_b, y_a, y_b, other_td = barrier((x_b, y_a, y_b, other_td))
    xs, ys = {}, {}
    xs[0], ys[0] = barrier(
        (jnp.concatenate([pair, x_b], axis=0), jnp.concatenate([y_a, y_b], axis=0))
    )
    for ring, k in RINGS[::-1]:
        if ring == "x":
            xs[k] = lax.ppermute(xs[0], "grp", along_x(-k))
        else:
            ys[k] = lax.ppermute(ys[0], "seq", along_y(-k))
    modp, gated = prepare(frame_counts, table, mods, own_td, other_td)
    w = [xs[k] for k in range(4)] + [ys[k] for k in range(4)]
    *w, modp, gated = barrier(w + [modp, gated])

    rows, grads = compute(frame_counts, jnp.asarray(row_table(32)), modp, gated, w)

    ring_in = []
    for ring, k in RINGS:
        if ring == "x":
            ring_in.append(lax.ppermute(grads[k], "grp", along_x(k)))
        else:
            ring_in.append(lax.ppermute(grads[4 + k], "seq", along_y(k)))
    own_part, other_part = back(table, rows, w)
    *ring_in, own_part, other_part = barrier(ring_in + [own_part, other_part])
    other_in = lax.ppermute(other_part, "seq", CORE_SWAP)
    x_all = [grads[0]] + [t for t, (ring, _) in zip(ring_in, RINGS) if ring == "x"]
    y_all = [grads[4]] + [t for t, (ring, _) in zip(ring_in, RINGS) if ring == "y"]
    y_b = add(*[t[PAIR:] for t in y_all])
    y_a = add(*[t[:PAIR] for t in y_all])
    x_next = add(*[t[PAIR:] for t in x_all])
    x_near = add(*[t[:PAIR] for t in x_all])
    z_in = [
        lax.ppermute(x_next, "grp", along_z(1)),
        lax.ppermute(y_a, both, slanted(1, -1)),
        lax.ppermute(y_b, both, slanted(1, 2)),
    ]
    gt = finish(mods, own_part, other_in, own_td)
    *z_in, g0, g1, g2, g3 = barrier(z_in + list(gt))
    keep, send = fold([x_near, *z_in])
    far = lax.ppermute(send, "grp", along_z(4))
    g_in = [lax.ppermute(g, "seq", along_y(-k)) for k, g in ((1, g1), (2, g2), (3, g3))]
    block = add(keep, far)
    r_in = [lax.ppermute(block, "seq", along_y(k)) for k in ORDER]
    r1, r3, r2, grad_x = barrier(r_in + [join_tokens([g0] + g_in)])
    total = (block.astype(F32) + r2.astype(F32)) + (r1.astype(F32) + r3.astype(F32))
    grad_qkv, grad_proj = unpack(total, lax.ppermute(total, "seq", CORE_SWAP))
    return (grad_x[None, None], grad_qkv, grad_proj)


def solution(mesh):
    in_specs = (
        P("grp", "seq", None, None),
        P("grp", "seq", None, None),
        P("grp", None, None),
        P("grp"),
        P("grp", None),
        P("grp", None),
    )
    out_specs = (P("grp", "seq", None, None), P("grp", None), P("grp", None))
    return jax.shard_map(local, mesh=mesh, in_specs=in_specs, out_specs=out_specs, check_vma=False)
```

```python
import jax
import jax.numpy as jnp
import numpy as np
from jax import lax
from jax.experimental import pallas as pl
from jax.experimental.pallas import tpu as pltpu
from jax.sharding import PartitionSpec as P

BF = jnp.bfloat16
F32 = jnp.float32
HEAD = 72
D = 1152
INNER = 576
QKV = 1728
OWN = 288
LANES = 896
NX, NY, NZ = 4, 4, 8
MSG = 64
PAIR = 96
RING = 4 * PAIR
ROWS = 4 * RING
PROJ = 512
KZ = ((0, 1, 7, 2), (0, 7, 1, 6))
ORDER = (1, 3, 2)
TOK = 512
WIDE = 384
VMEM_LIMIT = 40 * 1024 * 1024


def gid(z, x):
    return (z % NZ) * NX + x % NX


def sid(y, c):
    return (y % NY) * 2 + c % 2


CORE_SWAP = [(s, s ^ 1) for s in range(8)]


def along_y(dy):
    return [(sid(y, c), sid(y + dy, c)) for y in range(NY) for c in range(2)]


def moves(target):
    pairs = []
    for z in range(NZ):
        for x in range(NX):
            for y in range(NY):
                for c in range(2):
                    role = (c + x + y) % 2
                    to = target(x, y, z, role)
                    if to is not None:
                        u, v, w = to
                        home = gid(w, u) * 8 + sid(v, role + u + v)
                        pairs.append((gid(z, x) * 8 + sid(y, c), home))
    return pairs


def ring_moves(k):
    return moves(lambda x, y, z, role: (x, y + k, z) if role else (x + k, y, z))


def pair_moves(i, sign):
    return moves(lambda x, y, z, role: (x, y, z + sign * KZ[role][i]))


def first_moves(sign):
    return moves(lambda x, y, z, role: (x + sign * y, y, z) if role else (x, y, z + 4))


def second_moves(sign):
    return moves(lambda x, y, z, role: (x + sign * y, y, z + 4) if role else None)


def over_y(k):
    return moves(lambda x, y, z, role: (x, y + k, z))


def row_table(per_pair):
    n = np.arange(16 * per_pair)
    pair, r = n // per_pair, n % per_pair + PAIR - per_pair
    zero = np.zeros_like(n)
    kz0, kz1 = np.array(KZ)[:, pair % 4]
    return np.stack([pair // 4, kz0, kz1, r, zero, zero, zero, zero]).astype(np.int32)


def position():
    g = lax.axis_index("grp")
    s = lax.axis_index("seq")
    return g & 3, s >> 1, g >> 2, s & 1


def role_of():
    x, y, _, c = position()
    return (c + x + y) & 1


def dot(a, b, ca, cb):
    return lax.dot_general(a, b, (((ca,), (cb,)), ((), ())), preferred_element_type=F32)


def places(tab):
    x, y, z, _ = position()
    role = role_of()
    xs = (x + role * y + tab[0:1, :]) & 3
    kz = jnp.where(role == 0, tab[1:2, :], tab[2:3, :])
    return xs, (z + kz) & 7, tab[3:4, :]


def fill_perm(tab, perm):
    xs, a, r = places(tab)
    first = (a * 4 + xs) * 36 + r
    second = (((a + 4) & 7) * 4 + xs) * 36 + r - 36
    natural = jnp.where(r < 36, first, jnp.where(r < 72, second, -1))
    for i in range(0, D, 128):
        ids = lax.broadcasted_iota(jnp.int32, (128, ROWS), 0) + i
        perm[i : i + 128, :] = jnp.where(ids == natural, 1.0, 0.0).astype(BF)


def pack_kernel(wq_ref, wp_ref, out_ref, buf):
    wq = wq_ref[...].astype(F32)
    pad = jnp.zeros((36, LANES - 3 * OWN), F32)

    def part(core):
        cols = [wq[:, b * INNER + core * OWN : b * INNER + core * OWN + OWN] for b in range(3)]
        return jnp.concatenate(cols + [pad], axis=1)

    buf[...] = jnp.zeros_like(buf)
    buf[0:36, :] = jnp.where(role_of() == 0, part(0), part(1))
    wp = wp_ref[...].astype(F32)
    buf[40:58, :] = wp[:, 0:LANES]
    for u in range(3):
        buf[58:64, 256 * u : 256 * u + 256] = wp[6 * u : 6 * u + 6, LANES:D]
    out_ref[...] = buf[...].astype(BF)


def pack(w_qkv, w_proj):
    return pl.pallas_call(
        pack_kernel,
        out_shape=jax.ShapeDtypeStruct((MSG, LANES), BF),
        scratch_shapes=[pltpu.VMEM((MSG, LANES), F32)],
        name="pack_weights",
    )(w_qkv, w_proj)


def pair_kernel(mine_ref, first_ref, second_ref, out_ref, buf):
    _, _, z, _ = position()
    role = role_of()
    first = first_ref[...].astype(F32)
    near = jnp.where(role == 0, mine_ref[...].astype(F32), first)
    far = jnp.where(role == 0, first, second_ref[...].astype(F32))
    buf[0:36, :] = near[0:36, :]
    buf[36:72, :] = far[0:36, :]
    buf[72:96, :] = jnp.where((z >> 2) == role, near[40:64, :], far[40:64, :])
    out_ref[...] = buf[...].astype(BF)


def make_pair(mine, first, second):
    return pl.pallas_call(
        pair_kernel,
        out_shape=jax.ShapeDtypeStruct((PAIR, LANES), BF),
        scratch_shapes=[pltpu.VMEM((PAIR, LANES), F32)],
        name="pair_weights",
    )(mine, first, second)


def split_kernel(tok_ref, dy_ref, *outs):
    _, y, _, _ = position()
    for k in range(4):
        off = pl.multiple_of(((y + k) & 3) * 64, 64)
        outs[k][0:64, :] = tok_ref[pl.ds(off, 64), :]
        outs[k][64:128, :] = dy_ref[pl.ds(off, 64), :]


def split_tokens(x, dy):
    return pl.pallas_call(
        split_kernel,
        out_shape=[jax.ShapeDtypeStruct((128, D), BF)] * 4,
        name="split_tokens",
    )(x, dy)


def join_kernel(g0, g1, g2, g3, out_ref):
    _, y, _, _ = position()
    for k, g in enumerate((g0, g1, g2, g3)):
        out_ref[pl.ds(pl.multiple_of(((y + k) & 3) * 64, 64), 64), :] = g[...]


def join_tokens(parts):
    return pl.pallas_call(
        join_kernel,
        out_shape=jax.ShapeDtypeStruct((256, D), BF),
        name="join_tokens",
    )(*parts)


def normalize(xf):
    mean = jnp.mean(xf, axis=-1, keepdims=True)
    cent = xf - mean
    rstd = lax.rsqrt(jnp.mean(cent * cent, axis=-1, keepdims=True) + 1e-06)
    return cent * rstd, rstd


def gather_rows(parts, base):
    return jnp.concatenate(
        [p[base + 32 * s : base + 32 * s + 32, :].astype(F32) for s in range(2) for p in parts], axis=0
    )


def frames_of(index, y, c):
    return (((y - (index >> 5)) & 3) * 2) + (c ^ ((index >> 7) & 1))


def prepare_kernel(count_ref, tab_ref, mods_ref, *refs):
    td, (modp_ref, gated_ref, perm) = refs[0:8], refs[8:]
    _, y, _, c = position()
    fill_perm(tab_ref[...], perm)
    normed, _ = normalize(gather_rows(td, 0))
    modded = (normed * (1.0 + mods_ref[1:2, :]) + mods_ref[0:1, :]).astype(BF)
    modp_ref[...] = dot(modded, perm[...], 1, 0).astype(BF)
    index = lax.broadcasted_iota(jnp.int32, (TOK, 1), 0)
    live = jnp.where(frames_of(index, y, c) < count_ref[0], 1.0, 0.0)
    gated_ref[...] = (mods_ref[2:3, :] * live * gather_rows(td, 64)).astype(BF)


def specs(kinds):
    of = {"s": pltpu.SMEM, "v": pltpu.VMEM, "a": pl.ANY}
    return [pl.BlockSpec(memory_space=of[k]) for k in kinds]


def prepare(count, table, mods, td):
    return pl.pallas_call(
        prepare_kernel,
        in_specs=specs("s" + "v" * 10),
        out_specs=specs("vv"),
        out_shape=[jax.ShapeDtypeStruct((TOK, ROWS), BF), jax.ShapeDtypeStruct((TOK, D), BF)],
        scratch_shapes=[pltpu.VMEM((D, ROWS), BF)],
        compiler_params=pltpu.CompilerParams(vmem_limit_bytes=VMEM_LIMIT),
        cost_estimate=pl.CostEstimate(
            flops=2_000_000_000, bytes_accessed=6_000_000, transcendentals=512
        ),
        name="prepare",
    )(count, table, mods, *td)


def load_weights(w, wbuf, sem):
    loads = []
    for i in range(4):
        copy = pltpu.make_async_copy(w[i], wbuf.at[pl.ds(i * RING, RING), :], sem.at[i])
        copy.start()
        loads.append(copy)
    return loads


def main_kernel(count_ref, tab_ref, modp, gated, *refs):
    w = refs[0:4]
    rows_ref = refs[4]
    g_out = refs[5:9]
    wbuf, g, gf, gp, q_s, k_s, v_s, h_s, o_s, dq_s, dk_s, dv_s, in_sem, out_sem = refs[9:]
    _, y, _, c = position()
    loads = load_weights(w, wbuf, in_sem)

    xs, a, r = places(tab_ref[...])
    inner = jnp.where((r >= 72) & (r < 90), ((a & 3) * 4 + xs) * 18 + r - 72, -1)
    pick = jnp.where(
        lax.broadcasted_iota(jnp.int32, (WIDE, PROJ), 0) == inner, 1.0, 0.0
    ).astype(BF)
    main_lane = (r >= 72) & (r < 90)
    tail_lane = r >= 90

    for copy in loads:
        copy.wait()

    lane = lax.broadcasted_iota(jnp.int32, (1, WIDE), 1)
    own_lane = lane < OWN
    qkv = dot(modp[...], wbuf[...], 1, 0)
    q_s[...] = jnp.where(own_lane, qkv[:, 0:384], 0.0).astype(BF)
    k_s[...] = jnp.where(own_lane, pltpu.roll(qkv[:, 256:640], WIDE - 32, 1), 0.0).astype(BF)
    v_s[...] = jnp.where(own_lane, pltpu.roll(qkv[:, 512:896], WIDE - 64, 1), 0.0).astype(BF)

    wp = jnp.concatenate([wbuf[PAIR * p + 64 : PAIR * p + 96, :] for p in range(16)], axis=0)
    g_lo = gated[:, 0:LANES]
    g_hi = gated[:, LANES:D]
    ghp = jnp.where(main_lane, dot(g_lo, wp, 1, 1), 0.0)
    for u in range(3):
        tail = dot(g_hi, wp[:, 256 * u : 256 * u + 256], 1, 1)
        ghp += pltpu.roll(jnp.where(tail_lane, tail, 0.0), PROJ + 6 * u - 18, 1)
    h_s[...] = dot(ghp.astype(BF), pick, 1, 1).astype(BF)

    row = lax.broadcasted_iota(jnp.int32, (256, 1), 0)
    col = lax.broadcasted_iota(jnp.int32, (1, 256), 1)
    same = ((row & 31) == (col & 31)) & (frames_of(col, y, c) < count_ref[0])
    factor = HEAD ** (-0.5)
    for ref in (o_s, dq_s, dk_s, dv_s):
        ref[...] = jnp.zeros_like(ref)
    zero = jnp.zeros((), BF)
    for s in range(2):
        at = slice(256 * s, 256 * s + 256)
        for h in range(4):
            lo = h * HEAD
            start = lo // 128 * 128
            stop = -(-(lo + HEAD) // 128) * 128
            win = slice(start, stop)
            lanes = lax.broadcasted_iota(jnp.int32, (1, stop - start), 1) + start
            inside = (lanes >= lo) & (lanes < lo + HEAD)
            qm = jnp.where(inside, q_s[at, win], zero)
            km = jnp.where(inside, k_s[at, win], zero)
            vm = jnp.where(inside, v_s[at, win], zero)
            gm = jnp.where(inside, h_s[at, win], zero)
            scores = jnp.where(same, dot(qm, km, 1, 1) * factor, -1e30)
            top = jnp.max(scores, axis=-1, keepdims=True)
            expd = jnp.exp(scores - top)
            probs = expd / jnp.sum(expd, axis=-1, keepdims=True)
            probs_b = probs.astype(BF)
            o_s[at, win] += dot(probs_b, vm, 1, 0)
            dprobs = dot(gm, vm, 1, 1)
            dv_s[at, win] += dot(probs_b, gm, 0, 0)
            delta = jnp.sum(probs * dprobs, axis=-1, keepdims=True)
            ds = (probs * (dprobs - delta) * factor).astype(BF)
            dq_s[at, win] += dot(ds, km, 1, 0)
            dk_s[at, win] += dot(ds, qm, 0, 0)

    dkr = pltpu.roll(dk_s[...], 32, 1)
    dvr = pltpu.roll(dv_s[...], 64, 1)
    rows_ref[:, 0:256] = dq_s[:, 0:256].astype(BF)
    rows_ref[:, 256:384] = (dq_s[:, 256:384] + dkr[:, 0:128]).astype(BF)
    rows_ref[:, 384:512] = dkr[:, 128:256].astype(BF)
    rows_ref[:, 512:640] = (dkr[:, 256:384] + dvr[:, 0:128]).astype(BF)
    rows_ref[:, 640:896] = dvr[:, 128:384].astype(BF)

    hmf = dot(o_s[...].astype(BF), pick, 1, 0)
    gp[...] = dot(hmf.astype(BF), g_lo, 0, 0)
    for u in range(3):
        h_u = jnp.where(tail_lane, pltpu.roll(hmf, 18 - 6 * u, 1), 0.0).astype(BF)
        gp[:, 256 * u : 256 * u + 256] += dot(h_u, g_hi, 0, 0)
    rows = rows_ref[...]
    stores = []
    for j in range(4):
        gf[...] = dot(modp[:, 384 * j : 384 * j + 384], rows, 0, 0)
        for p in range(4):
            n = 4 * j + p
            gf[PAIR * p + 64 : PAIR * p + 96, :] += gp[32 * n : 32 * n + 32, :]
        g[384 * j : 384 * j + 384, :] = gf[...].astype(BF)
        copy = pltpu.make_async_copy(g.at[pl.ds(j * RING, RING), :], g_out[j], out_sem.at[j])
        copy.start()
        stores.append(copy)
    for copy in stores:
        copy.wait()


def compute(count, table, modp, gated, w):
    wide = pltpu.VMEM((TOK, WIDE), F32)
    wide_b = pltpu.VMEM((TOK, WIDE), BF)
    outs = pl.pallas_call(
        main_kernel,
        in_specs=specs("svvv" + "a" * 4),
        out_specs=specs("v" + "a" * 4),
        out_shape=[jax.ShapeDtypeStruct((TOK, LANES), BF)]
        + [jax.ShapeDtypeStruct((RING, LANES), BF)] * 4,
        scratch_shapes=[
            pltpu.VMEM((ROWS, LANES), BF),
            pltpu.VMEM((ROWS, LANES), BF),
            pltpu.VMEM((384, LANES), F32),
            pltpu.VMEM((PROJ, LANES), F32),
            wide_b,
            wide_b,
            wide_b,
            wide_b,
            wide,
            wide,
            wide,
            wide,
            pltpu.SemaphoreType.DMA((4,)),
            pltpu.SemaphoreType.DMA((4,)),
        ],
        compiler_params=pltpu.CompilerParams(vmem_limit_bytes=VMEM_LIMIT),
        cost_estimate=pl.CostEstimate(
            flops=7_000_000_000, bytes_accessed=9_000_000, transcendentals=600_000
        ),
        name="block",
    )(count, table, modp, gated, *w)
    return outs[0], outs[1:]


def back_kernel(tab_ref, rows, *refs):
    w = refs[0:4]
    own_ref, other_ref, wbuf, perm, sem = refs[4:]
    loads = load_weights(w, wbuf, sem)
    fill_perm(tab_ref[...], perm)
    for copy in loads:
        copy.wait()
    packed = dot(rows[...], wbuf[...], 1, 1).astype(BF)
    part = dot(packed, perm[...], 1, 1).astype(BF)
    for s in range(2):
        own_ref[128 * s : 128 * s + 128, :] = part[256 * s : 256 * s + 128, :]
        other_ref[128 * s : 128 * s + 128, :] = part[256 * s + 128 : 256 * s + 256, :]


def back(table, rows, w):
    return pl.pallas_call(
        back_kernel,
        in_specs=specs("vv" + "a" * 4),
        out_specs=specs("vv"),
        out_shape=[jax.ShapeDtypeStruct((256, D), BF)] * 2,
        scratch_shapes=[
            pltpu.VMEM((ROWS, LANES), BF),
            pltpu.VMEM((D, ROWS), BF),
            pltpu.SemaphoreType.DMA((4,)),
        ],
        compiler_params=pltpu.CompilerParams(vmem_limit_bytes=VMEM_LIMIT),
        cost_estimate=pl.CostEstimate(
            flops=3_400_000_000, bytes_accessed=6_000_000, transcendentals=0
        ),
        name="back",
    )(table, rows, *w)


def final_kernel(mods_ref, own_ref, other_ref, *refs):
    td, gt = refs[0:4], refs[4:]
    normed, rstd = normalize(gather_rows(td, 0))
    grad_modded = (own_ref[...].astype(F32) + other_ref[...].astype(F32)).astype(BF).astype(F32)
    dn = grad_modded * (1.0 + mods_ref[1:2, :])
    mean_dn = jnp.mean(dn, axis=-1, keepdims=True)
    mean_dnn = jnp.mean(dn * normed, axis=-1, keepdims=True)
    grad_x = (gather_rows(td, 64) + rstd * (dn - mean_dn - normed * mean_dnn)).astype(BF)
    for s in range(2):
        for k in range(4):
            gt[k][32 * s : 32 * s + 32, :] = grad_x[128 * s + 32 * k : 128 * s + 32 * k + 32, :]


def finish(mods, own, other, td):
    return pl.pallas_call(
        final_kernel,
        out_shape=[jax.ShapeDtypeStruct((64, D), BF)] * 4,
        compiler_params=pltpu.CompilerParams(vmem_limit_bytes=VMEM_LIMIT),
        name="finish",
    )(mods, own, other, *td)


def fold_kernel(*refs):
    parts, (keep, first, second, buf) = refs[:4], refs[4:]
    role = role_of()
    total = parts[0][...].astype(F32)
    for part in parts[1:]:
        total = total + part[...].astype(F32)
    near, far = total[0:36, :], total[36:72, :]
    buf[36:40, :] = jnp.zeros((4, LANES), F32)
    buf[40:64, :] = total[72:96, :]
    buf[0:36, :] = far
    second[...] = buf[...].astype(BF)
    buf[0:36, :] = jnp.where(role == 0, far, near)
    first[...] = buf[...].astype(BF)
    buf[0:36, :] = near
    keep[...] = jnp.where(role == 0, buf[...], 0.0).astype(BF)


def fold(parts):
    return pl.pallas_call(
        fold_kernel,
        out_shape=[jax.ShapeDtypeStruct((MSG, LANES), BF)] * 3,
        scratch_shapes=[pltpu.VMEM((MSG, LANES), F32)],
        name="fold",
    )(*parts)


def unpack_kernel(own_ref, other_ref, gq_ref, gp_ref):
    _, _, z, _ = position()
    role = role_of()
    own, other = own_ref[...], other_ref[...]
    first = jnp.where(role == 0, own, other)[0:36, :]
    second = jnp.where(role == 0, other, own)[0:36, :]
    cols = []
    for b in range(3):
        cols += [first[:, b * OWN : b * OWN + OWN], second[:, b * OWN : b * OWN + OWN]]
    gq_ref[...] = jnp.concatenate(cols, axis=1)
    proj = jnp.where((z >> 2) == role, own, other)
    gp_ref[:, 0:LANES] = proj[40:58, :]
    for u in range(3):
        gp_ref[6 * u : 6 * u + 6, LANES:D] = proj[58:64, 256 * u : 256 * u + 256]


def unpack(own, other):
    return pl.pallas_call(
        unpack_kernel,
        out_shape=[jax.ShapeDtypeStruct((36, QKV), F32), jax.ShapeDtypeStruct((18, D), F32)],
        name="unpack_grads",
    )(own, other)


def add(*parts):
    total = parts[0].astype(F32)
    for part in parts[1:]:
        total = total + part.astype(F32)
    return total.astype(BF)


def local(tokens, grad_out, modulation, frame_counts, w_qkv, w_proj):
    both = ("grp", "seq")
    barrier = lax.optimization_barrier
    mods = modulation[0]
    table = jnp.asarray(row_table(PAIR))
    mine = pack(w_qkv, w_proj)
    first = lax.ppermute(mine, both, first_moves(-1))
    second = lax.ppermute(mine, both, second_moves(-1))
    td = split_tokens(tokens[0, 0], grad_out[0, 0])
    td_in = [lax.ppermute(td[k], "seq", along_y(k)) for k in ORDER]
    first, own0, td_in[0], td_in[1] = barrier((first, td[0], td_in[0], td_in[1]))
    pair = make_pair(mine, first, second)
    pairs = barrier([lax.ppermute(pair, both, pair_moves(i, -1)) for i in (1, 2, 3)])
    own_td = [own0, td_in[0], td_in[2], td_in[1]]
    other_td = [lax.ppermute(t, "seq", CORE_SWAP) for t in own_td]
    w0 = jnp.concatenate([pair] + pairs, axis=0)
    w = [w0] + [lax.ppermute(w0, both, ring_moves(-k)) for k in (1, 2, 3)]
    modp, gated = prepare(frame_counts, table, mods, own_td + other_td)
    *w, modp, gated = barrier(w + [modp, gated])

    rows, grads = compute(frame_counts, jnp.asarray(row_table(32)), modp, gated, w)

    ring_in = [lax.ppermute(grads[k], both, ring_moves(k)) for k in (2, 1, 3)]
    own_part, other_part = back(table, rows, w)
    *ring_in, own_part, other_part = barrier(ring_in + [own_part, other_part])
    other_in = lax.ppermute(other_part, "seq", CORE_SWAP)
    sums = [add(*[t[PAIR * b : PAIR * b + PAIR] for t in [grads[0]] + ring_in]) for b in range(4)]
    z_in = [lax.ppermute(sums[i], both, pair_moves(i, 1)) for i in (1, 2, 3)]
    gt = finish(mods, own_part, other_in, own_td)
    *z_in, g0, g1, g2, g3 = barrier(z_in + list(gt))
    keep, first, second = fold([sums[0], *z_in])
    first = lax.ppermute(first, both, first_moves(1))
    second = lax.ppermute(second, both, second_moves(1))
    g_in = [lax.ppermute(g, "seq", along_y(-k)) for k, g in ((1, g1), (2, g2), (3, g3))]
    block = add(keep, first, second)
    r_in = [lax.ppermute(block, both, over_y(k)) for k in ORDER]
    r1, r3, r2, grad_x = barrier(r_in + [join_tokens([g0] + g_in)])
    total = (block.astype(F32) + r2.astype(F32)) + (r1.astype(F32) + r3.astype(F32))
    grad_qkv, grad_proj = unpack(total, lax.ppermute(total, "seq", CORE_SWAP))
    return (grad_x[None, None], grad_qkv, grad_proj)


def solution(mesh):
    in_specs = (
        P("grp", "seq", None, None),
        P("grp", "seq", None, None),
        P("grp", None, None),
        P("grp"),
        P("grp", None),
        P("grp", None),
    )
    out_specs = (P("grp", "seq", None, None), P("grp", None), P("grp", None))
    return jax.shard_map(local, mesh=mesh, in_specs=in_specs, out_specs=out_specs, check_vma=False)
```

```python
import jax
import jax.numpy as jnp
import numpy as np
from jax import lax
from jax.experimental import pallas as pl
from jax.experimental.pallas import tpu as pltpu
from jax.sharding import PartitionSpec as P

BF = jnp.bfloat16
F32 = jnp.float32
HEAD = 72
D = 1152
INNER = 576
QKV = 1728
OWN = 288
LANES = 896
NX, NY, NZ = 4, 4, 8
MSG = 64
PAIR = 96
RING = 4 * PAIR
ROWS = 4 * RING
PROJ = 512
KZ = ((0, 1, 7, 2), (0, 7, 1, 6))
ORDER = (1, 3, 2)
TOK = 512
WIDE = 384
VMEM_LIMIT = 40 * 1024 * 1024


def gid(z, x):
    return (z % NZ) * NX + x % NX


def sid(y, c):
    return (y % NY) * 2 + c % 2


CORE_SWAP = [(s, s ^ 1) for s in range(8)]


def along_y(dy):
    return [(sid(y, c), sid(y + dy, c)) for y in range(NY) for c in range(2)]


def moves(target):
    pairs = []
    for z in range(NZ):
        for x in range(NX):
            for y in range(NY):
                for c in range(2):
                    role = (c + x + y) % 2
                    to = target(x, y, z, role)
                    if to is not None:
                        u, v, w = to
                        home = gid(w, u) * 8 + sid(v, role + u + v)
                        pairs.append((gid(z, x) * 8 + sid(y, c), home))
    return pairs


def ring_moves(k):
    return moves(lambda x, y, z, role: (x, y + k, z) if role else (x + k, y, z))


def pair_moves(i, sign):
    return moves(lambda x, y, z, role: (x, y, z + sign * KZ[role][i]))


def first_moves(sign):
    return moves(lambda x, y, z, role: (x + sign * y, y, z) if role else (x, y, z + 4))


def second_moves(sign):
    return moves(lambda x, y, z, role: (x + sign * y, y, z + 4) if role else None)


def over_y(k):
    return moves(lambda x, y, z, role: (x, y + k, z))


def row_table(per_pair):
    n = np.arange(16 * per_pair)
    pair, r = n // per_pair, n % per_pair + PAIR - per_pair
    zero = np.zeros_like(n)
    kz0, kz1 = np.array(KZ)[:, pair % 4]
    return np.stack([pair // 4, kz0, kz1, r, zero, zero, zero, zero]).astype(np.int32)


def position():
    g = lax.axis_index("grp")
    s = lax.axis_index("seq")
    return g & 3, s >> 1, g >> 2, s & 1


def role_of():
    x, y, _, c = position()
    return (c + x + y) & 1


def dot(a, b, ca, cb):
    return lax.dot_general(a, b, (((ca,), (cb,)), ((), ())), preferred_element_type=F32)


def places(tab):
    x, y, z, _ = position()
    role = role_of()
    xs = (x + role * y + tab[0:1, :]) & 3
    kz = jnp.where(role == 0, tab[1:2, :], tab[2:3, :])
    return xs, (z + kz) & 7, tab[3:4, :]


def fill_perm(tab, perm):
    xs, a, r = places(tab)
    first = (a * 4 + xs) * 36 + r
    second = (((a + 4) & 7) * 4 + xs) * 36 + r - 36
    natural = jnp.where(r < 36, first, jnp.where(r < 72, second, -1))
    for i in range(0, D, 128):
        ids = lax.broadcasted_iota(jnp.int32, (128, ROWS), 0) + i
        perm[i : i + 128, :] = jnp.where(ids == natural, 1.0, 0.0).astype(BF)


def pack_kernel(tok_ref, dy_ref, wq_ref, wp_ref, *refs):
    outs, out_ref, buf = refs[0:4], refs[4], refs[5]
    wq = wq_ref[...].astype(F32)
    pad = jnp.zeros((36, LANES - 3 * OWN), F32)

    def part(core):
        cols = [wq[:, b * INNER + core * OWN : b * INNER + core * OWN + OWN] for b in range(3)]
        return jnp.concatenate(cols + [pad], axis=1)

    buf[...] = jnp.zeros_like(buf)
    buf[0:36, :] = jnp.where(role_of() == 0, part(0), part(1))
    wp = wp_ref[...].astype(F32)
    buf[40:58, :] = wp[:, 0:LANES]
    for u in range(3):
        buf[58:64, 256 * u : 256 * u + 256] = wp[6 * u : 6 * u + 6, LANES:D]
    out_ref[...] = buf[...].astype(BF)
    _, y, _, _ = position()
    for k in range(4):
        off = pl.multiple_of(((y + k) & 3) * 64, 64)
        outs[k][0:64, :] = tok_ref[pl.ds(off, 64), :]
        outs[k][64:128, :] = dy_ref[pl.ds(off, 64), :]


def pack(x, dy, w_qkv, w_proj):
    outs = pl.pallas_call(
        pack_kernel,
        out_shape=[jax.ShapeDtypeStruct((128, D), BF)] * 4
        + [jax.ShapeDtypeStruct((MSG, LANES), BF)],
        scratch_shapes=[pltpu.VMEM((MSG, LANES), F32)],
        name="pack",
    )(x, dy, w_qkv, w_proj)
    return outs[0:4], outs[4]


def pair_kernel(mine_ref, first_ref, second_ref, out_ref, buf):
    _, _, z, _ = position()
    role = role_of()
    first = first_ref[...].astype(F32)
    near = jnp.where(role == 0, mine_ref[...].astype(F32), first)
    far = jnp.where(role == 0, first, second_ref[...].astype(F32))
    buf[0:36, :] = near[0:36, :]
    buf[36:72, :] = far[0:36, :]
    buf[72:96, :] = jnp.where((z >> 2) == role, near[40:64, :], far[40:64, :])
    out_ref[...] = buf[...].astype(BF)


def make_pair(mine, first, second):
    return pl.pallas_call(
        pair_kernel,
        out_shape=jax.ShapeDtypeStruct((PAIR, LANES), BF),
        scratch_shapes=[pltpu.VMEM((PAIR, LANES), F32)],
        name="pair_weights",
    )(mine, first, second)


def join_kernel(g0, g1, g2, g3, out_ref):
    _, y, _, _ = position()
    for k, g in enumerate((g0, g1, g2, g3)):
        out_ref[pl.ds(pl.multiple_of(((y + k) & 3) * 64, 64), 64), :] = g[...]


def join_tokens(parts):
    return pl.pallas_call(
        join_kernel,
        out_shape=jax.ShapeDtypeStruct((256, D), BF),
        name="join_tokens",
    )(*parts)


def normalize(xf):
    mean = jnp.mean(xf, axis=-1, keepdims=True)
    cent = xf - mean
    rstd = lax.rsqrt(jnp.mean(cent * cent, axis=-1, keepdims=True) + 1e-06)
    return cent * rstd, rstd


def gather_rows(parts, base):
    return jnp.concatenate(
        [p[base + 32 * s : base + 32 * s + 32, :].astype(F32) for s in range(2) for p in parts], axis=0
    )


def frames_of(index, y, c):
    return (((y - (index >> 5)) & 3) * 2) + (c ^ ((index >> 7) & 1))


def prepare_kernel(count_ref, tab_ref, mods_ref, *refs):
    td, (modp_ref, gated_ref, perm) = refs[0:8], refs[8:]
    _, y, _, c = position()
    fill_perm(tab_ref[...], perm)
    normed, _ = normalize(gather_rows(td, 0))
    modded = (normed * (1.0 + mods_ref[1:2, :]) + mods_ref[0:1, :]).astype(BF)
    modp_ref[...] = dot(modded, perm[...], 1, 0).astype(BF)
    index = lax.broadcasted_iota(jnp.int32, (TOK, 1), 0)
    live = jnp.where(frames_of(index, y, c) < count_ref[0], 1.0, 0.0)
    gated_ref[...] = (mods_ref[2:3, :] * live * gather_rows(td, 64)).astype(BF)


def specs(kinds):
    of = {"s": pltpu.SMEM, "v": pltpu.VMEM, "a": pl.ANY}
    return [pl.BlockSpec(memory_space=of[k]) for k in kinds]


def prepare(count, table, mods, td):
    return pl.pallas_call(
        prepare_kernel,
        in_specs=specs("s" + "v" * 10),
        out_specs=specs("vv"),
        out_shape=[jax.ShapeDtypeStruct((TOK, ROWS), BF), jax.ShapeDtypeStruct((TOK, D), BF)],
        scratch_shapes=[pltpu.VMEM((D, ROWS), BF)],
        compiler_params=pltpu.CompilerParams(vmem_limit_bytes=VMEM_LIMIT),
        cost_estimate=pl.CostEstimate(
            flops=2_000_000_000, bytes_accessed=6_000_000, transcendentals=512
        ),
        name="prepare",
    )(count, table, mods, *td)


def load_weights(w, wbuf, sem):
    loads = []
    for i in range(4):
        copy = pltpu.make_async_copy(w[i], wbuf.at[pl.ds(i * RING, RING), :], sem.at[i])
        copy.start()
        loads.append(copy)
    return loads


def main_kernel(count_ref, tab_ref, modp, gated, *refs):
    w = refs[0:4]
    rows_ref = refs[4]
    g_out = refs[5:9]
    wbuf, g, gf, gp, q_s, k_s, v_s, h_s, o_s, dq_s, dk_s, dv_s, in_sem, out_sem = refs[9:]
    _, y, _, c = position()
    loads = load_weights(w, wbuf, in_sem)

    xs, a, r = places(tab_ref[...])
    inner = jnp.where((r >= 72) & (r < 90), ((a & 3) * 4 + xs) * 18 + r - 72, -1)
    pick = jnp.where(
        lax.broadcasted_iota(jnp.int32, (WIDE, PROJ), 0) == inner, 1.0, 0.0
    ).astype(BF)
    main_lane = (r >= 72) & (r < 90)
    tail_lane = r >= 90

    for copy in loads:
        copy.wait()

    lane = lax.broadcasted_iota(jnp.int32, (1, WIDE), 1)
    own_lane = lane < OWN
    qkv = dot(modp[...], wbuf[...], 1, 0)
    q_s[...] = jnp.where(own_lane, qkv[:, 0:384], 0.0).astype(BF)
    k_s[...] = jnp.where(own_lane, pltpu.roll(qkv[:, 256:640], WIDE - 32, 1), 0.0).astype(BF)
    v_s[...] = jnp.where(own_lane, pltpu.roll(qkv[:, 512:896], WIDE - 64, 1), 0.0).astype(BF)

    wp = jnp.concatenate([wbuf[PAIR * p + 64 : PAIR * p + 96, :] for p in range(16)], axis=0)
    g_lo = gated[:, 0:LANES]
    g_hi = gated[:, LANES:D]
    ghp = jnp.where(main_lane, dot(g_lo, wp, 1, 1), 0.0)
    for u in range(3):
        tail = dot(g_hi, wp[:, 256 * u : 256 * u + 256], 1, 1)
        ghp += pltpu.roll(jnp.where(tail_lane, tail, 0.0), PROJ + 6 * u - 18, 1)
    h_s[...] = dot(ghp.astype(BF), pick, 1, 1).astype(BF)

    row = lax.broadcasted_iota(jnp.int32, (256, 1), 0)
    col = lax.broadcasted_iota(jnp.int32, (1, 256), 1)
    same = ((row & 31) == (col & 31)) & (frames_of(col, y, c) < count_ref[0])
    factor = HEAD ** (-0.5)
    for ref in (o_s, dq_s, dk_s, dv_s):
        ref[...] = jnp.zeros_like(ref)
    zero = jnp.zeros((), BF)
    for s in range(2):
        at = slice(256 * s, 256 * s + 256)
        for h in range(4):
            lo = h * HEAD
            start = lo // 128 * 128
            stop = -(-(lo + HEAD) // 128) * 128
            win = slice(start, stop)
            lanes = lax.broadcasted_iota(jnp.int32, (1, stop - start), 1) + start
            inside = (lanes >= lo) & (lanes < lo + HEAD)
            qm = jnp.where(inside, q_s[at, win], zero)
            km = jnp.where(inside, k_s[at, win], zero)
            vm = jnp.where(inside, v_s[at, win], zero)
            gm = jnp.where(inside, h_s[at, win], zero)
            scores = jnp.where(same, dot(qm, km, 1, 1) * factor, -1e30)
            top = jnp.max(scores, axis=-1, keepdims=True)
            expd = jnp.exp(scores - top)
            probs = expd / jnp.sum(expd, axis=-1, keepdims=True)
            probs_b = probs.astype(BF)
            o_s[at, win] += dot(probs_b, vm, 1, 0)
            dprobs = dot(gm, vm, 1, 1)
            dv_s[at, win] += dot(probs_b, gm, 0, 0)
            delta = jnp.sum(probs * dprobs, axis=-1, keepdims=True)
            ds = (probs * (dprobs - delta) * factor).astype(BF)
            dq_s[at, win] += dot(ds, km, 1, 0)
            dk_s[at, win] += dot(ds, qm, 0, 0)

    dkr = pltpu.roll(dk_s[...], 32, 1)
    dvr = pltpu.roll(dv_s[...], 64, 1)
    rows_ref[:, 0:256] = dq_s[:, 0:256].astype(BF)
    rows_ref[:, 256:384] = (dq_s[:, 256:384] + dkr[:, 0:128]).astype(BF)
    rows_ref[:, 384:512] = dkr[:, 128:256].astype(BF)
    rows_ref[:, 512:640] = (dkr[:, 256:384] + dvr[:, 0:128]).astype(BF)
    rows_ref[:, 640:896] = dvr[:, 128:384].astype(BF)

    hmf = dot(o_s[...].astype(BF), pick, 1, 0)
    gp[...] = dot(hmf.astype(BF), g_lo, 0, 0)
    for u in range(3):
        h_u = jnp.where(tail_lane, pltpu.roll(hmf, 18 - 6 * u, 1), 0.0).astype(BF)
        gp[:, 256 * u : 256 * u + 256] += dot(h_u, g_hi, 0, 0)
    rows = rows_ref[...]
    stores = []
    for j in range(4):
        gf[...] = dot(modp[:, 384 * j : 384 * j + 384], rows, 0, 0)
        for p in range(4):
            n = 4 * j + p
            gf[PAIR * p + 64 : PAIR * p + 96, :] += gp[32 * n : 32 * n + 32, :]
        g[384 * j : 384 * j + 384, :] = gf[...].astype(BF)
        copy = pltpu.make_async_copy(g.at[pl.ds(j * RING, RING), :], g_out[j], out_sem.at[j])
        copy.start()
        stores.append(copy)
    for copy in stores:
        copy.wait()


def compute(count, table, modp, gated, w):
    wide = pltpu.VMEM((TOK, WIDE), F32)
    wide_b = pltpu.VMEM((TOK, WIDE), BF)
    outs = pl.pallas_call(
        main_kernel,
        in_specs=specs("svvv" + "a" * 4),
        out_specs=specs("v" + "a" * 4),
        out_shape=[jax.ShapeDtypeStruct((TOK, LANES), BF)]
        + [jax.ShapeDtypeStruct((RING, LANES), BF)] * 4,
        scratch_shapes=[
            pltpu.VMEM((ROWS, LANES), BF),
            pltpu.VMEM((ROWS, LANES), BF),
            pltpu.VMEM((384, LANES), F32),
            pltpu.VMEM((PROJ, LANES), F32),
            wide_b,
            wide_b,
            wide_b,
            wide_b,
            wide,
            wide,
            wide,
            wide,
            pltpu.SemaphoreType.DMA((4,)),
            pltpu.SemaphoreType.DMA((4,)),
        ],
        compiler_params=pltpu.CompilerParams(vmem_limit_bytes=VMEM_LIMIT),
        cost_estimate=pl.CostEstimate(
            flops=7_000_000_000, bytes_accessed=9_000_000, transcendentals=600_000
        ),
        name="block",
    )(count, table, modp, gated, *w)
    return outs[0], outs[1:]


def back_kernel(tab_ref, rows, *refs):
    w = refs[0:4]
    own_ref, other_ref, wbuf, perm, sem = refs[4:]
    loads = load_weights(w, wbuf, sem)
    fill_perm(tab_ref[...], perm)
    for copy in loads:
        copy.wait()
    packed = dot(rows[...], wbuf[...], 1, 1).astype(BF)
    part = dot(packed, perm[...], 1, 1).astype(BF)
    for s in range(2):
        own_ref[128 * s : 128 * s + 128, :] = part[256 * s : 256 * s + 128, :]
        other_ref[128 * s : 128 * s + 128, :] = part[256 * s + 128 : 256 * s + 256, :]


def back(table, rows, w):
    return pl.pallas_call(
        back_kernel,
        in_specs=specs("vv" + "a" * 4),
        out_specs=specs("vv"),
        out_shape=[jax.ShapeDtypeStruct((256, D), BF)] * 2,
        scratch_shapes=[
            pltpu.VMEM((ROWS, LANES), BF),
            pltpu.VMEM((D, ROWS), BF),
            pltpu.SemaphoreType.DMA((4,)),
        ],
        compiler_params=pltpu.CompilerParams(vmem_limit_bytes=VMEM_LIMIT),
        cost_estimate=pl.CostEstimate(
            flops=3_400_000_000, bytes_accessed=6_000_000, transcendentals=0
        ),
        name="back",
    )(table, rows, *w)


def final_kernel(mods_ref, own_ref, other_ref, *refs):
    td, gt = refs[0:4], refs[4:]
    normed, rstd = normalize(gather_rows(td, 0))
    grad_modded = (own_ref[...].astype(F32) + other_ref[...].astype(F32)).astype(BF).astype(F32)
    dn = grad_modded * (1.0 + mods_ref[1:2, :])
    mean_dn = jnp.mean(dn, axis=-1, keepdims=True)
    mean_dnn = jnp.mean(dn * normed, axis=-1, keepdims=True)
    grad_x = (gather_rows(td, 64) + rstd * (dn - mean_dn - normed * mean_dnn)).astype(BF)
    for s in range(2):
        for k in range(4):
            gt[k][32 * s : 32 * s + 32, :] = grad_x[128 * s + 32 * k : 128 * s + 32 * k + 32, :]


def finish(mods, own, other, td):
    return pl.pallas_call(
        final_kernel,
        out_shape=[jax.ShapeDtypeStruct((64, D), BF)] * 4,
        compiler_params=pltpu.CompilerParams(vmem_limit_bytes=VMEM_LIMIT),
        name="finish",
    )(mods, own, other, *td)


def fold_kernel(*refs):
    parts, (keep, first, second, buf) = refs[:4], refs[4:]
    role = role_of()
    total = parts[0][...].astype(F32)
    for part in parts[1:]:
        total = total + part[...].astype(F32)
    near, far = total[0:36, :], total[36:72, :]
    buf[36:40, :] = jnp.zeros((4, LANES), F32)
    buf[40:64, :] = total[72:96, :]
    buf[0:36, :] = far
    second[...] = buf[...].astype(BF)
    buf[0:36, :] = jnp.where(role == 0, far, near)
    first[...] = buf[...].astype(BF)
    buf[0:36, :] = near
    keep[...] = jnp.where(role == 0, buf[...], 0.0).astype(BF)


def fold(parts):
    return pl.pallas_call(
        fold_kernel,
        out_shape=[jax.ShapeDtypeStruct((MSG, LANES), BF)] * 3,
        scratch_shapes=[pltpu.VMEM((MSG, LANES), F32)],
        name="fold",
    )(*parts)


def unpack_kernel(own_ref, other_ref, gq_ref, gp_ref):
    _, _, z, _ = position()
    role = role_of()
    own, other = own_ref[...], other_ref[...]
    first = jnp.where(role == 0, own, other)[0:36, :]
    second = jnp.where(role == 0, other, own)[0:36, :]
    cols = []
    for b in range(3):
        cols += [first[:, b * OWN : b * OWN + OWN], second[:, b * OWN : b * OWN + OWN]]
    gq_ref[...] = jnp.concatenate(cols, axis=1)
    proj = jnp.where((z >> 2) == role, own, other)
    gp_ref[:, 0:LANES] = proj[40:58, :]
    for u in range(3):
        gp_ref[6 * u : 6 * u + 6, LANES:D] = proj[58:64, 256 * u : 256 * u + 256]


def unpack(own, other):
    return pl.pallas_call(
        unpack_kernel,
        out_shape=[jax.ShapeDtypeStruct((36, QKV), F32), jax.ShapeDtypeStruct((18, D), F32)],
        name="unpack_grads",
    )(own, other)


def add(*parts):
    total = parts[0].astype(F32)
    for part in parts[1:]:
        total = total + part.astype(F32)
    return total.astype(BF)


def local(tokens, grad_out, modulation, frame_counts, w_qkv, w_proj):
    both = ("grp", "seq")
    barrier = lax.optimization_barrier
    mods = modulation[0]
    table = jnp.asarray(row_table(PAIR))
    td, mine = pack(tokens[0, 0], grad_out[0, 0], w_qkv, w_proj)
    first = lax.ppermute(mine, both, first_moves(-1))
    second = lax.ppermute(mine, both, second_moves(-1))
    td_in = [lax.ppermute(td[k], "seq", along_y(k)) for k in ORDER]
    first, own0, *td_in = barrier([first, td[0]] + td_in)
    pair = make_pair(mine, first, second)
    pairs = [lax.ppermute(pair, both, pair_moves(i, -1)) for i in (1, 2, 3)]
    together = barrier(pairs + [own0, td_in[0], td_in[2], td_in[1]])
    pairs, own_td = together[:3], together[3:]
    other_td = [lax.ppermute(t, "seq", CORE_SWAP) for t in own_td]
    w0, *other_td = barrier([jnp.concatenate([pair] + pairs, axis=0)] + other_td)
    w = [w0] + [lax.ppermute(w0, both, ring_moves(-k)) for k in (1, 2, 3)]
    modp, gated = prepare(frame_counts, table, mods, own_td + other_td)
    *w, modp, gated = barrier(w + [modp, gated])

    rows, grads = compute(frame_counts, jnp.asarray(row_table(32)), modp, gated, w)

    ring_in = [lax.ppermute(grads[k], both, ring_moves(k)) for k in (2, 1, 3)]
    own_part, other_part = back(table, rows, w)
    *ring_in, own_part, other_part = barrier(ring_in + [own_part, other_part])
    other_in = lax.ppermute(other_part, "seq", CORE_SWAP)
    sums = [add(*[t[PAIR * b : PAIR * b + PAIR] for t in [grads[0]] + ring_in]) for b in range(4)]
    z_in = [lax.ppermute(sums[i], both, pair_moves(i, 1)) for i in (1, 2, 3)]
    gt = finish(mods, own_part, other_in, own_td)
    g_in = [lax.ppermute(gt[k], "seq", along_y(-k)) for k in (1, 2, 3)]
    *z_in, g1, g2, g3 = barrier(z_in + g_in)
    keep, first, second = fold([sums[0], *z_in])
    first = lax.ppermute(first, both, first_moves(1))
    second = lax.ppermute(second, both, second_moves(1))
    first, second, grad_x = barrier((first, second, join_tokens([gt[0], g1, g2, g3])))
    block = add(keep, first, second)
    r1, r3, r2 = barrier([lax.ppermute(block, both, over_y(k)) for k in ORDER])
    total = (block.astype(F32) + r2.astype(F32)) + (r1.astype(F32) + r3.astype(F32))
    grad_qkv, grad_proj = unpack(total, lax.ppermute(total, "seq", CORE_SWAP))
    return (grad_x[None, None], grad_qkv, grad_proj)


def solution(mesh):
    in_specs = (
        P("grp", "seq", None, None),
        P("grp", "seq", None, None),
        P("grp", None, None),
        P("grp"),
        P("grp", None),
        P("grp", None),
    )
    out_specs = (P("grp", "seq", None, None), P("grp", None), P("grp", None))
    return jax.shard_map(local, mesh=mesh, in_specs=in_specs, out_specs=out_specs, check_vma=False)
```

```python
import jax
import jax.numpy as jnp
import numpy as np
from jax import lax
from jax.experimental import pallas as pl
from jax.experimental.pallas import tpu as pltpu
from jax.sharding import PartitionSpec as P

BF = jnp.bfloat16
F32 = jnp.float32
HEAD = 72
D = 1152
INNER = 576
QKV = 1728
OWN = 288
LANES = 896
NX, NY, NZ = 4, 4, 8
MSG = 64
PAIR = 96
RING = 4 * PAIR
ROWS = 4 * RING
PROJ = 512
KZ = ((0, 1, 7, 2), (0, 7, 1, 6))
ORDER = (1, 3, 2)
TOK = 512
WIDE = 384
VMEM_LIMIT = 40 * 1024 * 1024


def gid(z, x):
    return (z % NZ) * NX + x % NX


def sid(y, c):
    return (y % NY) * 2 + c % 2


CORE_SWAP = [(s, s ^ 1) for s in range(8)]


def along_y(dy):
    return [(sid(y, c), sid(y + dy, c)) for y in range(NY) for c in range(2)]


def moves(target):
    pairs = []
    for z in range(NZ):
        for x in range(NX):
            for y in range(NY):
                for c in range(2):
                    role = (c + x + y) % 2
                    to = target(x, y, z, role)
                    if to is not None:
                        u, v, w = to
                        home = gid(w, u) * 8 + sid(v, role + u + v)
                        pairs.append((gid(z, x) * 8 + sid(y, c), home))
    return pairs


def ring_moves(k):
    return moves(lambda x, y, z, role: (x, y + k, z) if role else (x + k, y, z))


def pair_moves(i, sign):
    return moves(lambda x, y, z, role: (x, y, z + sign * KZ[role][i]))


def first_moves(sign):
    return moves(lambda x, y, z, role: (x + sign * y, y, z) if role else (x, y, z + 4))


def second_moves(sign):
    return moves(lambda x, y, z, role: (x + sign * y, y, z + 4) if role else None)


def over_y(k):
    return moves(lambda x, y, z, role: (x, y + k, z))


def row_table(per_pair):
    n = np.arange(16 * per_pair)
    pair, r = n // per_pair, n % per_pair + PAIR - per_pair
    zero = np.zeros_like(n)
    kz0, kz1 = np.array(KZ)[:, pair % 4]
    return np.stack([pair // 4, kz0, kz1, r, zero, zero, zero, zero]).astype(np.int32)


def position():
    g = lax.axis_index("grp")
    s = lax.axis_index("seq")
    return g & 3, s >> 1, g >> 2, s & 1


def role_of():
    x, y, _, c = position()
    return (c + x + y) & 1


def dot(a, b, ca, cb):
    return lax.dot_general(a, b, (((ca,), (cb,)), ((), ())), preferred_element_type=F32)


def places(tab):
    x, y, z, _ = position()
    role = role_of()
    xs = (x + role * y + tab[0:1, :]) & 3
    kz = jnp.where(role == 0, tab[1:2, :], tab[2:3, :])
    return xs, (z + kz) & 7, tab[3:4, :]


def fill_perm(tab, perm):
    xs, a, r = places(tab)
    first = (a * 4 + xs) * 36 + r
    second = (((a + 4) & 7) * 4 + xs) * 36 + r - 36
    natural = jnp.where(r < 36, first, jnp.where(r < 72, second, -1))
    for i in range(0, D, 128):
        ids = lax.broadcasted_iota(jnp.int32, (128, ROWS), 0) + i
        perm[i : i + 128, :] = jnp.where(ids == natural, 1.0, 0.0).astype(BF)


def pack_kernel(tok_ref, dy_ref, wq_ref, wp_ref, *refs):
    outs, out_ref, buf = refs[0:4], refs[4], refs[5]
    wq = wq_ref[...].astype(F32)
    pad = jnp.zeros((36, LANES - 3 * OWN), F32)

    def part(core):
        cols = [wq[:, b * INNER + core * OWN : b * INNER + core * OWN + OWN] for b in range(3)]
        return jnp.concatenate(cols + [pad], axis=1)

    buf[...] = jnp.zeros_like(buf)
    buf[0:36, :] = jnp.where(role_of() == 0, part(0), part(1))
    wp = wp_ref[...].astype(F32)
    buf[40:58, :] = wp[:, 0:LANES]
    for u in range(3):
        buf[58:64, 256 * u : 256 * u + 256] = wp[6 * u : 6 * u + 6, LANES:D]
    out_ref[...] = buf[...].astype(BF)
    _, y, _, _ = position()
    for k in range(4):
        off = pl.multiple_of(((y + k) & 3) * 64, 64)
        outs[k][0:64, :] = tok_ref[pl.ds(off, 64), :]
        outs[k][64:128, :] = dy_ref[pl.ds(off, 64), :]


def pack(x, dy, w_qkv, w_proj):
    outs = pl.pallas_call(
        pack_kernel,
        out_shape=[jax.ShapeDtypeStruct((128, D), BF)] * 4
        + [jax.ShapeDtypeStruct((MSG, LANES), BF)],
        scratch_shapes=[pltpu.VMEM((MSG, LANES), F32)],
        name="pack",
    )(x, dy, w_qkv, w_proj)
    return outs[0:4], outs[4]


def pair_kernel(mine_ref, first_ref, second_ref, out_ref, buf):
    _, _, z, _ = position()
    role = role_of()
    first = first_ref[...].astype(F32)
    near = jnp.where(role == 0, mine_ref[...].astype(F32), first)
    far = jnp.where(role == 0, first, second_ref[...].astype(F32))
    buf[0:36, :] = near[0:36, :]
    buf[36:72, :] = far[0:36, :]
    buf[72:96, :] = jnp.where((z >> 2) == role, near[40:64, :], far[40:64, :])
    out_ref[...] = buf[...].astype(BF)


def make_pair(mine, first, second):
    return pl.pallas_call(
        pair_kernel,
        out_shape=jax.ShapeDtypeStruct((PAIR, LANES), BF),
        scratch_shapes=[pltpu.VMEM((PAIR, LANES), F32)],
        name="pair_weights",
    )(mine, first, second)


def join_kernel(g0, g1, g2, g3, out_ref):
    _, y, _, _ = position()
    for k, g in enumerate((g0, g1, g2, g3)):
        out_ref[pl.ds(pl.multiple_of(((y + k) & 3) * 64, 64), 64), :] = g[...]


def join_tokens(parts):
    return pl.pallas_call(
        join_kernel,
        out_shape=jax.ShapeDtypeStruct((256, D), BF),
        name="join_tokens",
    )(*parts)


def normalize(xf):
    mean = jnp.mean(xf, axis=-1, keepdims=True)
    cent = xf - mean
    rstd = lax.rsqrt(jnp.mean(cent * cent, axis=-1, keepdims=True) + 1e-06)
    return cent * rstd, rstd


def gather_rows(parts, base):
    return jnp.concatenate(
        [p[base + 32 * s : base + 32 * s + 32, :].astype(F32) for s in range(2) for p in parts], axis=0
    )


def frames_of(index, y, c):
    return (((y - (index >> 5)) & 3) * 2) + (c ^ ((index >> 7) & 1))


def prepare_kernel(count_ref, tab_ref, mods_ref, *refs):
    td, (modp_ref, gated_ref, perm) = refs[0:8], refs[8:]
    _, y, _, c = position()
    fill_perm(tab_ref[...], perm)
    normed, _ = normalize(gather_rows(td, 0))
    modded = (normed * (1.0 + mods_ref[1:2, :]) + mods_ref[0:1, :]).astype(BF)
    modp_ref[...] = dot(modded, perm[...], 1, 0).astype(BF)
    index = lax.broadcasted_iota(jnp.int32, (TOK, 1), 0)
    live = jnp.where(frames_of(index, y, c) < count_ref[0], 1.0, 0.0)
    gated_ref[...] = (mods_ref[2:3, :] * live * gather_rows(td, 64)).astype(BF)


def specs(kinds):
    of = {"s": pltpu.SMEM, "v": pltpu.VMEM, "a": pl.ANY}
    return [pl.BlockSpec(memory_space=of[k]) for k in kinds]


def prepare(count, table, mods, td):
    return pl.pallas_call(
        prepare_kernel,
        in_specs=specs("s" + "v" * 10),
        out_specs=specs("vv"),
        out_shape=[jax.ShapeDtypeStruct((TOK, ROWS), BF), jax.ShapeDtypeStruct((TOK, D), BF)],
        scratch_shapes=[pltpu.VMEM((D, ROWS), BF)],
        compiler_params=pltpu.CompilerParams(vmem_limit_bytes=VMEM_LIMIT),
        cost_estimate=pl.CostEstimate(
            flops=2_000_000_000, bytes_accessed=6_000_000, transcendentals=512
        ),
        name="prepare",
    )(count, table, mods, *td)


def load_weights(w, wbuf, sem):
    loads = []
    for i in range(4):
        copy = pltpu.make_async_copy(w[i], wbuf.at[pl.ds(i * RING, RING), :], sem.at[i])
        copy.start()
        loads.append(copy)
    return loads


def main_kernel(count_ref, tab_ref, modp, gated, *refs):
    w = refs[0:4]
    rows_ref = refs[4]
    g_out = refs[5:9]
    wbuf, g, gf, gp, q_s, k_s, v_s, h_s, o_s, dq_s, dk_s, dv_s, in_sem, out_sem = refs[9:]
    _, y, _, c = position()
    loads = load_weights(w, wbuf, in_sem)

    xs, a, r = places(tab_ref[...])
    inner = jnp.where((r >= 72) & (r < 90), ((a & 3) * 4 + xs) * 18 + r - 72, -1)
    pick = jnp.where(
        lax.broadcasted_iota(jnp.int32, (WIDE, PROJ), 0) == inner, 1.0, 0.0
    ).astype(BF)
    main_lane = (r >= 72) & (r < 90)
    tail_lane = r >= 90

    for copy in loads:
        copy.wait()

    lane = lax.broadcasted_iota(jnp.int32, (1, WIDE), 1)
    own_lane = lane < OWN
    qkv = dot(modp[...], wbuf[...], 1, 0)
    q_s[...] = jnp.where(own_lane, qkv[:, 0:384], 0.0).astype(BF)
    k_s[...] = jnp.where(own_lane, pltpu.roll(qkv[:, 256:640], WIDE - 32, 1), 0.0).astype(BF)
    v_s[...] = jnp.where(own_lane, pltpu.roll(qkv[:, 512:896], WIDE - 64, 1), 0.0).astype(BF)

    wp = jnp.concatenate([wbuf[PAIR * p + 64 : PAIR * p + 96, :] for p in range(16)], axis=0)
    g_lo = gated[:, 0:LANES]
    g_hi = gated[:, LANES:D]
    ghp = jnp.where(main_lane, dot(g_lo, wp, 1, 1), 0.0)
    for u in range(3):
        tail = dot(g_hi, wp[:, 256 * u : 256 * u + 256], 1, 1)
        ghp += pltpu.roll(jnp.where(tail_lane, tail, 0.0), PROJ + 6 * u - 18, 1)
    h_s[...] = dot(ghp.astype(BF), pick, 1, 1).astype(BF)

    row = lax.broadcasted_iota(jnp.int32, (256, 1), 0)
    col = lax.broadcasted_iota(jnp.int32, (1, 256), 1)
    same = ((row & 31) == (col & 31)) & (frames_of(col, y, c) < count_ref[0])
    factor = HEAD ** (-0.5)
    for ref in (o_s, dq_s, dk_s, dv_s):
        ref[...] = jnp.zeros_like(ref)
    zero = jnp.zeros((), BF)
    for s in range(2):
        at = slice(256 * s, 256 * s + 256)
        for h in range(4):
            lo = h * HEAD
            start = lo // 128 * 128
            stop = -(-(lo + HEAD) // 128) * 128
            win = slice(start, stop)
            lanes = lax.broadcasted_iota(jnp.int32, (1, stop - start), 1) + start
            inside = (lanes >= lo) & (lanes < lo + HEAD)
            qm = jnp.where(inside, q_s[at, win], zero)
            km = jnp.where(inside, k_s[at, win], zero)
            vm = jnp.where(inside, v_s[at, win], zero)
            gm = jnp.where(inside, h_s[at, win], zero)
            scores = jnp.where(same, dot(qm, km, 1, 1) * factor, -1e30)
            top = jnp.max(scores, axis=-1, keepdims=True)
            expd = jnp.exp(scores - top)
            probs = expd / jnp.sum(expd, axis=-1, keepdims=True)
            probs_b = probs.astype(BF)
            o_s[at, win] += dot(probs_b, vm, 1, 0)
            dprobs = dot(gm, vm, 1, 1)
            dv_s[at, win] += dot(probs_b, gm, 0, 0)
            delta = jnp.sum(probs * dprobs, axis=-1, keepdims=True)
            ds = (probs * (dprobs - delta) * factor).astype(BF)
            dq_s[at, win] += dot(ds, km, 1, 0)
            dk_s[at, win] += dot(ds, qm, 0, 0)

    dkr = pltpu.roll(dk_s[...], 32, 1)
    dvr = pltpu.roll(dv_s[...], 64, 1)
    rows_ref[:, 0:256] = dq_s[:, 0:256].astype(BF)
    rows_ref[:, 256:384] = (dq_s[:, 256:384] + dkr[:, 0:128]).astype(BF)
    rows_ref[:, 384:512] = dkr[:, 128:256].astype(BF)
    rows_ref[:, 512:640] = (dkr[:, 256:384] + dvr[:, 0:128]).astype(BF)
    rows_ref[:, 640:896] = dvr[:, 128:384].astype(BF)

    hmf = dot(o_s[...].astype(BF), pick, 1, 0)
    gp[...] = dot(hmf.astype(BF), g_lo, 0, 0)
    for u in range(3):
        h_u = jnp.where(tail_lane, pltpu.roll(hmf, 18 - 6 * u, 1), 0.0).astype(BF)
        gp[:, 256 * u : 256 * u + 256] += dot(h_u, g_hi, 0, 0)
    rows = rows_ref[...]
    stores = []
    for j in range(4):
        gf[...] = dot(modp[:, 384 * j : 384 * j + 384], rows, 0, 0)
        for p in range(4):
            n = 4 * j + p
            gf[PAIR * p + 64 : PAIR * p + 96, :] += gp[32 * n : 32 * n + 32, :]
        g[384 * j : 384 * j + 384, :] = gf[...].astype(BF)
        copy = pltpu.make_async_copy(g.at[pl.ds(j * RING, RING), :], g_out[j], out_sem.at[j])
        copy.start()
        stores.append(copy)
    for copy in stores:
        copy.wait()


def compute(count, table, modp, gated, w):
    wide = pltpu.VMEM((TOK, WIDE), F32)
    wide_b = pltpu.VMEM((TOK, WIDE), BF)
    outs = pl.pallas_call(
        main_kernel,
        in_specs=specs("svvv" + "a" * 4),
        out_specs=specs("v" + "a" * 4),
        out_shape=[jax.ShapeDtypeStruct((TOK, LANES), BF)]
        + [jax.ShapeDtypeStruct((RING, LANES), BF)] * 4,
        scratch_shapes=[
            pltpu.VMEM((ROWS, LANES), BF),
            pltpu.VMEM((ROWS, LANES), BF),
            pltpu.VMEM((384, LANES), F32),
            pltpu.VMEM((PROJ, LANES), F32),
            wide_b,
            wide_b,
            wide_b,
            wide_b,
            wide,
            wide,
            wide,
            wide,
            pltpu.SemaphoreType.DMA((4,)),
            pltpu.SemaphoreType.DMA((4,)),
        ],
        compiler_params=pltpu.CompilerParams(vmem_limit_bytes=VMEM_LIMIT),
        cost_estimate=pl.CostEstimate(
            flops=7_000_000_000, bytes_accessed=9_000_000, transcendentals=600_000
        ),
        name="block",
    )(count, table, modp, gated, *w)
    return outs[0], outs[1:]


def back_kernel(tab_ref, rows, *refs):
    w = refs[0:4]
    own_ref, other_ref, wbuf, perm, sem = refs[4:]
    loads = load_weights(w, wbuf, sem)
    fill_perm(tab_ref[...], perm)
    for copy in loads:
        copy.wait()
    packed = dot(rows[...], wbuf[...], 1, 1).astype(BF)
    part = dot(packed, perm[...], 1, 1).astype(BF)
    for s in range(2):
        own_ref[128 * s : 128 * s + 128, :] = part[256 * s : 256 * s + 128, :]
        other_ref[128 * s : 128 * s + 128, :] = part[256 * s + 128 : 256 * s + 256, :]


def back(table, rows, w):
    return pl.pallas_call(
        back_kernel,
        in_specs=specs("vv" + "a" * 4),
        out_specs=specs("vv"),
        out_shape=[jax.ShapeDtypeStruct((256, D), BF)] * 2,
        scratch_shapes=[
            pltpu.VMEM((ROWS, LANES), BF),
            pltpu.VMEM((D, ROWS), BF),
            pltpu.SemaphoreType.DMA((4,)),
        ],
        compiler_params=pltpu.CompilerParams(vmem_limit_bytes=VMEM_LIMIT),
        cost_estimate=pl.CostEstimate(
            flops=3_400_000_000, bytes_accessed=6_000_000, transcendentals=0
        ),
        name="back",
    )(table, rows, *w)


def final_kernel(mods_ref, own_ref, other_ref, *refs):
    td, gt = refs[0:4], refs[4:]
    normed, rstd = normalize(gather_rows(td, 0))
    grad_modded = (own_ref[...].astype(F32) + other_ref[...].astype(F32)).astype(BF).astype(F32)
    dn = grad_modded * (1.0 + mods_ref[1:2, :])
    mean_dn = jnp.mean(dn, axis=-1, keepdims=True)
    mean_dnn = jnp.mean(dn * normed, axis=-1, keepdims=True)
    grad_x = (gather_rows(td, 64) + rstd * (dn - mean_dn - normed * mean_dnn)).astype(BF)
    for s in range(2):
        for k in range(4):
            gt[k][32 * s : 32 * s + 32, :] = grad_x[128 * s + 32 * k : 128 * s + 32 * k + 32, :]


def finish(mods, own, other, td):
    return pl.pallas_call(
        final_kernel,
        out_shape=[jax.ShapeDtypeStruct((64, D), BF)] * 4,
        compiler_params=pltpu.CompilerParams(vmem_limit_bytes=VMEM_LIMIT),
        name="finish",
    )(mods, own, other, *td)


def fold_kernel(*refs):
    parts, (keep, first, second, buf) = refs[:4], refs[4:]
    role = role_of()
    total = parts[0][...].astype(F32)
    for part in parts[1:]:
        total = total + part[...].astype(F32)
    near, far = total[0:36, :], total[36:72, :]
    buf[36:40, :] = jnp.zeros((4, LANES), F32)
    buf[40:64, :] = total[72:96, :]
    buf[0:36, :] = far
    second[...] = buf[...].astype(BF)
    buf[0:36, :] = jnp.where(role == 0, far, near)
    first[...] = buf[...].astype(BF)
    buf[0:36, :] = near
    keep[...] = jnp.where(role == 0, buf[...], 0.0).astype(BF)


def fold(parts):
    return pl.pallas_call(
        fold_kernel,
        out_shape=[jax.ShapeDtypeStruct((MSG, LANES), BF)] * 3,
        scratch_shapes=[pltpu.VMEM((MSG, LANES), F32)],
        name="fold",
    )(*parts)


def unpack_kernel(own_ref, other_ref, gq_ref, gp_ref):
    _, _, z, _ = position()
    role = role_of()
    own, other = own_ref[...], other_ref[...]
    first = jnp.where(role == 0, own, other)[0:36, :]
    second = jnp.where(role == 0, other, own)[0:36, :]
    cols = []
    for b in range(3):
        cols += [first[:, b * OWN : b * OWN + OWN], second[:, b * OWN : b * OWN + OWN]]
    gq_ref[...] = jnp.concatenate(cols, axis=1)
    proj = jnp.where((z >> 2) == role, own, other)
    gp_ref[:, 0:LANES] = proj[40:58, :]
    for u in range(3):
        gp_ref[6 * u : 6 * u + 6, LANES:D] = proj[58:64, 256 * u : 256 * u + 256]


def unpack(own, other):
    return pl.pallas_call(
        unpack_kernel,
        out_shape=[jax.ShapeDtypeStruct((36, QKV), F32), jax.ShapeDtypeStruct((18, D), F32)],
        name="unpack_grads",
    )(own, other)


def add(*parts):
    total = parts[0].astype(F32)
    for part in parts[1:]:
        total = total + part.astype(F32)
    return total.astype(BF)


def local(tokens, grad_out, modulation, frame_counts, w_qkv, w_proj):
    both = ("grp", "seq")
    barrier = lax.optimization_barrier
    mods = modulation[0]
    table = jnp.asarray(row_table(PAIR))
    td, mine = pack(tokens[0, 0], grad_out[0, 0], w_qkv, w_proj)
    first = lax.ppermute(mine, both, first_moves(-1))
    second = lax.ppermute(mine, both, second_moves(-1))
    td_in = [lax.ppermute(td[k], "seq", along_y(k)) for k in ORDER]
    first, second, *own_td = barrier([first, second, td[0], td_in[0], td_in[2], td_in[1]])
    other_td = [lax.ppermute(t, "seq", CORE_SWAP) for t in own_td]
    pair, *other_td = barrier([make_pair(mine, first, second)] + other_td)
    pairs = barrier([lax.ppermute(pair, both, pair_moves(i, -1)) for i in (1, 2, 3)])
    w0 = jnp.concatenate([pair] + pairs, axis=0)
    w = [w0] + [lax.ppermute(w0, both, ring_moves(-k)) for k in (1, 2, 3)]
    modp, gated = prepare(frame_counts, table, mods, own_td + other_td)
    *w, modp, gated = barrier(w + [modp, gated])

    rows, grads = compute(frame_counts, jnp.asarray(row_table(32)), modp, gated, w)

    ring_in = [lax.ppermute(grads[k], both, ring_moves(k)) for k in (2, 1, 3)]
    own_part, other_part = back(table, rows, w)
    *ring_in, own_part, other_part = barrier(ring_in + [own_part, other_part])
    other_in = lax.ppermute(other_part, "seq", CORE_SWAP)
    sums = [add(*[t[PAIR * b : PAIR * b + PAIR] for t in [grads[0]] + ring_in]) for b in range(4)]
    z_in = [lax.ppermute(sums[i], both, pair_moves(i, 1)) for i in (1, 2, 3)]
    gt = finish(mods, own_part, other_in, own_td)
    *z_in, g0, g1, g2, g3 = barrier(z_in + list(gt))
    keep, first, second = fold([sums[0], *z_in])
    first = lax.ppermute(first, both, first_moves(1))
    second = lax.ppermute(second, both, second_moves(1))
    g_in = [lax.ppermute(g, "seq", along_y(-k)) for k, g in ((1, g1), (2, g2), (3, g3))]
    block = add(keep, first, second)
    r_in = [lax.ppermute(block, both, over_y(k)) for k in ORDER]
    r1, r3, r2, grad_x = barrier(r_in + [join_tokens([g0] + g_in)])
    total = (block.astype(F32) + r2.astype(F32)) + (r1.astype(F32) + r3.astype(F32))
    grad_qkv, grad_proj = unpack(total, lax.ppermute(total, "seq", CORE_SWAP))
    return (grad_x[None, None], grad_qkv, grad_proj)


def solution(mesh):
    in_specs = (
        P("grp", "seq", None, None),
        P("grp", "seq", None, None),
        P("grp", None, None),
        P("grp"),
        P("grp", None),
        P("grp", None),
    )
    out_specs = (P("grp", "seq", None, None), P("grp", None), P("grp", None))
    return jax.shard_map(local, mesh=mesh, in_specs=in_specs, out_specs=out_specs, check_vma=False)
```

```python
import jax
import jax.numpy as jnp
import numpy as np
from jax import lax
from jax.experimental import pallas as pl
from jax.experimental.pallas import tpu as pltpu
from jax.sharding import PartitionSpec as P

BF = jnp.bfloat16
F32 = jnp.float32
HEAD = 72
D = 1152
INNER = 576
QKV = 1728
OWN = 288
LANES = 896
NX, NY, NZ = 4, 4, 8
MSG = 64
PAIR = 96
RING = 4 * PAIR
ROWS = 4 * RING
PROJ = 512
KZ = ((0, 1, 7, 2), (0, 7, 1, 6))
ORDER = (1, 3, 2)
TOK = 512
WIDE = 384
VMEM_LIMIT = 40 * 1024 * 1024


def gid(z, x):
    return (z % NZ) * NX + x % NX


def sid(y, c):
    return (y % NY) * 2 + c % 2


CORE_SWAP = [(s, s ^ 1) for s in range(8)]


def along_y(dy):
    return [(sid(y, c), sid(y + dy, c)) for y in range(NY) for c in range(2)]


def moves(target):
    pairs = []
    for z in range(NZ):
        for x in range(NX):
            for y in range(NY):
                for c in range(2):
                    role = (c + x + y) % 2
                    to = target(x, y, z, role)
                    if to is not None:
                        u, v, w = to
                        home = gid(w, u) * 8 + sid(v, role + u + v)
                        pairs.append((gid(z, x) * 8 + sid(y, c), home))
    return pairs


def ring_moves(k):
    return moves(lambda x, y, z, role: (x, y + k, z) if role else (x + k, y, z))


def pair_moves(i, sign):
    return moves(lambda x, y, z, role: (x, y, z + sign * KZ[role][i]))


def first_moves(sign):
    return moves(lambda x, y, z, role: (x + sign * y, y, z) if role else (x, y, z + 4))


def second_moves(sign):
    return moves(lambda x, y, z, role: (x + sign * y, y, z + 4) if role else None)


def over_y(k):
    return moves(lambda x, y, z, role: (x, y + k, z))


def row_table(per_pair):
    n = np.arange(16 * per_pair)
    pair, r = n // per_pair, n % per_pair + PAIR - per_pair
    zero = np.zeros_like(n)
    kz0, kz1 = np.array(KZ)[:, pair % 4]
    return np.stack([pair // 4, kz0, kz1, r, zero, zero, zero, zero]).astype(np.int32)


def position():
    g = lax.axis_index("grp")
    s = lax.axis_index("seq")
    return g & 3, s >> 1, g >> 2, s & 1


def role_of():
    x, y, _, c = position()
    return (c + x + y) & 1


def dot(a, b, ca, cb):
    return lax.dot_general(a, b, (((ca,), (cb,)), ((), ())), preferred_element_type=F32)


def places(tab):
    x, y, z, _ = position()
    role = role_of()
    xs = (x + role * y + tab[0:1, :]) & 3
    kz = jnp.where(role == 0, tab[1:2, :], tab[2:3, :])
    return xs, (z + kz) & 7, tab[3:4, :]


def fill_perm(tab, perm):
    xs, a, r = places(tab)
    first = (a * 4 + xs) * 36 + r
    second = (((a + 4) & 7) * 4 + xs) * 36 + r - 36
    natural = jnp.where(r < 36, first, jnp.where(r < 72, second, -1))
    for i in range(0, D, 128):
        ids = lax.broadcasted_iota(jnp.int32, (128, ROWS), 0) + i
        perm[i : i + 128, :] = jnp.where(ids == natural, 1.0, 0.0).astype(BF)


def pack_kernel(tok_ref, dy_ref, wq_ref, wp_ref, *refs):
    outs, out_ref, buf = refs[0:4], refs[4], refs[5]
    wq = wq_ref[...].astype(F32)
    pad = jnp.zeros((36, LANES - 3 * OWN), F32)

    def part(core):
        cols = [wq[:, b * INNER + core * OWN : b * INNER + core * OWN + OWN] for b in range(3)]
        return jnp.concatenate(cols + [pad], axis=1)

    buf[...] = jnp.zeros_like(buf)
    buf[0:36, :] = jnp.where(role_of() == 0, part(0), part(1))
    wp = wp_ref[...].astype(F32)
    buf[40:58, :] = wp[:, 0:LANES]
    for u in range(3):
        buf[58:64, 256 * u : 256 * u + 256] = wp[6 * u : 6 * u + 6, LANES:D]
    out_ref[...] = buf[...].astype(BF)
    _, y, _, _ = position()
    for k in range(4):
        off = pl.multiple_of(((y + k) & 3) * 64, 64)
        outs[k][0:64, :] = tok_ref[pl.ds(off, 64), :]
        outs[k][64:128, :] = dy_ref[pl.ds(off, 64), :]


def pack(x, dy, w_qkv, w_proj):
    outs = pl.pallas_call(
        pack_kernel,
        out_shape=[jax.ShapeDtypeStruct((128, D), BF)] * 4
        + [jax.ShapeDtypeStruct((MSG, LANES), BF)],
        scratch_shapes=[pltpu.VMEM((MSG, LANES), F32)],
        name="pack",
    )(x, dy, w_qkv, w_proj)
    return outs[0:4], outs[4]


def pair_kernel(mine_ref, first_ref, second_ref, out_ref, buf):
    _, _, z, _ = position()
    role = role_of()
    first = first_ref[...].astype(F32)
    near = jnp.where(role == 0, mine_ref[...].astype(F32), first)
    far = jnp.where(role == 0, first, second_ref[...].astype(F32))
    buf[0:36, :] = near[0:36, :]
    buf[36:72, :] = far[0:36, :]
    buf[72:96, :] = jnp.where((z >> 2) == role, near[40:64, :], far[40:64, :])
    out_ref[...] = buf[...].astype(BF)


def make_pair(mine, first, second):
    return pl.pallas_call(
        pair_kernel,
        out_shape=jax.ShapeDtypeStruct((PAIR, LANES), BF),
        scratch_shapes=[pltpu.VMEM((PAIR, LANES), F32)],
        name="pair_weights",
    )(mine, first, second)


def join_kernel(g0, g1, g2, g3, out_ref):
    _, y, _, _ = position()
    for k, g in enumerate((g0, g1, g2, g3)):
        out_ref[pl.ds(pl.multiple_of(((y + k) & 3) * 64, 64), 64), :] = g[...]


def join_tokens(parts):
    return pl.pallas_call(
        join_kernel,
        out_shape=jax.ShapeDtypeStruct((256, D), BF),
        name="join_tokens",
    )(*parts)


def normalize(xf):
    mean = jnp.mean(xf, axis=-1, keepdims=True)
    cent = xf - mean
    rstd = lax.rsqrt(jnp.mean(cent * cent, axis=-1, keepdims=True) + 1e-06)
    return cent * rstd, rstd


def gather_rows(parts, base):
    return jnp.concatenate(
        [p[base + 32 * s : base + 32 * s + 32, :].astype(F32) for s in range(2) for p in parts], axis=0
    )


def frames_of(index, y, c):
    return (((y - (index >> 5)) & 3) * 2) + (c ^ ((index >> 7) & 1))


def prepare_kernel(count_ref, tab_ref, mods_ref, *refs):
    td, (modp_ref, gated_ref, perm) = refs[0:8], refs[8:]
    _, y, _, c = position()
    fill_perm(tab_ref[...], perm)
    normed, _ = normalize(gather_rows(td, 0))
    modded = (normed * (1.0 + mods_ref[1:2, :]) + mods_ref[0:1, :]).astype(BF)
    modp_ref[...] = dot(modded, perm[...], 1, 0).astype(BF)
    index = lax.broadcasted_iota(jnp.int32, (TOK, 1), 0)
    live = jnp.where(frames_of(index, y, c) < count_ref[0], 1.0, 0.0)
    gated_ref[...] = (mods_ref[2:3, :] * live * gather_rows(td, 64)).astype(BF)


def specs(kinds):
    of = {"s": pltpu.SMEM, "v": pltpu.VMEM, "a": pl.ANY}
    return [pl.BlockSpec(memory_space=of[k]) for k in kinds]


def prepare(count, table, mods, td):
    return pl.pallas_call(
        prepare_kernel,
        in_specs=specs("s" + "v" * 10),
        out_specs=specs("vv"),
        out_shape=[jax.ShapeDtypeStruct((TOK, ROWS), BF), jax.ShapeDtypeStruct((TOK, D), BF)],
        scratch_shapes=[pltpu.VMEM((D, ROWS), BF)],
        compiler_params=pltpu.CompilerParams(vmem_limit_bytes=VMEM_LIMIT),
        cost_estimate=pl.CostEstimate(
            flops=2_000_000_000, bytes_accessed=6_000_000, transcendentals=512
        ),
        name="prepare",
    )(count, table, mods, *td)


def load_weights(w, wbuf, sem):
    loads = []
    for i in range(4):
        copy = pltpu.make_async_copy(w[i], wbuf.at[pl.ds(i * RING, RING), :], sem.at[i])
        copy.start()
        loads.append(copy)
    return loads


def main_kernel(count_ref, tab_ref, modp, gated, *refs):
    w = refs[0:4]
    rows_ref = refs[4]
    g_out = refs[5:9]
    wbuf, g, gf, gp, q_s, k_s, v_s, h_s, o_s, dq_s, dk_s, dv_s, in_sem, out_sem = refs[9:]
    _, y, _, c = position()
    loads = load_weights(w, wbuf, in_sem)

    xs, a, r = places(tab_ref[...])
    inner = jnp.where((r >= 72) & (r < 90), ((a & 3) * 4 + xs) * 18 + r - 72, -1)
    pick = jnp.where(
        lax.broadcasted_iota(jnp.int32, (WIDE, PROJ), 0) == inner, 1.0, 0.0
    ).astype(BF)
    main_lane = (r >= 72) & (r < 90)
    tail_lane = r >= 90

    for copy in loads:
        copy.wait()

    lane = lax.broadcasted_iota(jnp.int32, (1, WIDE), 1)
    own_lane = lane < OWN
    qkv = dot(modp[...], wbuf[...], 1, 0)
    q_s[...] = jnp.where(own_lane, qkv[:, 0:384], 0.0).astype(BF)
    k_s[...] = jnp.where(own_lane, pltpu.roll(qkv[:, 256:640], WIDE - 32, 1), 0.0).astype(BF)
    v_s[...] = jnp.where(own_lane, pltpu.roll(qkv[:, 512:896], WIDE - 64, 1), 0.0).astype(BF)

    wp = jnp.concatenate([wbuf[PAIR * p + 64 : PAIR * p + 96, :] for p in range(16)], axis=0)
    g_lo = gated[:, 0:LANES]
    g_hi = gated[:, LANES:D]
    ghp = jnp.where(main_lane, dot(g_lo, wp, 1, 1), 0.0)
    for u in range(3):
        tail = dot(g_hi, wp[:, 256 * u : 256 * u + 256], 1, 1)
        ghp += pltpu.roll(jnp.where(tail_lane, tail, 0.0), PROJ + 6 * u - 18, 1)
    h_s[...] = dot(ghp.astype(BF), pick, 1, 1).astype(BF)

    row = lax.broadcasted_iota(jnp.int32, (256, 1), 0)
    col = lax.broadcasted_iota(jnp.int32, (1, 256), 1)
    same = ((row & 31) == (col & 31)) & (frames_of(col, y, c) < count_ref[0])
    factor = HEAD ** (-0.5)
    for ref in (o_s, dq_s, dk_s, dv_s):
        ref[...] = jnp.zeros_like(ref)
    zero = jnp.zeros((), BF)
    for s in range(2):
        at = slice(256 * s, 256 * s + 256)
        for h in range(4):
            lo = h * HEAD
            start = lo // 128 * 128
            stop = -(-(lo + HEAD) // 128) * 128
            win = slice(start, stop)
            lanes = lax.broadcasted_iota(jnp.int32, (1, stop - start), 1) + start
            inside = (lanes >= lo) & (lanes < lo + HEAD)
            qm = jnp.where(inside, q_s[at, win], zero)
            km = jnp.where(inside, k_s[at, win], zero)
            vm = jnp.where(inside, v_s[at, win], zero)
            gm = jnp.where(inside, h_s[at, win], zero)
            scores = jnp.where(same, dot(qm, km, 1, 1) * factor, -1e30)
            top = jnp.max(scores, axis=-1, keepdims=True)
            expd = jnp.exp(scores - top)
            probs = expd / jnp.sum(expd, axis=-1, keepdims=True)
            probs_b = probs.astype(BF)
            o_s[at, win] += dot(probs_b, vm, 1, 0)
            dprobs = dot(gm, vm, 1, 1)
            dv_s[at, win] += dot(probs_b, gm, 0, 0)
            delta = jnp.sum(probs * dprobs, axis=-1, keepdims=True)
            ds = (probs * (dprobs - delta) * factor).astype(BF)
            dq_s[at, win] += dot(ds, km, 1, 0)
            dk_s[at, win] += dot(ds, qm, 0, 0)

    dkr = pltpu.roll(dk_s[...], 32, 1)
    dvr = pltpu.roll(dv_s[...], 64, 1)
    rows_ref[:, 0:256] = dq_s[:, 0:256].astype(BF)
    rows_ref[:, 256:384] = (dq_s[:, 256:384] + dkr[:, 0:128]).astype(BF)
    rows_ref[:, 384:512] = dkr[:, 128:256].astype(BF)
    rows_ref[:, 512:640] = (dkr[:, 256:384] + dvr[:, 0:128]).astype(BF)
    rows_ref[:, 640:896] = dvr[:, 128:384].astype(BF)

    hmf = dot(o_s[...].astype(BF), pick, 1, 0)
    gp[...] = dot(hmf.astype(BF), g_lo, 0, 0)
    for u in range(3):
        h_u = jnp.where(tail_lane, pltpu.roll(hmf, 18 - 6 * u, 1), 0.0).astype(BF)
        gp[:, 256 * u : 256 * u + 256] += dot(h_u, g_hi, 0, 0)
    rows = rows_ref[...]
    stores = []
    for j in range(4):
        gf[...] = dot(modp[:, 384 * j : 384 * j + 384], rows, 0, 0)
        for p in range(4):
            n = 4 * j + p
            gf[PAIR * p + 64 : PAIR * p + 96, :] += gp[32 * n : 32 * n + 32, :]
        g[384 * j : 384 * j + 384, :] = gf[...].astype(BF)
        copy = pltpu.make_async_copy(g.at[pl.ds(j * RING, RING), :], g_out[j], out_sem.at[j])
        copy.start()
        stores.append(copy)
    for copy in stores:
        copy.wait()


def compute(count, table, modp, gated, w):
    wide = pltpu.VMEM((TOK, WIDE), F32)
    wide_b = pltpu.VMEM((TOK, WIDE), BF)
    outs = pl.pallas_call(
        main_kernel,
        in_specs=specs("svvv" + "a" * 4),
        out_specs=specs("v" + "a" * 4),
        out_shape=[jax.ShapeDtypeStruct((TOK, LANES), BF)]
        + [jax.ShapeDtypeStruct((RING, LANES), BF)] * 4,
        scratch_shapes=[
            pltpu.VMEM((ROWS, LANES), BF),
            pltpu.VMEM((ROWS, LANES), BF),
            pltpu.VMEM((384, LANES), F32),
            pltpu.VMEM((PROJ, LANES), F32),
            wide_b,
            wide_b,
            wide_b,
            wide_b,
            wide,
            wide,
            wide,
            wide,
            pltpu.SemaphoreType.DMA((4,)),
            pltpu.SemaphoreType.DMA((4,)),
        ],
        compiler_params=pltpu.CompilerParams(vmem_limit_bytes=VMEM_LIMIT),
        cost_estimate=pl.CostEstimate(
            flops=7_000_000_000, bytes_accessed=9_000_000, transcendentals=600_000
        ),
        name="block",
    )(count, table, modp, gated, *w)
    return outs[0], outs[1:]


def back_kernel(tab_ref, rows, *refs):
    w = refs[0:4]
    own_ref, other_ref, wbuf, perm, sem = refs[4:]
    loads = load_weights(w, wbuf, sem)
    fill_perm(tab_ref[...], perm)
    for copy in loads:
        copy.wait()
    packed = dot(rows[...], wbuf[...], 1, 1).astype(BF)
    part = dot(packed, perm[...], 1, 1).astype(BF)
    for s in range(2):
        own_ref[128 * s : 128 * s + 128, :] = part[256 * s : 256 * s + 128, :]
        other_ref[128 * s : 128 * s + 128, :] = part[256 * s + 128 : 256 * s + 256, :]


def back(table, rows, w):
    return pl.pallas_call(
        back_kernel,
        in_specs=specs("vv" + "a" * 4),
        out_specs=specs("vv"),
        out_shape=[jax.ShapeDtypeStruct((256, D), BF)] * 2,
        scratch_shapes=[
            pltpu.VMEM((ROWS, LANES), BF),
            pltpu.VMEM((D, ROWS), BF),
            pltpu.SemaphoreType.DMA((4,)),
        ],
        compiler_params=pltpu.CompilerParams(vmem_limit_bytes=VMEM_LIMIT),
        cost_estimate=pl.CostEstimate(
            flops=3_400_000_000, bytes_accessed=6_000_000, transcendentals=0
        ),
        name="back",
    )(table, rows, *w)


def final_kernel(mods_ref, own_ref, other_ref, *refs):
    td, gt = refs[0:4], refs[4:]
    normed, rstd = normalize(gather_rows(td, 0))
    grad_modded = (own_ref[...].astype(F32) + other_ref[...].astype(F32)).astype(BF).astype(F32)
    dn = grad_modded * (1.0 + mods_ref[1:2, :])
    mean_dn = jnp.mean(dn, axis=-1, keepdims=True)
    mean_dnn = jnp.mean(dn * normed, axis=-1, keepdims=True)
    grad_x = (gather_rows(td, 64) + rstd * (dn - mean_dn - normed * mean_dnn)).astype(BF)
    for s in range(2):
        for k in range(4):
            gt[k][32 * s : 32 * s + 32, :] = grad_x[128 * s + 32 * k : 128 * s + 32 * k + 32, :]


def finish(mods, own, other, td):
    return pl.pallas_call(
        final_kernel,
        out_shape=[jax.ShapeDtypeStruct((64, D), BF)] * 4,
        compiler_params=pltpu.CompilerParams(vmem_limit_bytes=VMEM_LIMIT),
        name="finish",
    )(mods, own, other, *td)


def fold_kernel(*refs):
    parts, (keep, first, second, buf) = refs[:4], refs[4:]
    role = role_of()
    total = parts[0][...].astype(F32)
    for part in parts[1:]:
        total = total + part[...].astype(F32)
    near, far = total[0:36, :], total[36:72, :]
    buf[36:40, :] = jnp.zeros((4, LANES), F32)
    buf[40:64, :] = total[72:96, :]
    buf[0:36, :] = far
    second[...] = buf[...].astype(BF)
    buf[0:36, :] = jnp.where(role == 0, far, near)
    first[...] = buf[...].astype(BF)
    buf[0:36, :] = near
    keep[...] = jnp.where(role == 0, buf[...], 0.0).astype(BF)


def fold(parts):
    return pl.pallas_call(
        fold_kernel,
        out_shape=[jax.ShapeDtypeStruct((MSG, LANES), BF)] * 3,
        scratch_shapes=[pltpu.VMEM((MSG, LANES), F32)],
        name="fold",
    )(*parts)


def unpack_kernel(own_ref, other_ref, gq_ref, gp_ref):
    _, _, z, _ = position()
    role = role_of()
    own, other = own_ref[...], other_ref[...]
    first = jnp.where(role == 0, own, other)[0:36, :]
    second = jnp.where(role == 0, other, own)[0:36, :]
    cols = []
    for b in range(3):
        cols += [first[:, b * OWN : b * OWN + OWN], second[:, b * OWN : b * OWN + OWN]]
    gq_ref[...] = jnp.concatenate(cols, axis=1)
    proj = jnp.where((z >> 2) == role, own, other)
    gp_ref[:, 0:LANES] = proj[40:58, :]
    for u in range(3):
        gp_ref[6 * u : 6 * u + 6, LANES:D] = proj[58:64, 256 * u : 256 * u + 256]


def unpack(own, other):
    return pl.pallas_call(
        unpack_kernel,
        out_shape=[jax.ShapeDtypeStruct((36, QKV), F32), jax.ShapeDtypeStruct((18, D), F32)],
        name="unpack_grads",
    )(own, other)


def add(*parts):
    total = parts[0].astype(F32)
    for part in parts[1:]:
        total = total + part.astype(F32)
    return total.astype(BF)


def local(tokens, grad_out, modulation, frame_counts, w_qkv, w_proj):
    both = ("grp", "seq")
    barrier = lax.optimization_barrier
    mods = modulation[0]
    table = jnp.asarray(row_table(PAIR))
    td, mine = pack(tokens[0, 0], grad_out[0, 0], w_qkv, w_proj)
    first = lax.ppermute(mine, both, first_moves(-1))
    second = lax.ppermute(mine, both, second_moves(-1))
    td_in = [lax.ppermute(td[k], "seq", along_y(k)) for k in ORDER]
    first, second, *own_td = barrier([first, second, td[0], td_in[0], td_in[2], td_in[1]])
    other_td = [lax.ppermute(t, "seq", CORE_SWAP) for t in own_td]
    pair, *other_td = barrier([make_pair(mine, first, second)] + other_td)
    pairs = barrier([lax.ppermute(pair, both, pair_moves(i, -1)) for i in (1, 2, 3)])
    w0 = jnp.concatenate([pair] + pairs, axis=0)
    w3, w1, w2 = [lax.ppermute(w0, both, ring_moves(-k)) for k in (3, 1, 2)]
    modp, gated = prepare(frame_counts, table, mods, own_td + other_td)
    w0, w3, w1, w2, modp, gated = barrier((w0, w3, w1, w2, modp, gated))
    w = [w0, w1, w2, w3]

    rows, grads = compute(frame_counts, jnp.asarray(row_table(32)), modp, gated, w)

    ring_in = [lax.ppermute(grads[k], both, ring_moves(k)) for k in (2, 1, 3)]
    own_part, other_part = back(table, rows, w)
    *ring_in, own_part, other_part = barrier(ring_in + [own_part, other_part])
    other_in = lax.ppermute(other_part, "seq", CORE_SWAP)
    sums = [add(*[t[PAIR * b : PAIR * b + PAIR] for t in [grads[0]] + ring_in]) for b in range(4)]
    z_in = [lax.ppermute(sums[i], both, pair_moves(i, 1)) for i in (1, 2, 3)]
    gt = finish(mods, own_part, other_in, own_td)
    *z_in, g0, g1, g2, g3 = barrier(z_in + list(gt))
    keep, first, second = fold([sums[0], *z_in])
    first = lax.ppermute(first, both, first_moves(1))
    second = lax.ppermute(second, both, second_moves(1))
    g_in = [lax.ppermute(g, "seq", along_y(-k)) for k, g in ((1, g1), (2, g2), (3, g3))]
    block = add(keep, first, second)
    r_in = [lax.ppermute(block, both, over_y(k)) for k in ORDER]
    r1, r3, r2, *g_in = barrier(r_in + g_in)
    total = (block.astype(F32) + r2.astype(F32)) + (r1.astype(F32) + r3.astype(F32))
    other_total = lax.ppermute(total, "seq", CORE_SWAP)
    other_total, grad_x = barrier((other_total, join_tokens([g0] + g_in)))
    grad_qkv, grad_proj = unpack(total, other_total)
    return (grad_x[None, None], grad_qkv, grad_proj)


def solution(mesh):
    in_specs = (
        P("grp", "seq", None, None),
        P("grp", "seq", None, None),
        P("grp", None, None),
        P("grp"),
        P("grp", None),
        P("grp", None),
    )
    out_specs = (P("grp", "seq", None, None), P("grp", None), P("grp", None))
    return jax.shard_map(local, mesh=mesh, in_specs=in_specs, out_specs=out_specs, check_vma=False)
```

```python
import jax
import jax.numpy as jnp
import numpy as np
from jax import lax
from jax.experimental import pallas as pl
from jax.experimental.pallas import tpu as pltpu
from jax.sharding import PartitionSpec as P

BF = jnp.bfloat16
F32 = jnp.float32
HEAD = 72
D = 1152
INNER = 576
QKV = 1728
OWN = 288
LANES = 896
NX, NY, NZ = 4, 4, 8
MSG = 64
PAIR = 96
RING = 4 * PAIR
ROWS = 4 * RING
PROJ = 512
KZ = ((0, 1, 7, 2), (0, 7, 1, 6))
ORDER = (1, 3, 2)
TOK = 512
WIDE = 384
VMEM_LIMIT = 40 * 1024 * 1024


def gid(z, x):
    return (z % NZ) * NX + x % NX


def sid(y, c):
    return (y % NY) * 2 + c % 2


CORE_SWAP = [(s, s ^ 1) for s in range(8)]


def along_y(dy):
    return [(sid(y, c), sid(y + dy, c)) for y in range(NY) for c in range(2)]


def moves(target):
    pairs = []
    for z in range(NZ):
        for x in range(NX):
            for y in range(NY):
                for c in range(2):
                    role = (c + x + y) % 2
                    to = target(x, y, z, role)
                    if to is not None:
                        u, v, w = to
                        home = gid(w, u) * 8 + sid(v, role + u + v)
                        pairs.append((gid(z, x) * 8 + sid(y, c), home))
    return pairs


def ring_moves(k):
    return moves(lambda x, y, z, role: (x, y + k, z) if role else (x + k, y, z))


def pair_moves(i, sign):
    return moves(lambda x, y, z, role: (x, y, z + sign * KZ[role][i]))


def first_moves(sign):
    return moves(lambda x, y, z, role: (x + sign * y, y, z) if role else (x, y, z + 4))


def second_moves(sign):
    return moves(lambda x, y, z, role: (x + sign * y, y, z + 4) if role else None)


def over_y(k):
    return moves(lambda x, y, z, role: (x, y + k, z))


def row_table(per_pair):
    n = np.arange(16 * per_pair)
    pair, r = n // per_pair, n % per_pair + PAIR - per_pair
    zero = np.zeros_like(n)
    kz0, kz1 = np.array(KZ)[:, pair % 4]
    return np.stack([pair // 4, kz0, kz1, r, zero, zero, zero, zero]).astype(np.int32)


def position():
    g = lax.axis_index("grp")
    s = lax.axis_index("seq")
    return g & 3, s >> 1, g >> 2, s & 1


def role_of():
    x, y, _, c = position()
    return (c + x + y) & 1


def dot(a, b, ca, cb):
    return lax.dot_general(a, b, (((ca,), (cb,)), ((), ())), preferred_element_type=F32)


def places(tab):
    x, y, z, _ = position()
    role = role_of()
    xs = (x + role * y + tab[0:1, :]) & 3
    kz = jnp.where(role == 0, tab[1:2, :], tab[2:3, :])
    return xs, (z + kz) & 7, tab[3:4, :]


def fill_perm(tab, perm):
    xs, a, r = places(tab)
    first = (a * 4 + xs) * 36 + r
    second = (((a + 4) & 7) * 4 + xs) * 36 + r - 36
    natural = jnp.where(r < 36, first, jnp.where(r < 72, second, -1))
    for i in range(0, D, 128):
        ids = lax.broadcasted_iota(jnp.int32, (128, ROWS), 0) + i
        perm[i : i + 128, :] = jnp.where(ids == natural, 1.0, 0.0).astype(BF)


def pack_kernel(tok_ref, dy_ref, wq_ref, wp_ref, *refs):
    outs, out_ref, buf = refs[0:4], refs[4], refs[5]
    wq = wq_ref[...].astype(F32)
    pad = jnp.zeros((36, LANES - 3 * OWN), F32)

    def part(core):
        cols = [wq[:, b * INNER + core * OWN : b * INNER + core * OWN + OWN] for b in range(3)]
        return jnp.concatenate(cols + [pad], axis=1)

    buf[...] = jnp.zeros_like(buf)
    buf[0:36, :] = jnp.where(role_of() == 0, part(0), part(1))
    wp = wp_ref[...].astype(F32)
    buf[40:58, :] = wp[:, 0:LANES]
    for u in range(3):
        buf[58:64, 256 * u : 256 * u + 256] = wp[6 * u : 6 * u + 6, LANES:D]
    out_ref[...] = buf[...].astype(BF)
    _, y, _, _ = position()
    for k in range(4):
        off = pl.multiple_of(((y + k) & 3) * 64, 64)
        outs[k][0:64, :] = tok_ref[pl.ds(off, 64), :]
        outs[k][64:128, :] = dy_ref[pl.ds(off, 64), :]


def pack(x, dy, w_qkv, w_proj):
    outs = pl.pallas_call(
        pack_kernel,
        out_shape=[jax.ShapeDtypeStruct((128, D), BF)] * 4
        + [jax.ShapeDtypeStruct((MSG, LANES), BF)],
        scratch_shapes=[pltpu.VMEM((MSG, LANES), F32)],
        name="pack",
    )(x, dy, w_qkv, w_proj)
    return outs[0:4], outs[4]


def pair_kernel(mine_ref, first_ref, second_ref, out_ref, buf):
    _, _, z, _ = position()
    role = role_of()
    first = first_ref[...].astype(F32)
    near = jnp.where(role == 0, mine_ref[...].astype(F32), first)
    far = jnp.where(role == 0, first, second_ref[...].astype(F32))
    buf[0:36, :] = near[0:36, :]
    buf[36:72, :] = far[0:36, :]
    buf[72:96, :] = jnp.where((z >> 2) == role, near[40:64, :], far[40:64, :])
    out_ref[...] = buf[...].astype(BF)


def make_pair(mine, first, second):
    return pl.pallas_call(
        pair_kernel,
        out_shape=jax.ShapeDtypeStruct((PAIR, LANES), BF),
        scratch_shapes=[pltpu.VMEM((PAIR, LANES), F32)],
        name="pair_weights",
    )(mine, first, second)


def join_kernel(g0, g1, g2, g3, out_ref):
    _, y, _, _ = position()
    for k, g in enumerate((g0, g1, g2, g3)):
        out_ref[pl.ds(pl.multiple_of(((y + k) & 3) * 64, 64), 64), :] = g[...]


def join_tokens(parts):
    return pl.pallas_call(
        join_kernel,
        out_shape=jax.ShapeDtypeStruct((256, D), BF),
        name="join_tokens",
    )(*parts)


def normalize(xf):
    mean = jnp.mean(xf, axis=-1, keepdims=True)
    cent = xf - mean
    rstd = lax.rsqrt(jnp.mean(cent * cent, axis=-1, keepdims=True) + 1e-06)
    return cent * rstd, rstd


def gather_rows(parts, base):
    return jnp.concatenate(
        [p[base + 32 * s : base + 32 * s + 32, :].astype(F32) for s in range(2) for p in parts], axis=0
    )


def frames_of(index, y, c):
    return (((y - (index >> 5)) & 3) * 2) + (c ^ ((index >> 7) & 1))


def prepare_kernel(count_ref, tab_ref, mods_ref, *refs):
    two = refs[4]
    td = [*refs[0:4], two.at[pl.ds(0, 128), :], two.at[pl.ds(128, 128), :], *refs[5:7]]
    modp_ref, gated_ref, perm = refs[7:]
    _, y, _, c = position()
    fill_perm(tab_ref[...], perm)
    normed, _ = normalize(gather_rows(td, 0))
    modded = (normed * (1.0 + mods_ref[1:2, :]) + mods_ref[0:1, :]).astype(BF)
    modp_ref[...] = dot(modded, perm[...], 1, 0).astype(BF)
    index = lax.broadcasted_iota(jnp.int32, (TOK, 1), 0)
    live = jnp.where(frames_of(index, y, c) < count_ref[0], 1.0, 0.0)
    gated_ref[...] = (mods_ref[2:3, :] * live * gather_rows(td, 64)).astype(BF)


def specs(kinds):
    of = {"s": pltpu.SMEM, "v": pltpu.VMEM, "a": pl.ANY}
    return [pl.BlockSpec(memory_space=of[k]) for k in kinds]


def prepare(count, table, mods, td):
    return pl.pallas_call(
        prepare_kernel,
        in_specs=specs("s" + "v" * 9),
        out_specs=specs("vv"),
        out_shape=[jax.ShapeDtypeStruct((TOK, ROWS), BF), jax.ShapeDtypeStruct((TOK, D), BF)],
        scratch_shapes=[pltpu.VMEM((D, ROWS), BF)],
        compiler_params=pltpu.CompilerParams(vmem_limit_bytes=VMEM_LIMIT),
        cost_estimate=pl.CostEstimate(
            flops=2_000_000_000, bytes_accessed=6_000_000, transcendentals=512
        ),
        name="prepare",
    )(count, table, mods, *td)


def load_weights(w, wbuf, sem):
    loads = []
    for i in range(4):
        copy = pltpu.make_async_copy(w[i], wbuf.at[pl.ds(i * RING, RING), :], sem.at[i])
        copy.start()
        loads.append(copy)
    return loads


def main_kernel(count_ref, tab_ref, modp, gated, *refs):
    w = refs[0:4]
    rows_ref = refs[4]
    g_out = refs[5:9]
    wbuf, g, gf, gp, q_s, k_s, v_s, h_s, o_s, dq_s, dk_s, dv_s, in_sem, out_sem = refs[9:]
    _, y, _, c = position()
    loads = load_weights(w, wbuf, in_sem)

    xs, a, r = places(tab_ref[...])
    inner = jnp.where((r >= 72) & (r < 90), ((a & 3) * 4 + xs) * 18 + r - 72, -1)
    pick = jnp.where(
        lax.broadcasted_iota(jnp.int32, (WIDE, PROJ), 0) == inner, 1.0, 0.0
    ).astype(BF)
    main_lane = (r >= 72) & (r < 90)
    tail_lane = r >= 90

    for copy in loads:
        copy.wait()

    lane = lax.broadcasted_iota(jnp.int32, (1, WIDE), 1)
    own_lane = lane < OWN
    qkv = dot(modp[...], wbuf[...], 1, 0)
    q_s[...] = jnp.where(own_lane, qkv[:, 0:384], 0.0).astype(BF)
    k_s[...] = jnp.where(own_lane, pltpu.roll(qkv[:, 256:640], WIDE - 32, 1), 0.0).astype(BF)
    v_s[...] = jnp.where(own_lane, pltpu.roll(qkv[:, 512:896], WIDE - 64, 1), 0.0).astype(BF)

    wp = jnp.concatenate([wbuf[PAIR * p + 64 : PAIR * p + 96, :] for p in range(16)], axis=0)
    g_lo = gated[:, 0:LANES]
    g_hi = gated[:, LANES:D]
    ghp = jnp.where(main_lane, dot(g_lo, wp, 1, 1), 0.0)
    for u in range(3):
        tail = dot(g_hi, wp[:, 256 * u : 256 * u + 256], 1, 1)
        ghp += pltpu.roll(jnp.where(tail_lane, tail, 0.0), PROJ + 6 * u - 18, 1)
    h_s[...] = dot(ghp.astype(BF), pick, 1, 1).astype(BF)

    row = lax.broadcasted_iota(jnp.int32, (256, 1), 0)
    col = lax.broadcasted_iota(jnp.int32, (1, 256), 1)
    same = ((row & 31) == (col & 31)) & (frames_of(col, y, c) < count_ref[0])
    factor = HEAD ** (-0.5)
    for ref in (o_s, dq_s, dk_s, dv_s):
        ref[...] = jnp.zeros_like(ref)
    zero = jnp.zeros((), BF)
    for s in range(2):
        at = slice(256 * s, 256 * s + 256)
        for h in range(4):
            lo = h * HEAD
            start = lo // 128 * 128
            stop = -(-(lo + HEAD) // 128) * 128
            win = slice(start, stop)
            lanes = lax.broadcasted_iota(jnp.int32, (1, stop - start), 1) + start
            inside = (lanes >= lo) & (lanes < lo + HEAD)
            qm = jnp.where(inside, q_s[at, win], zero)
            km = jnp.where(inside, k_s[at, win], zero)
            vm = jnp.where(inside, v_s[at, win], zero)
            gm = jnp.where(inside, h_s[at, win], zero)
            scores = jnp.where(same, dot(qm, km, 1, 1) * factor, -1e30)
            top = jnp.max(scores, axis=-1, keepdims=True)
            expd = jnp.exp(scores - top)
            probs = expd / jnp.sum(expd, axis=-1, keepdims=True)
            probs_b = probs.astype(BF)
            o_s[at, win] += dot(probs_b, vm, 1, 0)
            dprobs = dot(gm, vm, 1, 1)
            dv_s[at, win] += dot(probs_b, gm, 0, 0)
            delta = jnp.sum(probs * dprobs, axis=-1, keepdims=True)
            ds = (probs * (dprobs - delta) * factor).astype(BF)
            dq_s[at, win] += dot(ds, km, 1, 0)
            dk_s[at, win] += dot(ds, qm, 0, 0)

    dkr = pltpu.roll(dk_s[...], 32, 1)
    dvr = pltpu.roll(dv_s[...], 64, 1)
    rows_ref[:, 0:256] = dq_s[:, 0:256].astype(BF)
    rows_ref[:, 256:384] = (dq_s[:, 256:384] + dkr[:, 0:128]).astype(BF)
    rows_ref[:, 384:512] = dkr[:, 128:256].astype(BF)
    rows_ref[:, 512:640] = (dkr[:, 256:384] + dvr[:, 0:128]).astype(BF)
    rows_ref[:, 640:896] = dvr[:, 128:384].astype(BF)

    hmf = dot(o_s[...].astype(BF), pick, 1, 0)
    gp[...] = dot(hmf.astype(BF), g_lo, 0, 0)
    for u in range(3):
        h_u = jnp.where(tail_lane, pltpu.roll(hmf, 18 - 6 * u, 1), 0.0).astype(BF)
        gp[:, 256 * u : 256 * u + 256] += dot(h_u, g_hi, 0, 0)
    rows = rows_ref[...]
    stores = []
    for j in range(4):
        gf[...] = dot(modp[:, 384 * j : 384 * j + 384], rows, 0, 0)
        for p in range(4):
            n = 4 * j + p
            gf[PAIR * p + 64 : PAIR * p + 96, :] += gp[32 * n : 32 * n + 32, :]
        g[384 * j : 384 * j + 384, :] = gf[...].astype(BF)
        copy = pltpu.make_async_copy(g.at[pl.ds(j * RING, RING), :], g_out[j], out_sem.at[j])
        copy.start()
        stores.append(copy)
    for copy in stores:
        copy.wait()


def compute(count, table, modp, gated, w):
    wide = pltpu.VMEM((TOK, WIDE), F32)
    wide_b = pltpu.VMEM((TOK, WIDE), BF)
    outs = pl.pallas_call(
        main_kernel,
        in_specs=specs("svvv" + "a" * 4),
        out_specs=specs("v" + "a" * 4),
        out_shape=[jax.ShapeDtypeStruct((TOK, LANES), BF)]
        + [jax.ShapeDtypeStruct((RING, LANES), BF)] * 4,
        scratch_shapes=[
            pltpu.VMEM((ROWS, LANES), BF),
            pltpu.VMEM((ROWS, LANES), BF),
            pltpu.VMEM((384, LANES), F32),
            pltpu.VMEM((PROJ, LANES), F32),
            wide_b,
            wide_b,
            wide_b,
            wide_b,
            wide,
            wide,
            wide,
            wide,
            pltpu.SemaphoreType.DMA((4,)),
            pltpu.SemaphoreType.DMA((4,)),
        ],
        compiler_params=pltpu.CompilerParams(vmem_limit_bytes=VMEM_LIMIT),
        cost_estimate=pl.CostEstimate(
            flops=7_000_000_000, bytes_accessed=9_000_000, transcendentals=600_000
        ),
        name="block",
    )(count, table, modp, gated, *w)
    return outs[0], outs[1:]


def back_kernel(tab_ref, rows, *refs):
    w = refs[0:4]
    own_ref, other_ref, wbuf, perm, sem = refs[4:]
    loads = load_weights(w, wbuf, sem)
    fill_perm(tab_ref[...], perm)
    for copy in loads:
        copy.wait()
    packed = dot(rows[...], wbuf[...], 1, 1).astype(BF)
    part = dot(packed, perm[...], 1, 1).astype(BF)
    for s in range(2):
        own_ref[128 * s : 128 * s + 128, :] = part[256 * s : 256 * s + 128, :]
        other_ref[128 * s : 128 * s + 128, :] = part[256 * s + 128 : 256 * s + 256, :]


def back(table, rows, w):
    return pl.pallas_call(
        back_kernel,
        in_specs=specs("vv" + "a" * 4),
        out_specs=specs("vv"),
        out_shape=[jax.ShapeDtypeStruct((256, D), BF)] * 2,
        scratch_shapes=[
            pltpu.VMEM((ROWS, LANES), BF),
            pltpu.VMEM((D, ROWS), BF),
            pltpu.SemaphoreType.DMA((4,)),
        ],
        compiler_params=pltpu.CompilerParams(vmem_limit_bytes=VMEM_LIMIT),
        cost_estimate=pl.CostEstimate(
            flops=3_400_000_000, bytes_accessed=6_000_000, transcendentals=0
        ),
        name="back",
    )(table, rows, *w)


def final_kernel(mods_ref, own_ref, other_ref, *refs):
    td, gt = refs[0:4], refs[4:]
    normed, rstd = normalize(gather_rows(td, 0))
    grad_modded = (own_ref[...].astype(F32) + other_ref[...].astype(F32)).astype(BF).astype(F32)
    dn = grad_modded * (1.0 + mods_ref[1:2, :])
    mean_dn = jnp.mean(dn, axis=-1, keepdims=True)
    mean_dnn = jnp.mean(dn * normed, axis=-1, keepdims=True)
    grad_x = (gather_rows(td, 64) + rstd * (dn - mean_dn - normed * mean_dnn)).astype(BF)
    for s in range(2):
        for k in range(4):
            gt[k][32 * s : 32 * s + 32, :] = grad_x[128 * s + 32 * k : 128 * s + 32 * k + 32, :]


def finish(mods, own, other, td):
    return pl.pallas_call(
        final_kernel,
        out_shape=[jax.ShapeDtypeStruct((64, D), BF)] * 4,
        compiler_params=pltpu.CompilerParams(vmem_limit_bytes=VMEM_LIMIT),
        name="finish",
    )(mods, own, other, *td)


def fold_kernel(*refs):
    parts, (keep, first, second, buf) = refs[:4], refs[4:]
    role = role_of()
    total = parts[0][...].astype(F32)
    for part in parts[1:]:
        total = total + part[...].astype(F32)
    near, far = total[0:36, :], total[36:72, :]
    buf[36:40, :] = jnp.zeros((4, LANES), F32)
    buf[40:64, :] = total[72:96, :]
    buf[0:36, :] = far
    second[...] = buf[...].astype(BF)
    buf[0:36, :] = jnp.where(role == 0, far, near)
    first[...] = buf[...].astype(BF)
    buf[0:36, :] = near
    keep[...] = jnp.where(role == 0, buf[...], 0.0).astype(BF)


def fold(parts):
    return pl.pallas_call(
        fold_kernel,
        out_shape=[jax.ShapeDtypeStruct((MSG, LANES), BF)] * 3,
        scratch_shapes=[pltpu.VMEM((MSG, LANES), F32)],
        name="fold",
    )(*parts)


def unpack_kernel(own_ref, other_ref, gq_ref, gp_ref):
    _, _, z, _ = position()
    role = role_of()
    own, other = own_ref[...], other_ref[...]
    first = jnp.where(role == 0, own, other)[0:36, :]
    second = jnp.where(role == 0, other, own)[0:36, :]
    cols = []
    for b in range(3):
        cols += [first[:, b * OWN : b * OWN + OWN], second[:, b * OWN : b * OWN + OWN]]
    gq_ref[...] = jnp.concatenate(cols, axis=1)
    proj = jnp.where((z >> 2) == role, own, other)
    gp_ref[:, 0:LANES] = proj[40:58, :]
    for u in range(3):
        gp_ref[6 * u : 6 * u + 6, LANES:D] = proj[58:64, 256 * u : 256 * u + 256]


def unpack(own, other):
    return pl.pallas_call(
        unpack_kernel,
        out_shape=[jax.ShapeDtypeStruct((36, QKV), F32), jax.ShapeDtypeStruct((18, D), F32)],
        name="unpack_grads",
    )(own, other)


def add(*parts):
    total = parts[0].astype(F32)
    for part in parts[1:]:
        total = total + part.astype(F32)
    return total.astype(BF)


def local(tokens, grad_out, modulation, frame_counts, w_qkv, w_proj):
    both = ("grp", "seq")
    barrier = lax.optimization_barrier
    mods = modulation[0]
    table = jnp.asarray(row_table(PAIR))
    td, mine = pack(tokens[0, 0], grad_out[0, 0], w_qkv, w_proj)
    first = lax.ppermute(mine, both, first_moves(-1))
    second = lax.ppermute(mine, both, second_moves(-1))
    td_in = [lax.ppermute(td[k], "seq", along_y(k)) for k in ORDER]
    first, second, *own_td = barrier([first, second, td[0], td_in[0], td_in[2], td_in[1]])
    two = jnp.concatenate(own_td[:2], axis=0)
    other_td = [lax.ppermute(t, "seq", CORE_SWAP) for t in [two] + own_td[2:]]
    pair, *other_td = barrier([make_pair(mine, first, second)] + other_td)
    pairs = barrier([lax.ppermute(pair, both, pair_moves(i, -1)) for i in (1, 2, 3)])
    w0 = jnp.concatenate([pair] + pairs, axis=0)
    w = [w0] + [lax.ppermute(w0, both, ring_moves(-k)) for k in (1, 2, 3)]
    modp, gated = prepare(frame_counts, table, mods, own_td + other_td)
    *w, modp, gated = barrier(w + [modp, gated])

    rows, grads = compute(frame_counts, jnp.asarray(row_table(32)), modp, gated, w)

    ring_in = [lax.ppermute(grads[k], both, ring_moves(k)) for k in (2, 1, 3)]
    own_part, other_part = back(table, rows, w)
    *ring_in, own_part, other_part = barrier(ring_in + [own_part, other_part])
    other_in = lax.ppermute(other_part, "seq", CORE_SWAP)
    sums = [add(*[t[PAIR * b : PAIR * b + PAIR] for t in [grads[0]] + ring_in]) for b in range(4)]
    z_in = [lax.ppermute(sums[i], both, pair_moves(i, 1)) for i in (1, 2, 3)]
    gt = finish(mods, own_part, other_in, own_td)
    *z_in, g0, g1, g2, g3 = barrier(z_in + list(gt))
    keep, first, second = fold([sums[0], *z_in])
    first = lax.ppermute(first, both, first_moves(1))
    second = lax.ppermute(second, both, second_moves(1))
    g_in = [lax.ppermute(g, "seq", along_y(-k)) for k, g in ((1, g1), (2, g2), (3, g3))]
    block = add(keep, first, second)
    r_in = [lax.ppermute(block, both, over_y(k)) for k in ORDER]
    r1, r3, r2, grad_x = barrier(r_in + [join_tokens([g0] + g_in)])
    total = (block.astype(F32) + r2.astype(F32)) + (r1.astype(F32) + r3.astype(F32))
    grad_qkv, grad_proj = unpack(total, lax.ppermute(total, "seq", CORE_SWAP))
    return (grad_x[None, None], grad_qkv, grad_proj)


def solution(mesh):
    in_specs = (
        P("grp", "seq", None, None),
        P("grp", "seq", None, None),
        P("grp", None, None),
        P("grp"),
        P("grp", None),
        P("grp", None),
    )
    out_specs = (P("grp", "seq", None, None), P("grp", None), P("grp", None))
    return jax.shard_map(local, mesh=mesh, in_specs=in_specs, out_specs=out_specs, check_vma=False)
```
